128 devices in a mesh: gz: 8 (over z_hi, y), row: 16 (over z_lo, x, core).
Axes of the slice: x: 4, y: 4, z: 4 (z_hi: 2, z_lo: 2; z = z_hi * 2 + z_lo), core: 2. Of those that a mesh axis runs over, the one named last changes fastest.
Arguments:
- swirl: float32 [1536, 16384], P('gz', 'row'), may hold values from -6 to 6
- vorticity: float32 [1536, 16384], P('gz', 'row'), may hold values from -5 to 5
- base_swirl: float32 [1536, 16384], P('gz', 'row'), may hold values from -6 to 6
- vel_r: float32 [1536, 16384], P('gz', 'row'), may hold values from -6 to 6
- vel_z: float32 [1536, 16384], P('gz', 'row'), may hold values from -6 to 6
- swirl_coef: float32 [1536, 16384], P('gz', 'row'), may hold values from 0.5 to 2
- vort_coef: float32 [1536, 16384], P('gz', 'row'), may hold values from 0.5 to 2
Outputs:
- swirl_rate: float32 [1536, 16384], P('gz', 'row')
- vort_rate: float32 [1536, 16384], P('gz', 'row')
- potential: float32 [1536, 16384], P('gz', 'row')
The draws below stay inside these ranges and needn't reach their ends.
All inputs are finite; a program needn't handle non-finite values.
Results may differ from the reference program's by a relative error of at most 0.0001.
Values sent between devices are 32-bit elements; how exact they have to be, the bound alone decides.
No kernel may reach another device: no remote copies, remote signals or barrier semaphores. Data moves between devices by JAX's collectives and lax.ppermute only.
A program may use at most 64 MiB of HBM per device.

```python
import jax
import jax.numpy as jnp
from jax import lax

LEVELS = 3
COARSE_ITERS = 10
NZ = 1536
NR = 16384


def draw_vorticity(key, part):
    return jnp.clip(jax.random.normal(key, (NZ, NR), jnp.float32), -5.0, 5.0)


def levels(rng, extent, split, low, high):
    level = 1.0
    for axis_at, parts in split:
        heights = jax.random.uniform(jax.random.fold_in(jax.random.fold_in(rng, 6), axis_at), (parts,), jnp.float32, low / len(split), high / len(split))
        level = level * jnp.repeat(jnp.exp(heights), extent[axis_at] // parts).reshape((-1,) + (1,) * (len(extent) - 1 - axis_at))
    return level


def centred(rng, dims, deviation, bound, pieces=(), dtype=jnp.bfloat16):
    entries = jax.random.normal(rng, dims, jnp.float32) * deviation
    if len(pieces) > 0:
        entries = levels(rng, dims, pieces, -0.22, 0.18) * entries
    return jnp.clip(entries, min=-bound, max=bound).astype(dtype)


def setup_inputs(seed: int = 0) -> dict:
    keys = jax.random.split(jax.random.key(seed), 8)
    swirl = centred(keys[0], (NZ, NR), 1.0, 6.0, ((0, 8), (1, 16)), jnp.float32)
    vorticity = draw_vorticity(jax.random.fold_in(keys[7], 71), 0)
    base_swirl = centred(keys[2], (NZ, NR), 1.0, 6.0, ((0, 8), (1, 16)), jnp.float32)
    vel_r = centred(keys[3], (NZ, NR), 1.0, 6.0, ((0, 8), (1, 16)), jnp.float32)
    vel_z = centred(keys[4], (NZ, NR), 1.0, 6.0, ((0, 8), (1, 16)), jnp.float32)
    swirl_coef = jnp.clip(0.5 + 1.5 * jax.random.uniform(keys[5], (NZ, NR), jnp.float32) ** levels(keys[5], (NZ, NR), ((0, 8), (1, 16)), -0.2, 0.2), 0.5, 2.0)
    vort_coef = jnp.clip(0.5 + 1.5 * jax.random.uniform(keys[6], (NZ, NR), jnp.float32) ** levels(keys[6], (NZ, NR), ((0, 8), (1, 16)), -0.2, 0.2), 0.5, 2.0)
    return {"swirl": swirl, "vorticity": vorticity, "base_swirl": base_swirl, "vel_r": vel_r, "vel_z": vel_z, "swirl_coef": swirl_coef, "vort_coef": vort_coef}


def radial_coefs(col_start, col_count, level_no):
    spacing = float(2 ** level_no)
    columns = (jnp.arange(col_count) + col_start).astype(jnp.float32)
    radius = spacing * (columns + 0.5) + 16.0
    radial_term = (1.5 * spacing) / radius
    return 1.0 + radial_term, 1.0 - radial_term


def neighbours(padded, east_coef, west_coef):
    beside = padded[:-2, 1:-1] + padded[2:, 1:-1]
    beside = beside + east_coef * padded[1:-1, 2:]
    beside = beside + west_coef * padded[1:-1, :-2]
    return beside


def checker(row_count, col_count):
    total = jnp.arange(row_count)[:, None] + jnp.arange(col_count)[None, :]
    return total % 2 == 0


def relax_half(field, padded, source, cells, east_coef, west_coef, factor):
    updated = (factor * source + neighbours(padded, east_coef, west_coef)) * 0.25
    return jnp.where(cells, updated, field)


def apply_operator(field, padded, east_coef, west_coef, factor):
    return (4.0 * field - neighbours(padded, east_coef, west_coef)) / factor


def residual_of(field, padded, source, east_coef, west_coef, factor):
    return source - apply_operator(field, padded, east_coef, west_coef, factor)


def restrict_avg(resid):
    return (resid[0::2, 0::2] + resid[1::2, 0::2] + resid[0::2, 1::2] + resid[1::2, 1::2]) * 0.25


def prolongate(correction):
    return jnp.repeat(jnp.repeat(correction, 2, axis=0), 2, axis=1)


def coarse_solve(source):
    row_count, col_count = source.shape
    east_coef, west_coef = radial_coefs(0, col_count, LEVELS)
    factor = float(4 ** LEVELS)
    count = float(row_count * col_count)

    def one_turn(turn_no, carry):
        field, resid = carry
        image = apply_operator(resid, jnp.pad(resid, 1), east_coef, west_coef, factor)
        upper = jnp.sum(resid * image) / count
        lower = jnp.sum(image * image) / count
        alpha = upper / (lower + 1e-12)
        return field + alpha * resid, resid - alpha * image

    field, resid = lax.fori_loop(0, COARSE_ITERS, one_turn, (jnp.zeros_like(source), source))
    return field


def v_cycle(source, level_no):
    row_count, col_count = source.shape
    east_coef, west_coef = radial_coefs(0, col_count, level_no)
    red_cells = checker(row_count, col_count)
    black_cells = jnp.logical_not(red_cells)
    factor = float(4 ** level_no)
    field = jnp.zeros_like(source)
    field = relax_half(field, jnp.pad(field, 1), source, red_cells, east_coef, west_coef, factor)
    field = relax_half(field, jnp.pad(field, 1), source, black_cells, east_coef, west_coef, factor)
    resid = residual_of(field, jnp.pad(field, 1), source, east_coef, west_coef, factor)
    coarse = restrict_avg(resid)
    if level_no + 1 == LEVELS:
        correction = coarse_solve(coarse)
    else:
        correction = v_cycle(coarse, level_no + 1)
    field = field + prolongate(correction)
    field = relax_half(field, jnp.pad(field, 1), source, red_cells, east_coef, west_coef, factor)
    field = relax_half(field, jnp.pad(field, 1), source, black_cells, east_coef, west_coef, factor)
    return field


def reference(swirl, vorticity, base_swirl, vel_r, vel_z, swirl_coef, vort_coef):
    stacked = jnp.stack([swirl, vorticity, 2.0 * base_swirl * swirl])
    padded = jnp.pad(stacked, ((0, 0), (1, 1), (1, 1)))
    along_z = (padded[:, 2:, 1:-1] - padded[:, :-2, 1:-1]) * 0.5
    along_r = (padded[:, 1:-1, 2:] - padded[:, 1:-1, :-2]) * 0.5
    swirl_rate = swirl_coef * swirl - vel_r * along_r[0] - vel_z * along_z[0]
    vort_rate = vort_coef * vorticity - vel_r * along_r[1] - vel_z * along_z[1] + along_z[2]
    potential = v_cycle(vorticity, 0)
    return (swirl_rate, vort_rate, potential)
```

```python
import functools

import jax
import jax.numpy as jnp
from jax import lax
from jax.experimental import pallas as pl
from jax.experimental.pallas import tpu as pltpu
from jax.sharding import PartitionSpec as P

LEVELS = 3
ITERS = 10
BASIS = ITERS + 1
PAIRS = [(i, j) for i in range(BASIS) for j in range(i, BASIS)]
SLOTS = 72
AXES = ("gz", "row")

ROWS, COLS = 192, 1024
MARGIN = 32
EXT = ROWS + 2 * MARGIN
WIDE = COLS + 128
PAD = 8
TILES = WIDE // 128
F32 = jnp.float32


def iota(shape, dim):
    return lax.broadcasted_iota(jnp.int32, shape, dim)


def local_cols():
    lane = iota((8, WIDE), 1)
    return jnp.where(lane < COLS + 64, lane, lane - WIDE)


def place():
    return lax.axis_index("gz"), lax.axis_index("row"), lax.axis_size("gz"), lax.axis_size("row")


def lanes_inside(cols, width, row, row_count):
    low = jnp.where(row == 0, 0, -width)
    high = jnp.where(row == row_count - 1, width, 2 * width)
    return (cols >= low) & (cols < high)


def fill_coefs(coef):
    _, row, _, _ = place()
    cols = local_cols() + row * COLS
    for level in range(LEVELS):
        spacing = float(2**level)
        radius = spacing * (lax.shift_right_arithmetic(cols, level).astype(F32) + 0.5) + 16.0
        term = (1.5 * spacing) / radius
        coef[pl.ds(16 * level, 8), :] = 1.0 + term
        coef[pl.ds(16 * level + 8, 8), :] = 1.0 - term


def shift(x, by):
    return pltpu.roll(x, by % x.shape[1], 1)


def beside_of(ref, start, coef, level):
    step = 2**level
    view = ref.at[pl.ds(pl.multiple_of(start - 8, 8), 24), :]
    here = view[8:16, :]
    total = view[7:15, :] + view[9:17, :]
    total = total + coef[pl.ds(16 * level, 8), :] * shift(here, -step)
    return total + coef[pl.ds(16 * level + 8, 8), :] * shift(here, step), here


def masks(level):
    _, row, _, row_count = place()
    cols = local_cols()
    inside = lanes_inside(cols, COLS, row, row_count)
    odd = ((lax.shift_right_arithmetic(cols, level) + iota((8, WIDE), 0)) & 1) == 1
    return odd & inside, jnp.logical_not(odd) & inside, inside


def row_factor(first, count, margin, amount):
    gz, _, gz_count, _ = place()
    low = jnp.where(gz == 0, margin, 0)
    high = jnp.where(gz == gz_count - 1, count - margin, count)
    at = iota((8, 1), 0) + first
    return jnp.where((at >= low) & (at < high), amount, 0.0).astype(F32)


def down_level(level, source, black, pairs, coarse, coef):
    count = EXT >> level
    margin = MARGIN >> level
    scale = float(4**level)
    step = 2**level

    black_cells, _, _ = masks(level)

    @pl.loop(0, count // 8)
    def _(k):
        start = pl.multiple_of(PAD + 8 * k, 8)
        beside, here = beside_of(source, start, coef, level)
        value = here + 0.25 * beside
        factor = row_factor(8 * k, count, margin, 0.25 * scale)
        black[pl.ds(start, 8), :] = jnp.where(black_cells, value * factor, 0.0)

    @pl.loop(0, count // 8)
    def _(k):
        start = pl.multiple_of(PAD + 8 * k, 8)
        beside, _ = beside_of(black, start, coef, level)
        both = beside + shift(beside, -step)
        for tile in range(TILES):
            pairs[pl.ds(pl.multiple_of(EXT * tile + 8 * k, 8), 8), :] = both[:, 128 * tile : 128 * tile + 128]

    _, _, inside = masks(level)
    offset = PAD if level < LEVELS - 1 else 0

    @pl.loop(0, count // 16)
    def _(k):
        factor = row_factor(8 * k, count // 2, margin // 2, 0.25 / scale)
        for tile in range(TILES):
            lanes = slice(128 * tile, 128 * tile + 128)
            view = pairs.at[pl.ds(pl.multiple_of(EXT * tile + 16 * k, 16), 16), :]
            top = view[pl.ds(0, 8, stride=2), :]
            low = view[pl.ds(1, 8, stride=2), :]
            value = jnp.where(inside[:, lanes], (top + low) * factor, 0.0)
            coarse[pl.ds(pl.multiple_of(offset + 8 * k, 8), 8), lanes] = value


def zero_pads(refs, counts):
    for ref, count in zip(refs, counts):
        ref[pl.ds(0, PAD), :] = jnp.zeros((PAD, WIDE), F32)
        ref[pl.ds(PAD + count, PAD), :] = jnp.zeros((PAD, WIDE), F32)


def two_sum(a, b):
    total = a + b
    part = total - a
    return total, (a - (total - part)) + (b - part)


def halves(a):
    wide = a * 4097.0
    high = wide - (wide - a)
    return high, a - high


def two_prod(a, b):
    total = a * b
    ah, al = halves(a)
    bh, bl = halves(b)
    return total, ((ah * bh - total) + ah * bl + al * bh) + al * bl


def dd_add(a, b):
    total, rest = two_sum(a[0], b[0])
    rest = rest + (a[1] + b[1])
    high = total + rest
    return high, rest - (high - total)


def dd_mul(a, b):
    total, rest = two_prod(a[0], b[0])
    rest = rest + (a[0] * b[1] + a[1] * b[0])
    high = total + rest
    return high, rest - (high - total)


def first_kernel(vort, swirl, part, to_east, to_west, s0, s1, s2, b0, b1, b2, pairs, c3, coef):
    fill_coefs(coef)
    zero_pads((s0, s1, s2, b0, b1, b2), (EXT, EXT // 2, EXT // 4) * 2)
    s0[pl.ds(PAD, MARGIN), :] = jnp.zeros((MARGIN, WIDE), F32)
    s0[pl.ds(PAD + MARGIN + ROWS, MARGIN), :] = jnp.zeros((MARGIN, WIDE), F32)
    s0[pl.ds(PAD + MARGIN, ROWS), :COLS] = vort[...]
    s0[pl.ds(PAD + MARGIN, ROWS), COLS:] = jnp.zeros((ROWS, 128), F32)
    down_level(0, s0, b0, pairs, s1, coef)
    down_level(1, s1, b1, pairs, s2, coef)
    down_level(2, s2, b2, pairs, c3, coef)

    lane = iota((32, 128), 1)
    pick = (lane & 15) * 8
    main = jnp.zeros((32, 128), F32)
    for tile in range(TILES - 1):
        got = jnp.take_along_axis(c3[:, 128 * tile : 128 * tile + 128], pick, axis=1)
        main = jnp.where(lax.shift_right_logical(lane, 4) == tile, got, main)
    got = jnp.take_along_axis(c3[:, COLS:], pick, axis=1)
    side = jnp.where((lane < 8) | (lane >= 120), got, 0.0)
    part[:, :128] = main
    part[:, 128:] = side

    lane = iota((ROWS, 128), 1)
    last = vort[:, COLS - 128 :]
    to_east[:ROWS, :] = jnp.where(lane >= 96, last, pltpu.roll(swirl[:, COLS - 128 :], 64, 1))
    to_west[:ROWS, :] = jnp.where(lane < 32, vort[:, :128], pltpu.roll(swirl[:, :128], 64, 1))
    high = iota((32, 128), 1) >= 64
    to_east[ROWS:, :] = jnp.where(high, main, side)
    to_west[ROWS:, :] = jnp.where(high, side, main)


def level_scratch():
    shapes = [(EXT >> level) + 2 * PAD for level in range(LEVELS)]
    sources = [pltpu.VMEM((n, WIDE), F32) for n in shapes]
    blacks = [pltpu.VMEM((n, WIDE), F32) for n in shapes]
    return sources + blacks


def vmem():
    return pl.BlockSpec(memory_space=pltpu.VMEM)


def shaped(*dims):
    return jax.ShapeDtypeStruct(dims, F32)


PARAMS = dict(compiler_params=pltpu.CompilerParams(vmem_limit_bytes=40 * 2**20))


def run_first(vort, swirl):
    return pl.pallas_call(
        first_kernel,
        out_shape=(shaped(32, 256), shaped(ROWS + 32, 128), shaped(ROWS + 32, 128)),
        in_specs=[vmem()] * 2,
        out_specs=[vmem()] * 3,
        scratch_shapes=level_scratch()
        + [pltpu.VMEM((TILES * EXT, 128), F32), pltpu.VMEM((32, WIDE), F32), pltpu.VMEM((48, WIDE), F32)],
        name="down_own",
        **PARAMS,
    )(vort, swirl)


def second_kernel(part, from_west, from_east, vort, swirl, base, whole, to_next, to_prev):
    high = iota((32, 128), 1) >= 64
    west, east = from_west[ROWS:, :], from_east[ROWS:, :]
    main = part[:, :128] + jnp.where(high, east, west)
    side = part[:, 128:] + jnp.where(high, west, east)
    whole[:, :128] = main
    whole[:, 128:] = side
    lane = iota((32, 128), 1)
    for dest, first, edge, rows in ((to_next, ROWS - 32, ROWS - 1, slice(16, 32)), (to_prev, 0, 0, slice(0, 16))):
        for tile in range(TILES - 1):
            lanes = slice(128 * tile, 128 * tile + 128)
            dest[32 * tile : 32 * tile + 32, :] = vort[first : first + 32, lanes]
            row = swirl[edge : edge + 1, lanes]
            dest[320 + tile : 321 + tile, :] = row
            dest[328 + tile : 329 + tile, :] = 2.0 * base[edge : edge + 1, lanes] * row
        beyond = jnp.where(lane < 32, from_east[first : first + 32, :], 0.0)
        dest[256:288, :] = jnp.where(lane >= 96, from_west[first : first + 32, :], beyond)
        dest[288:304, :] = main[rows]
        dest[304:320, :] = side[rows]


def run_second(part, from_west, from_east, vort, swirl, base):
    return pl.pallas_call(
        second_kernel,
        out_shape=(shaped(32, 256), shaped(336, 128), shaped(336, 128)),
        in_specs=[vmem()] * 6,
        out_specs=[vmem()] * 3,
        name="pack_gz",
        **PARAMS,
    )(part, from_west, from_east, vort, swirl, base)


def third_kernel(whole, from_prev, from_next, basis, message, grid, gram_high, gram_low):
    gz, row, gz_count, row_count = place()
    grid[...] = jnp.zeros((48, 256), F32)
    grid[8:40, :] = whole[...]
    grid[0:16, :128] += from_prev[288:304, :]
    grid[0:16, 128:] += from_prev[304:320, :]
    grid[32:48, :128] += from_next[288:304, :]
    grid[32:48, 128:] += from_next[304:320, :]

    lane = iota((48, 256), 1)
    cols = jnp.where(lane < 192, lane, lane - 256)
    width = COLS >> LEVELS
    at = iota((48, 256), 0) - 12
    inside = lanes_inside(cols, width, row, row_count)
    low = jnp.where(gz == 0, 0, -64)
    high = jnp.where(gz == gz_count - 1, ROWS >> LEVELS, 128)
    inside = inside & (at >= low) & (at < high)
    spacing = float(2**LEVELS)
    radius = spacing * ((cols + row * width).astype(F32) + 0.5) + 16.0
    term = (1.5 * spacing) / radius
    east = jnp.where(inside, 0.25 + 0.25 * term, 0.0)
    west = jnp.where(inside, 0.25 - 0.25 * term, 0.0)
    quarter = jnp.where(inside, 0.25, 0.0)

    def average(x):
        total = quarter * (pltpu.roll(x, 1, 0) + pltpu.roll(x, 47, 0))
        total = total + east * pltpu.roll(x, 255, 1)
        return total + west * pltpu.roll(x, 1, 1)

    older = jnp.where(inside, grid[...], 0.0)
    newer = average(older)
    vectors = [older, newer]
    for _ in range(BASIS - 2):
        older, newer = newer, 2.0 * average(newer) - older
        vectors.append(newer)
    at = iota((32, 128), 0)
    own = (at >= 4) & (at < 28)
    parts = []
    for k in range(BASIS):
        if k < ITERS:
            basis[32 * k : 32 * k + 32, :] = vectors[k][8:40]
        masked = jnp.where(own, vectors[k][8:40, :128], 0.0)
        parts.append((masked,) + halves(masked))
    for slot, (i, j) in enumerate(PAIRS):
        a, ah, al = parts[i]
        b, bh, bl = parts[j]
        product = a * b
        error = ((ah * bh - product) + ah * bl + al * bh) + al * bl
        top, first = two_sum(product[0:8], product[8:16])
        bottom, second = two_sum(product[16:24], product[24:32])
        total, third = two_sum(top, bottom)
        rest = (error[0:8] + error[8:16]) + (error[16:24] + error[24:32])
        gram_high[8 * slot : 8 * slot + 8, :] = total
        gram_low[8 * slot : 8 * slot + 8, :] = rest + (first + second + third)
    gram_high[8 * len(PAIRS) :, :] = jnp.zeros((8 * (SLOTS - len(PAIRS)), 128), F32)
    gram_low[8 * len(PAIRS) :, :] = jnp.zeros((8 * (SLOTS - len(PAIRS)), 128), F32)
    total = None
    for s in range(8):
        term = (gram_high[pl.ds(s, SLOTS, stride=8), :], gram_low[pl.ds(s, SLOTS, stride=8), :])
        total = term if total is None else dd_add(total, term)
    for by in (64, 32, 16, 8, 4, 2, 1):
        total = dd_add(total, tuple(pltpu.roll(t, by, 1) for t in total))
    slot = iota((SLOTS, 128), 0)
    lane = iota((SLOTS, 128), 1)
    keep = lane < 0
    for number, (i, j) in enumerate(PAIRS):
        keep = keep | ((slot == number) & ((lane == BASIS * i + j) | (lane == BASIS * j + i)))
    rows = [jnp.sum(jnp.where(keep, t, 0.0), axis=0, keepdims=True) for t in total]
    odd = (iota(message.shape, 0) & 1) == 1
    message[...] = jnp.where(odd, rows[1], rows[0])


def run_third(whole, from_prev, from_next, devices):
    return pl.pallas_call(
        third_kernel,
        out_shape=(shaped(32 * ITERS, 256), shaped(2 * devices, 128)),
        in_specs=[vmem()] * 3,
        out_specs=[vmem()] * 2,
        scratch_shapes=[pltpu.VMEM((48, 256), F32), pltpu.VMEM((8 * SLOTS, 128), F32), pltpu.VMEM((8 * SLOTS, 128), F32)],
        name="basis_gram",
        **PARAMS,
    )(whole, from_prev, from_next)


def coarse_coefs(grams, cells):
    devices = grams.shape[0] // 2
    gram = (grams[pl.ds(0, devices, stride=2), :], grams[pl.ds(1, devices, stride=2), :])
    while gram[0].shape[0] > 8:
        half = gram[0].shape[0] // 2
        gram = dd_add(tuple(g[:half] for g in gram), tuple(g[half:] for g in gram))
    for by in (4, 2, 1):
        gram = dd_add(gram, tuple(pltpu.roll(g, by, 0) for g in gram))

    lane = iota((8, 128), 1)
    i = lane // BASIS
    j = lane - BASIS * i
    used = lane < BASIS * BASIS

    def weights(index):
        below = jnp.where(index == 0, 0.0, jnp.where(index == 1, 1.0, 0.5))
        above = jnp.where(index < BASIS - 1, 0.5, 0.0)
        return jnp.where(used, below, 0.0), jnp.where(used, above, 0.0)

    def image(a, weight, step):
        below, above = weight
        moved = dd_add(
            tuple(below * pltpu.roll(t, step, 1) for t in a), tuple(above * pltpu.roll(t, 128 - step, 1) for t in a)
        )
        return dd_add(a, tuple(-t for t in moved))

    weight_i, weight_j = weights(i), weights(j)
    none = jnp.zeros((8, 128), F32)
    a_i = (jnp.where(used & (i == 0), 1.0, 0.0), none)
    a_j = (jnp.where(used & (j == 0), 1.0, 0.0), none)
    first = iota((8, 128), 0) == 0
    solved = none
    tiny = float(4 ** (2 * LEVELS)) / 16.0 * cells * 1e-12
    for _ in range(ITERS):
        b_i = image(a_i, weight_i, BASIS)
        b_j = image(a_j, weight_j, 1)
        left = tuple(jnp.where(first, a, b) for a, b in zip(a_i, b_i))
        form = dd_mul(dd_mul(left, b_j), gram)
        for by in (64, 32, 16, 8, 4, 2, 1):
            form = dd_add(form, tuple(pltpu.roll(t, by, 1) for t in form))
        alpha = form[0][0:1] / (form[0][1:2] + tiny)
        alpha = jnp.broadcast_to(alpha, (8, 128))
        solved = solved + alpha * a_j[0]

        def less(a, b):
            high, rest = two_prod(alpha, b[0])
            return dd_add(a, (-high, -(rest + alpha * b[1])))

        a_i, a_j = less(a_i, b_i), less(a_j, b_j)
    return solved * (float(4**LEVELS) * 0.25)


def up_level(level, source, black, error, spread, work, coef, store):
    count = EXT >> level
    margin = MARGIN >> level
    scale = float(4**level)
    step = 2**level
    black_cells, red_cells, inside = masks(level)
    cols = local_cols()
    near = (lax.shift_right_arithmetic(cols, level) & 1) == 0

    @pl.loop(0, count // 16)
    def _(k):
        here = error[pl.ds(pl.multiple_of(8 * k, 8), 8), :]
        both = jnp.where(near, here, shift(here, step))
        for tile in range(TILES):
            value = both[:, 128 * tile : 128 * tile + 128]
            view = spread.at[pl.ds(pl.multiple_of(EXT * tile + 16 * k, 16), 16), :]
            view[pl.ds(0, 8, stride=2), :] = value
            view[pl.ds(1, 8, stride=2), :] = value

    @pl.loop(0, count // 8)
    def _(k):
        start = pl.multiple_of(PAD + 8 * k, 8)
        for tile in range(TILES):
            lanes = slice(128 * tile, 128 * tile + 128)
            add = spread[pl.ds(pl.multiple_of(EXT * tile + 8 * k, 8), 8), :]
            black[pl.ds(start, 8), lanes] += jnp.where(black_cells[:, lanes], add, 0.0)

    @pl.loop(0, count // 8)
    def _(k):
        start = pl.multiple_of(PAD + 8 * k, 8)
        beside, _ = beside_of(black, start, coef, level)
        value = scale * source[pl.ds(start, 8), :] + beside
        work[pl.ds(start, 8), :] = jnp.where(red_cells, value * row_factor(8 * k, count, margin, 0.25), 0.0)

    skip = margin // 8 if level == 0 else 0

    @pl.loop(skip, count // 8 - skip)
    def _(k):
        start = pl.multiple_of(PAD + 8 * k, 8)
        beside, here = beside_of(work, start, coef, level)
        value = scale * source[pl.ds(start, 8), :] + beside
        value = value * row_factor(8 * k, count, margin, 0.25)
        store(k - skip, jnp.where(black_cells, value, here))


def fourth_kernel(
    grams, basis, vort, from_west, from_east, from_prev, from_next, out,
    s0, s1, s2, b0, b1, b2, pairs, c3, coef, work, cells,
):
    fill_coefs(coef)
    zero_pads((s0, s1, s2, b0, b1, b2), (EXT, EXT // 2, EXT // 4) * 2)
    lane = iota((ROWS, 128), 1)
    s0[pl.ds(PAD + MARGIN, ROWS), :COLS] = vort[...]
    beyond = jnp.where(lane < 32, from_east[:ROWS, :], 0.0)
    s0[pl.ds(PAD + MARGIN, ROWS), COLS:] = jnp.where(lane >= 96, from_west[:ROWS, :], beyond)
    for tile in range(TILES):
        lanes = slice(128 * tile, 128 * tile + 128)
        s0[pl.ds(PAD, MARGIN), lanes] = from_prev[32 * tile : 32 * tile + 32, :]
        s0[pl.ds(PAD + MARGIN + ROWS, MARGIN), lanes] = from_next[32 * tile : 32 * tile + 32, :]
    down_level(0, s0, b0, pairs, s1, coef)
    down_level(1, s1, b1, pairs, s2, coef)
    down_level(2, s2, b2, pairs, c3, coef)

    solved = coarse_coefs(grams, cells)
    value = jnp.zeros((32, 256), F32)
    for k in range(ITERS):
        value = value + solved[0:1, k : k + 1] * basis[32 * k : 32 * k + 32, :]
    lane = iota((32, 128), 1)
    for tile in range(TILES):
        pick = lax.shift_right_logical(lane, 3) + 16 * tile
        half = value[:, :128]
        if tile == TILES - 1:
            pick = jnp.where(lane < 64, lax.shift_right_logical(lane, 3), lax.shift_right_logical(lane, 3) + 112)
            half = value[:, 128:]
        c3[:, 128 * tile : 128 * tile + 128] = jnp.take_along_axis(half, pick, axis=1)

    def keep(ref):
        def store(k, v):
            ref[pl.ds(pl.multiple_of(8 * k, 8), 8), :] = v

        return store

    def give(k, v):
        out[pl.ds(pl.multiple_of(8 * k, 8), 8), :] = v[:, :COLS]

    zero_pads((work,), (EXT // 4,))
    up_level(2, s2, b2, c3, pairs, work, coef, keep(s2))
    zero_pads((work,), (EXT // 2,))
    up_level(1, s1, b1, s2, pairs, work, coef, keep(s1))
    zero_pads((work,), (EXT,))
    up_level(0, s0, b0, s1, pairs, work, coef, give)


def run_fourth(grams, basis, vort, from_west, from_east, from_prev, from_next):
    cells = float((ROWS >> LEVELS) * (COLS >> LEVELS) * lax.axis_size("gz") * lax.axis_size("row"))
    return pl.pallas_call(
        functools.partial(fourth_kernel, cells=cells),
        out_shape=shaped(ROWS, COLS),
        in_specs=[vmem()] * 7,
        out_specs=vmem(),
        scratch_shapes=level_scratch()
        + [pltpu.VMEM((TILES * EXT, 128), F32), pltpu.VMEM((32, WIDE), F32), pltpu.VMEM((48, WIDE), F32)]
        + [pltpu.VMEM((EXT + 2 * PAD, WIDE), F32)],
        name="v_cycle",
        **PARAMS,
    )(grams, basis, vort, from_west, from_east, from_prev, from_next)


def rates_kernel(
    swirl, vort, base, from_west, from_east, from_prev, from_next, vel_r, vel_z, swirl_coef, vort_coef, swirl_out, vort_out
):
    tile = pl.program_id(0)
    lane = iota((ROWS, 128), 1)
    at = iota((ROWS, 128), 0)
    start = pl.multiple_of(128 * tile, 128)
    lanes = pl.ds(start, 128)
    before = pl.ds(pl.multiple_of(jnp.maximum(start - 128, 0), 128), 128)
    after = pl.ds(pl.multiple_of(jnp.minimum(start + 128, COLS - 128), 128), 128)

    def slope_r(ref, west, east):
        here = ref[:, lanes]
        left = jnp.where(tile == 0, west, pltpu.roll(ref[:, before], 1, 1))
        right = jnp.where(tile == COLS // 128 - 1, east, pltpu.roll(ref[:, after], 127, 1))
        ahead = jnp.where(lane == 127, right, pltpu.roll(here, 127, 1))
        behind = jnp.where(lane == 0, left, pltpu.roll(here, 1, 1))
        return (ahead - behind) * 0.5

    def slope_z(here, top, bottom):
        ahead = jnp.where(at == ROWS - 1, bottom, pltpu.roll(here, ROWS - 1, 0))
        behind = jnp.where(at == 0, top, pltpu.roll(here, 1, 0))
        return (ahead - behind) * 0.5

    west, east = from_west[:ROWS, :], from_east[:ROWS, :]
    u_r = slope_r(swirl, pltpu.roll(west, 65, 1), pltpu.roll(east, 63, 1))
    w_r = slope_r(vort, pltpu.roll(west, 1, 1), pltpu.roll(east, 127, 1))
    u, w = swirl[:, lanes], vort[:, lanes]
    product = 2.0 * base[:, lanes] * u
    u_z = slope_z(u, from_prev[pl.ds(320 + tile, 1), :], from_next[pl.ds(320 + tile, 1), :])
    p_z = slope_z(product, from_prev[pl.ds(328 + tile, 1), :], from_next[pl.ds(328 + tile, 1), :])
    w_z = slope_z(w, from_prev[pl.ds(32 * tile + 31, 1), :], from_next[pl.ds(32 * tile, 1), :])
    swirl_out[...] = swirl_coef[...] * u - vel_r[...] * u_r - vel_z[...] * u_z
    vort_out[...] = vort_coef[...] * w - vel_r[...] * w_r - vel_z[...] * w_z + p_z


def run_rates(swirl, vort, base, from_west, from_east, from_prev, from_next, vel_r, vel_z, swirl_coef, vort_coef):
    block = pl.BlockSpec((ROWS, 128), lambda t: (0, t))

    def whole(shape):
        return pl.BlockSpec(shape, lambda t: (0, 0))

    big = whole((ROWS, COLS))
    return pl.pallas_call(
        rates_kernel,
        grid=(COLS // 128,),
        out_shape=(shaped(ROWS, COLS), shaped(ROWS, COLS)),
        in_specs=[big] * 3 + [whole((ROWS + 32, 128))] * 2 + [whole((336, 128))] * 2 + [block] * 4,
        out_specs=[block] * 2,
        name="rates",
        cost_estimate=pl.CostEstimate(flops=30 * ROWS * COLS, bytes_accessed=36 * ROWS * COLS, transcendentals=0),
        **PARAMS,
    )(swirl, vort, base, from_west, from_east, from_prev, from_next, vel_r, vel_z, swirl_coef, vort_coef)


def both_ways(axis, up, down):
    count = lax.axis_size(axis)
    ahead = [(i, i + 1) for i in range(count - 1)]
    back = [(i + 1, i) for i in range(count - 1)]
    return lax.ppermute(up, axis, ahead), lax.ppermute(down, axis, back)


def per_device(swirl, vorticity, base_swirl, vel_r, vel_z, swirl_coef, vort_coef):
    devices = lax.axis_size("gz") * lax.axis_size("row")
    part, to_east, to_west = run_first(vorticity, swirl)
    from_west, from_east = both_ways("row", to_east, to_west)
    whole, to_next, to_prev = run_second(part, from_west, from_east, vorticity, swirl, base_swirl)
    from_prev, from_next = both_ways("gz", to_next, to_prev)
    basis, message = run_third(whole, from_prev, from_next, devices)
    grams = lax.all_to_all(message, AXES, 0, 0, tiled=True)
    potential = run_fourth(grams, basis, vorticity, from_west, from_east, from_prev, from_next)
    swirl_rate, vort_rate = run_rates(
        swirl, vorticity, base_swirl, from_west, from_east, from_prev, from_next, vel_r, vel_z, swirl_coef, vort_coef
    )
    return swirl_rate, vort_rate, potential


def solution(mesh):
    spec = P("gz", "row")
    return jax.shard_map(per_device, mesh=mesh, in_specs=(spec,) * 7, out_specs=(spec,) * 3, check_vma=False)
```

```python
import functools

import jax
import jax.numpy as jnp
from jax import lax
from jax.experimental import pallas as pl
from jax.experimental.pallas import tpu as pltpu
from jax.sharding import PartitionSpec as P

LEVELS = 3
ITERS = 10
BASIS = ITERS + 1
PAIRS = [(i, j) for i in range(BASIS) for j in range(i, BASIS)]
SLOTS = 72
AXES = ("gz", "row")

ROWS, COLS = 192, 1024
SPAN = 32
PAD = 8
TALL = SPAN + 2 * PAD
F32 = jnp.float32


def iota(shape, dim):
    return lax.broadcasted_iota(jnp.int32, shape, dim)


def place():
    return lax.axis_index("gz"), lax.axis_index("row"), lax.axis_size("gz"), lax.axis_size("row")


def lanes_inside(cols, width, row, row_count):
    low = jnp.where(row == 0, 0, -width)
    high = jnp.where(row == row_count - 1, width, 2 * width)
    return (cols >= low) & (cols < high)


def planes_of(level):
    return 8 >> level


def plane_rows(level):
    return planes_of(level) * (planes_of(level) + 1) * TALL


def base(level, b, p):
    return (b * (planes_of(level) + 1) + p) * TALL


COEF_AT = [0, 9, 14]
COEF_ROWS = 2 * 8 * 17


def side_place():
    lane = iota((8, 128), 1)
    h = lane & 15
    return lax.shift_right_logical(lane, 4), h, jnp.where(h < 8, h + 128, h - 16)


def fill_coefs(coef):
    _, row, _, _ = place()
    lane = iota((8, 128), 1)
    p_side, _, q_side = side_place()
    for level in range(LEVELS):
        count = planes_of(level)
        spacing = float(2**level)
        for p in range(count + 1):
            if p < count:
                cols = count * lane + p
            else:
                cols = count * q_side + lax.shift_right_logical(p_side, level)
            cols = cols + row * (COLS >> level)
            term = (1.5 * spacing) / (spacing * (cols.astype(F32) + 0.5) + 16.0)
            at = 16 * (COEF_AT[level] + p)
            coef[at : at + 8, :] = 1.0 + term
            coef[at + 8 : at + 16, :] = 1.0 - term


def coefs_of(coef, level, p):
    at = 16 * (COEF_AT[level] + p)
    return coef[at : at + 8, :], coef[at + 8 : at + 16, :]


def turn(x, by):
    return pltpu.roll(x, by % 128, 1)


def view_of(ref, level, b, p, k):
    return ref.at[pl.ds(pl.multiple_of(base(level, b, p) + 8 * k, 8), 24), :]


def here_of(ref, level, b, p, k):
    return view_of(ref, level, b, p, k)[8:16, :]


def put(ref, level, b, p, k, value):
    ref[pl.ds(pl.multiple_of(base(level, b, p) + PAD + 8 * k, 8), 8), :] = value


def vertical(ref, level, b, p, k):
    count = planes_of(level)
    above = view_of(ref, level, b - 1, p, k)[8:16, :] if b > 0 else view_of(ref, level, count - 1, p, k)[7:15, :]
    below = view_of(ref, level, b + 1, p, k)[8:16, :] if b < count - 1 else view_of(ref, level, 0, p, k)[9:17, :]
    return above + below


def beside_main(ref, coef, level, b, p, k):
    count = planes_of(level)
    step = 2**level
    lane = iota((8, 128), 1)
    east, west = coefs_of(coef, level, p)
    side = None
    if p == 0 or p == count - 1:
        side = here_of(ref, level, b, count, k)
    if p < count - 1:
        right = here_of(ref, level, b, p + 1, k)
    else:
        right = jnp.where(lane == 127, turn(side, -1), turn(here_of(ref, level, b, 0, k), -1))
    if p > 0:
        left = here_of(ref, level, b, p - 1, k)
    else:
        left = jnp.where(lane == 0, turn(side, 16 * step - 15), turn(here_of(ref, level, b, count - 1, k), 1))
    return (vertical(ref, level, b, p, k) + east * right) + west * left


def beside_side(ref, coef, level, b, k):
    count = planes_of(level)
    step = 2**level
    lane = iota((8, 128), 1)
    east, west = coefs_of(coef, level, count)
    side = here_of(ref, level, b, count, k)
    first, last = here_of(ref, level, b, 0, k), here_of(ref, level, b, count - 1, k)
    edge = 16 * (8 - step)
    right = jnp.where(lane >= edge, turn(side, -(16 * step + 1)), turn(side, -16 * step))
    right = jnp.where(lane == edge + 15, turn(first, edge + 15), right)
    left = jnp.where(lane < 16, turn(side, 16 * step + 1), turn(side, 16 * step))
    left = jnp.where(lane == 0, turn(last, 1), left)
    return (vertical(ref, level, b, count, k) + east * right) + west * left


def odd_side(level, b):
    p_side, _, _ = side_place()
    return ((lax.shift_right_logical(p_side, level) + b) & 1) == 1


def inside_factors(k):
    gz, row, gz_count, row_count = place()
    low = jnp.where(gz == 0, 4, 0)
    high = jnp.where(gz == gz_count - 1, SPAN - 4, SPAN)
    at = iota((8, 128), 0) + 8 * k
    main = jnp.where((at >= low) & (at < high), 1.0, 0.0).astype(F32)
    _, h, _ = side_place()
    first = jnp.where(row == row_count - 1, 8, 0)
    after = jnp.where(row == 0, 8, 16)
    return main, jnp.where((h >= first) & (h < after), main, 0.0)


def chunks(body):
    pl.loop(0, SPAN // 8)(body)


def down_level(level, source, black, coarse, coef):
    count = planes_of(level)

    @chunks
    def _(k):
        main, side = inside_factors(k)
        main, side = 0.25 * main, 0.25 * side
        for b in range(count):
            for p in range(1 - b % 2, count, 2):
                beside = beside_main(source, coef, level, b, p, k)
                put(black, level, b, p, k, (here_of(source, level, b, p, k) + 0.25 * beside) * main)
            beside = beside_side(source, coef, level, b, k)
            value = (here_of(source, level, b, count, k) + 0.25 * beside) * side
            put(black, level, b, count, k, jnp.where(odd_side(level, b), value, 0.0))

    step = 2**level
    p_side, _, _ = side_place()
    keep = (lax.shift_right_logical(p_side, level) & 1) == 0

    @chunks
    def _(k):
        main, side = inside_factors(k)
        for b in range(0, count, 2):
            for p in range(0, count, 2):
                value = beside_main(black, coef, level, b, p, k) + beside_main(black, coef, level, b + 1, p + 1, k)
                put(coarse, level + 1, b // 2, p // 2, k, value * main)
            even = beside_side(black, coef, level, b, k)
            odd = turn(beside_side(black, coef, level, b + 1, k), -16 * step)
            put(coarse, level + 1, b // 2, count // 2, k, jnp.where(keep, (even + odd) * side, 0.0))


def up_level(level, source, black, error, coef):
    count = planes_of(level)
    step = 2**level
    p_side, _, _ = side_place()
    moved = (lax.shift_right_logical(p_side, level) & 1) == 1

    @chunks
    def _(k):
        for b in range(count):
            for p in range(1 - b % 2, count, 2):
                value = here_of(error, level + 1, b // 2, p // 2, k)
                put(black, level, b, p, k, here_of(black, level, b, p, k) + value)
            value = here_of(error, level + 1, b // 2, count // 2, k)
            value = jnp.where(moved, turn(value, 16 * step), value)
            value = here_of(black, level, b, count, k) + value
            put(black, level, b, count, k, jnp.where(odd_side(level, b), value, 0.0))

    for colour in (0, 1):

        @chunks
        def _(k):
            main, side = inside_factors(k)
            main, side = 0.25 * main, 0.25 * side
            for b in range(count):
                for p in range((b + colour) % 2, count, 2):
                    beside = beside_main(black, coef, level, b, p, k)
                    put(black, level, b, p, k, (here_of(source, level, b, p, k) + beside) * main)
                beside = beside_side(black, coef, level, b, k)
                value = (here_of(source, level, b, count, k) + beside) * side
                mine = odd_side(level, b + 1 - colour)
                put(black, level, b, count, k, jnp.where(mine, value, here_of(black, level, b, count, k)))


def zero_pads(refs):
    for level, ref in refs:
        for b in range(planes_of(level)):
            for p in range(planes_of(level) + 1):
                at = base(level, b, p)
                ref[at : at + PAD, :] = jnp.zeros((PAD, 128), F32)
                ref[at + PAD + SPAN : at + TALL, :] = jnp.zeros((PAD, 128), F32)


def permuted(x):
    lane = iota(x.shape, 1)
    return jnp.take_along_axis(x, (lane & 15) * 8 + lax.shift_right_logical(lane, 4), axis=1)


def restored(x):
    lane = iota(x.shape, 1)
    return jnp.take_along_axis(x, (lane & 7) * 16 + lax.shift_right_logical(lane, 3), axis=1)


def exchanged(tiles):
    tiles = list(tiles)
    lane = iota(tiles[0].shape, 1)
    for bit in range(3):
        far = 2**bit
        low = (lax.shift_right_logical(lane, 4 + bit) & 1) == 0
        for k in range(8):
            if not k & far:
                a, c = tiles[k], tiles[k + far]
                tiles[k] = jnp.where(low, a, turn(c, 16 * far))
                tiles[k + far] = jnp.where(low, turn(a, -16 * far), c)
    return tiles


def two_sum(a, b):
    total = a + b
    part = total - a
    return total, (a - (total - part)) + (b - part)


def halves(a):
    wide = a * 4097.0
    high = wide - (wide - a)
    return high, a - high


def two_prod(a, b):
    total = a * b
    ah, al = halves(a)
    bh, bl = halves(b)
    return total, ((ah * bh - total) + ah * bl + al * bh) + al * bl


def dd_add(a, b):
    total, rest = two_sum(a[0], b[0])
    rest = rest + (a[1] + b[1])
    high = total + rest
    return high, rest - (high - total)


def dd_mul(a, b):
    total, rest = two_prod(a[0], b[0])
    rest = rest + (a[0] * b[1] + a[1] * b[0])
    high = total + rest
    return high, rest - (high - total)


def first_kernel(vort, swirl_first, swirl_last, part, to_east, to_west, planes, s0, s1, s2, s3, b0, b1, b2, coef):
    fill_coefs(coef)
    zero_pads(((0, s0), (1, s1), (2, s2), (0, b0), (1, b1), (2, b2)))
    low = (iota((8, 128), 1) & 15) < 8
    for b in range(8):
        for p in range(8):
            at = base(0, b, p) + PAD
            s0[at : at + 4, :] = jnp.zeros((4, 128), F32)
            s0[at + 28 : at + 32, :] = jnp.zeros((4, 128), F32)
        at = base(0, b, 8) + PAD
        s0[at : at + SPAN, :] = jnp.zeros((SPAN, 128), F32)
    for g in range(ROWS // 8):
        rows = slice(8 * g, 8 * g + 8)
        tiles = [permuted(vort[rows, 128 * k : 128 * k + 128]) for k in range(8)]
        to_east[rows, :] = jnp.where(low, turn(swirl_last[rows, :], 65), tiles[7])
        to_west[rows, :] = jnp.where(low, tiles[0], turn(swirl_first[rows, :], 8))
        for p, tile in enumerate(exchanged(tiles)):
            s0[pl.ds(base(0, 0, p) + PAD + 4 + g, 8, stride=9 * TALL), :] = tile
    for b in range(8):
        for p in range(8):
            at = base(0, b, p) + PAD + 4
            planes[24 * (8 * b + p) : 24 * (8 * b + p) + 24, :] = s0[at : at + 24, :]
    down_level(0, s0, b0, s1, coef)
    down_level(1, s1, b1, s2, coef)
    down_level(2, s2, b2, s3, coef)

    scale = 1.0 / float(4**LEVELS)
    main = s3[PAD : PAD + SPAN, :] * scale
    side = s3[TALL + PAD : TALL + PAD + SPAN, :] * scale
    lane = iota((SPAN, 128), 1)
    side = jnp.where(lane < 8, side, jnp.where(lane >= 120, turn(side, 112), 0.0))
    part[:, :128] = main
    part[:, 128:] = side
    high = lane >= 64
    to_east[ROWS:, :] = jnp.where(high, main, side)
    to_west[ROWS:, :] = jnp.where(high, side, main)


def level_scratch():
    sources = [pltpu.VMEM((plane_rows(level), 128), F32) for level in range(LEVELS + 1)]
    blacks = [pltpu.VMEM((plane_rows(level), 128), F32) for level in range(LEVELS)]
    return sources + blacks + [pltpu.VMEM((COEF_ROWS, 128), F32)]


def vmem():
    return pl.BlockSpec(memory_space=pltpu.VMEM)


def shaped(*dims):
    return jax.ShapeDtypeStruct(dims, F32)


def params(mebibytes):
    return dict(compiler_params=pltpu.CompilerParams(vmem_limit_bytes=mebibytes * 2**20))


def run_first(vort, swirl):
    return pl.pallas_call(
        first_kernel,
        grid=(1,),
        out_shape=(shaped(32, 256), shaped(ROWS + 32, 128), shaped(ROWS + 32, 128), shaped(64 * 24, 128)),
        in_specs=[
            pl.BlockSpec((ROWS, COLS), lambda t: (0, 0)),
            pl.BlockSpec((ROWS, 128), lambda t: (0, 0)),
            pl.BlockSpec((ROWS, 128), lambda t: (0, COLS // 128 - 1)),
        ],
        out_specs=[vmem()] * 4,
        scratch_shapes=level_scratch(),
        name="down_own",
        **params(40),
    )(vort, swirl, swirl)


def second_kernel(part, from_west, from_east, planes, vort_top, vort_end, swirl_top, swirl_end, base_top, base_end, whole, to_next, to_prev):
    high = iota((32, 128), 1) >= 64
    west, east = from_west[ROWS:, :], from_east[ROWS:, :]
    main = part[:, :128] + jnp.where(high, east, west)
    side = part[:, 128:] + jnp.where(high, west, east)
    whole[:, :128] = main
    whole[:, 128:] = side
    low = (iota((4, 128), 1) & 15) < 8
    ends = ((to_next, 20, 7, slice(16, 32), vort_end, swirl_end, base_end), (to_prev, 0, 0, slice(0, 16), vort_top, swirl_top, base_top))
    for dest, g, edge, rows, vort, swirl, back in ends:
        for b in range(8):
            for p in range(8):
                at = 4 * (9 * b + p)
                dest[at : at + 4, :] = planes[24 * (8 * b + p) + g : 24 * (8 * b + p) + g + 4, :]
            at = 4 * (9 * b + 8)
            beyond = (from_east[pl.ds(8 * g + b, 4, stride=8), :], from_west[pl.ds(8 * g + b, 4, stride=8), :])
            dest[at : at + 4, :] = jnp.where(low, beyond[0], beyond[1])
        for tile in range(COLS // 128):
            lanes = slice(128 * tile, 128 * tile + 128)
            row = swirl[edge : edge + 1, lanes]
            dest[320 + tile : 321 + tile, :] = row
            dest[328 + tile : 329 + tile, :] = 2.0 * back[edge : edge + 1, lanes] * row
            dest[336 + tile : 337 + tile, :] = vort[edge : edge + 1, lanes]
        dest[288:304, :] = main[rows]
        dest[304:320, :] = side[rows]


def run_second(part, from_west, from_east, planes, vort, swirl, back):
    top = pl.BlockSpec((8, COLS), lambda t: (0, 0))
    end = pl.BlockSpec((8, COLS), lambda t: (ROWS // 8 - 1, 0))
    return pl.pallas_call(
        second_kernel,
        grid=(1,),
        out_shape=(shaped(32, 256), shaped(344, 128), shaped(344, 128)),
        in_specs=[vmem()] * 4 + [top, end] * 3,
        out_specs=[vmem()] * 3,
        name="pack_gz",
        **params(40),
    )(part, from_west, from_east, planes, vort, vort, swirl, swirl, back, back)


def third_kernel(whole, from_prev, from_next, basis, message, grid, gram_high, gram_low):
    gz, row, gz_count, row_count = place()
    grid[...] = jnp.zeros((48, 256), F32)
    grid[8:40, :] = whole[...]
    grid[0:16, :128] += from_prev[288:304, :]
    grid[0:16, 128:] += from_prev[304:320, :]
    grid[32:48, :128] += from_next[288:304, :]
    grid[32:48, 128:] += from_next[304:320, :]

    lane = iota((48, 256), 1)
    cols = jnp.where(lane < 192, lane, lane - 256)
    width = COLS >> LEVELS
    at = iota((48, 256), 0) - 12
    inside = lanes_inside(cols, width, row, row_count)
    low = jnp.where(gz == 0, 0, -64)
    high = jnp.where(gz == gz_count - 1, ROWS >> LEVELS, 128)
    inside = inside & (at >= low) & (at < high)
    spacing = float(2**LEVELS)
    radius = spacing * ((cols + row * width).astype(F32) + 0.5) + 16.0
    term = (1.5 * spacing) / radius
    east = jnp.where(inside, 0.25 + 0.25 * term, 0.0)
    west = jnp.where(inside, 0.25 - 0.25 * term, 0.0)
    quarter = jnp.where(inside, 0.25, 0.0)

    def average(x):
        total = quarter * (pltpu.roll(x, 1, 0) + pltpu.roll(x, 47, 0))
        total = total + east * pltpu.roll(x, 255, 1)
        return total + west * pltpu.roll(x, 1, 1)

    source = jnp.where(inside, grid[...], 0.0)
    older = source - average(source)
    newer = average(older)
    vectors = [source, older, newer]
    for _ in range(BASIS - 3):
        older, newer = newer, 2.0 * average(newer) - older
        vectors.append(newer)
    at = iota((32, 128), 0)
    own = (at >= 4) & (at < 28)
    parts = []
    for k in range(BASIS):
        if k < ITERS:
            basis[32 * k : 32 * k + 32, :] = vectors[k][8:40]
        masked = jnp.where(own, vectors[k][8:40, :128], 0.0)
        parts.append((masked,) + halves(masked))
    for slot, (i, j) in enumerate(PAIRS):
        a, ah, al = parts[i]
        b, bh, bl = parts[j]
        product = a * b
        error = ((ah * bh - product) + ah * bl + al * bh) + al * bl
        top, first = two_sum(product[0:8], product[8:16])
        bottom, second = two_sum(product[16:24], product[24:32])
        total, third = two_sum(top, bottom)
        rest = (error[0:8] + error[8:16]) + (error[16:24] + error[24:32])
        gram_high[8 * slot : 8 * slot + 8, :] = total
        gram_low[8 * slot : 8 * slot + 8, :] = rest + (first + second + third)
    gram_high[8 * len(PAIRS) :, :] = jnp.zeros((8 * (SLOTS - len(PAIRS)), 128), F32)
    gram_low[8 * len(PAIRS) :, :] = jnp.zeros((8 * (SLOTS - len(PAIRS)), 128), F32)
    total = None
    for s in range(8):
        term = (gram_high[pl.ds(s, SLOTS, stride=8), :], gram_low[pl.ds(s, SLOTS, stride=8), :])
        total = term if total is None else dd_add(total, term)
    for by in (64, 32, 16, 8, 4, 2, 1):
        total = dd_add(total, tuple(pltpu.roll(t, by, 1) for t in total))
    slot = iota((SLOTS, 128), 0)
    lane = iota((SLOTS, 128), 1)
    keep = lane < 0
    for number, (i, j) in enumerate(PAIRS):
        keep = keep | ((slot == number) & ((lane == BASIS * i + j) | (lane == BASIS * j + i)))
    rows = [jnp.sum(jnp.where(keep, t, 0.0), axis=0, keepdims=True) for t in total]
    odd = (iota(message.shape, 0) & 1) == 1
    message[...] = jnp.where(odd, rows[1], rows[0])


def run_third(whole, from_prev, from_next, devices):
    return pl.pallas_call(
        third_kernel,
        out_shape=(shaped(32 * ITERS, 256), shaped(2 * devices, 128)),
        in_specs=[vmem()] * 3,
        out_specs=[vmem()] * 2,
        scratch_shapes=[pltpu.VMEM((48, 256), F32), pltpu.VMEM((8 * SLOTS, 128), F32), pltpu.VMEM((8 * SLOTS, 128), F32)],
        name="basis_gram",
        **params(40),
    )(whole, from_prev, from_next)


def coarse_coefs(grams, cells):
    devices = grams.shape[0] // 2
    gram = (grams[pl.ds(0, devices, stride=2), :], grams[pl.ds(1, devices, stride=2), :])
    while gram[0].shape[0] > 8:
        half = gram[0].shape[0] // 2
        gram = dd_add(tuple(g[:half] for g in gram), tuple(g[half:] for g in gram))
    for by in (4, 2, 1):
        gram = dd_add(gram, tuple(pltpu.roll(g, by, 0) for g in gram))

    lane = iota((8, 128), 1)
    i = lane // BASIS
    j = lane - BASIS * i
    used = lane < BASIS * BASIS

    def weights(index):
        below = jnp.where(index == 0, 0.0, jnp.where(index == 1, -1.0, jnp.where(index == 2, 1.0, 0.5)))
        above = jnp.where((index > 0) & (index < BASIS - 1), 0.5, 0.0)
        same = jnp.where(index > 0, 1.0, 0.0)
        return tuple(jnp.where(used, t, 0.0) for t in (below, above, same))

    def image(a, weight, step):
        below, above, same = weight
        moved = dd_add(
            tuple(below * pltpu.roll(t, step, 1) for t in a), tuple(above * pltpu.roll(t, 128 - step, 1) for t in a)
        )
        return dd_add(tuple(same * t for t in a), tuple(-t for t in moved))

    weight_i, weight_j = weights(i), weights(j)
    none = jnp.zeros((8, 128), F32)
    a_i = (jnp.where(used & (i == 0), 1.0, 0.0), none)
    a_j = (jnp.where(used & (j == 0), 1.0, 0.0), none)
    first = iota((8, 128), 0) == 0
    solved = none
    tiny = float(4 ** (2 * LEVELS)) / 16.0 * cells * 1e-12
    for _ in range(ITERS):
        b_i = image(a_i, weight_i, BASIS)
        b_j = image(a_j, weight_j, 1)
        left = tuple(jnp.where(first, a, b) for a, b in zip(a_i, b_i))
        form = dd_mul(dd_mul(left, b_j), gram)
        for by in (64, 32, 16, 8, 4, 2, 1):
            form = dd_add(form, tuple(pltpu.roll(t, by, 1) for t in form))
        alpha = form[0][0:1] / (form[0][1:2] + tiny)
        alpha = jnp.broadcast_to(alpha, (8, 128))
        solved = solved + alpha * a_j[0]

        def less(a, b):
            high, rest = two_prod(alpha, b[0])
            return dd_add(a, (-high, -(rest + alpha * b[1])))

        a_i, a_j = less(a_i, b_i), less(a_j, b_j)
    return solved * (float(4**LEVELS) * 0.25)


def fourth_kernel(
    grams, basis, planes, from_west, from_east, from_prev, from_next, out,
    s0, s1, s2, s3, b0, b1, b2, coef, *, cells,
):
    fill_coefs(coef)
    zero_pads(((0, s0), (1, s1), (2, s2), (0, b0), (1, b1), (2, b2)))
    low = (iota((24, 128), 1) & 15) < 8
    for b in range(8):
        for p in range(9):
            at = base(0, b, p) + PAD
            edge = 4 * (9 * b + p)
            s0[at : at + 4, :] = from_prev[edge : edge + 4, :]
            s0[at + 28 : at + 32, :] = from_next[edge : edge + 4, :]
            if p < 8:
                s0[at + 4 : at + 28, :] = planes[24 * (8 * b + p) : 24 * (8 * b + p) + 24, :]
            else:
                beyond = (from_east[pl.ds(b, 24, stride=8), :], from_west[pl.ds(b, 24, stride=8), :])
                s0[at + 4 : at + 28, :] = jnp.where(low, beyond[0], beyond[1])
    down_level(0, s0, b0, s1, coef)
    down_level(1, s1, b1, s2, coef)
    down_level(2, s2, b2, s3, coef)

    solved = coarse_coefs(grams, cells)
    value = jnp.zeros((32, 256), F32)
    for k in range(ITERS):
        value = value + solved[0:1, k : k + 1] * basis[32 * k : 32 * k + 32, :]
    lane = iota((SPAN, 128), 1)
    side = value[:, 128:]
    s3[PAD : PAD + SPAN, :] = value[:, :128]
    s3[TALL + PAD : TALL + PAD + SPAN, :] = jnp.where(lane < 8, side, turn(side, 16))
    up_level(2, s2, b2, s3, coef)
    up_level(1, s1, b1, b2, coef)
    up_level(0, s0, b0, b1, coef)
    for g in range(ROWS // 8):
        tiles = [b0[pl.ds(base(0, 0, p) + PAD + 4 + g, 8, stride=9 * TALL), :] for p in range(8)]
        for k, tile in enumerate(exchanged(tiles)):
            out[8 * g : 8 * g + 8, 128 * k : 128 * k + 128] = restored(tile)


def run_fourth(grams, basis, planes, from_west, from_east, from_prev, from_next):
    cells = float((ROWS >> LEVELS) * (COLS >> LEVELS) * lax.axis_size("gz") * lax.axis_size("row"))
    return pl.pallas_call(
        functools.partial(fourth_kernel, cells=cells),
        out_shape=shaped(ROWS, COLS),
        in_specs=[vmem()] * 7,
        out_specs=vmem(),
        scratch_shapes=level_scratch(),
        name="v_cycle",
        **params(40),
    )(grams, basis, planes, from_west, from_east, from_prev, from_next)


def rates_kernel(
    swirl, vort, back, from_west, from_east, from_prev, from_next, vel_r, vel_z, swirl_coef, vort_coef, swirl_out, vort_out
):
    tile = pl.program_id(0)
    lane = iota((ROWS, 128), 1)
    at = iota((ROWS, 128), 0)
    start = pl.multiple_of(128 * tile, 128)
    lanes = pl.ds(start, 128)
    before = pl.ds(pl.multiple_of(jnp.maximum(start - 128, 0), 128), 128)
    after = pl.ds(pl.multiple_of(jnp.minimum(start + 128, COLS - 128), 128), 128)

    def slope_r(ref, west, east):
        here = ref[:, lanes]
        left = jnp.where(tile == 0, west, pltpu.roll(ref[:, before], 1, 1))
        right = jnp.where(tile == COLS // 128 - 1, east, pltpu.roll(ref[:, after], 127, 1))
        ahead = jnp.where(lane == 127, right, pltpu.roll(here, 127, 1))
        behind = jnp.where(lane == 0, left, pltpu.roll(here, 1, 1))
        return (ahead - behind) * 0.5

    def slope_z(here, top, bottom):
        ahead = jnp.where(at == ROWS - 1, bottom, pltpu.roll(here, ROWS - 1, 0))
        behind = jnp.where(at == 0, top, pltpu.roll(here, 1, 0))
        return (ahead - behind) * 0.5

    west, east = from_west[:ROWS, :], from_east[:ROWS, :]
    u_r = slope_r(swirl, turn(west, 64), turn(east, 119))
    w_r = slope_r(vort, pltpu.roll(west, 1, 1), pltpu.roll(east, 127, 1))
    u, w = swirl[:, lanes], vort[:, lanes]
    product = 2.0 * back[:, lanes] * u
    u_z = slope_z(u, from_prev[pl.ds(320 + tile, 1), :], from_next[pl.ds(320 + tile, 1), :])
    p_z = slope_z(product, from_prev[pl.ds(328 + tile, 1), :], from_next[pl.ds(328 + tile, 1), :])
    w_z = slope_z(w, from_prev[pl.ds(336 + tile, 1), :], from_next[pl.ds(336 + tile, 1), :])
    swirl_out[...] = swirl_coef[...] * u - vel_r[...] * u_r - vel_z[...] * u_z
    vort_out[...] = vort_coef[...] * w - vel_r[...] * w_r - vel_z[...] * w_z + p_z


def run_rates(swirl, vort, back, from_west, from_east, from_prev, from_next, vel_r, vel_z, swirl_coef, vort_coef):
    block = pl.BlockSpec((ROWS, 128), lambda t: (0, t))

    def whole(shape):
        return pl.BlockSpec(shape, lambda t: (0, 0))

    big = whole((ROWS, COLS))
    return pl.pallas_call(
        rates_kernel,
        grid=(COLS // 128,),
        out_shape=(shaped(ROWS, COLS), shaped(ROWS, COLS)),
        in_specs=[big] * 3 + [whole((ROWS + 32, 128))] * 2 + [whole((344, 128))] * 2 + [block] * 4,
        out_specs=[block] * 2,
        name="rates",
        cost_estimate=pl.CostEstimate(flops=30 * ROWS * COLS, bytes_accessed=36 * ROWS * COLS, transcendentals=0),
        **params(60),
    )(swirl, vort, back, from_west, from_east, from_prev, from_next, vel_r, vel_z, swirl_coef, vort_coef)


def both_ways(axis, up, down):
    count = lax.axis_size(axis)
    ahead = [(i, i + 1) for i in range(count - 1)]
    back = [(i + 1, i) for i in range(count - 1)]
    return lax.ppermute(up, axis, ahead), lax.ppermute(down, axis, back)


def per_device(swirl, vorticity, base_swirl, vel_r, vel_z, swirl_coef, vort_coef):
    devices = lax.axis_size("gz") * lax.axis_size("row")
    part, to_east, to_west, planes = run_first(vorticity, swirl)
    from_west, from_east = both_ways("row", to_east, to_west)
    whole, to_next, to_prev = run_second(part, from_west, from_east, planes, vorticity, swirl, base_swirl)
    from_prev, from_next = both_ways("gz", to_next, to_prev)
    basis, message = run_third(whole, from_prev, from_next, devices)
    grams = lax.all_to_all(message, AXES, 0, 0, tiled=True)
    potential = run_fourth(grams, basis, planes, from_west, from_east, from_prev, from_next)
    swirl_rate, vort_rate = run_rates(
        swirl, vorticity, base_swirl, from_west, from_east, from_prev, from_next, vel_r, vel_z, swirl_coef, vort_coef
    )
    return swirl_rate, vort_rate, potential


def solution(mesh):
    spec = P("gz", "row")
    return jax.shard_map(per_device, mesh=mesh, in_specs=(spec,) * 7, out_specs=(spec,) * 3, check_vma=False)
```

```python
import functools

import jax
import jax.numpy as jnp
from jax import lax
from jax.experimental import pallas as pl
from jax.experimental.pallas import tpu as pltpu
from jax.sharding import PartitionSpec as P

LEVELS = 3
ITERS = 10
BASIS = ITERS + 1
PAIRS = [(i, j) for i in range(BASIS) for j in range(i, BASIS)]
SLOTS = 72
AXES = ("gz", "row")

ROWS, COLS = 192, 1024
SPAN = 32
PAD = 8
TALL = SPAN + 2 * PAD
F32 = jnp.float32


def iota(shape, dim):
    return lax.broadcasted_iota(jnp.int32, shape, dim)


def place():
    return lax.axis_index("gz"), lax.axis_index("row"), lax.axis_size("gz"), lax.axis_size("row")


def lanes_inside(cols, width, row, row_count):
    low = jnp.where(row == 0, 0, -width)
    high = jnp.where(row == row_count - 1, width, 2 * width)
    return (cols >= low) & (cols < high)


def planes_of(level):
    return 8 >> level


def plane_rows(level):
    return planes_of(level) * (planes_of(level) + 1) * TALL


def base(level, b, p):
    return (b * (planes_of(level) + 1) + p) * TALL


COEF_AT = [0, 9, 14]
COEF_ROWS = 2 * 8 * 17


def main_q():
    lane = iota((8, 128), 1)
    return 16 * (lane & 7) + lax.shift_right_logical(lane, 3)


def side_cols():
    lane = iota((8, 128), 1)
    return jnp.where(lane < 64, lane + COLS, lane - 128)


def fill_coefs(coef):
    _, row, _, _ = place()
    for level in range(LEVELS):
        count = planes_of(level)
        spacing = float(2**level)
        for p in range(count + 1):
            if p < count:
                cols = count * main_q() + p
            else:
                cols = lax.shift_right_arithmetic(side_cols(), level)
            cols = cols + row * (COLS >> level)
            term = (1.5 * spacing) / (spacing * (cols.astype(F32) + 0.5) + 16.0)
            at = 16 * (COEF_AT[level] + p)
            coef[at : at + 8, :] = 1.0 + term
            coef[at + 8 : at + 16, :] = 1.0 - term


def coefs_of(coef, level, p):
    at = 16 * (COEF_AT[level] + p)
    return coef[at : at + 8, :], coef[at + 8 : at + 16, :]


def turn(x, by):
    return pltpu.roll(x, by % 128, 1)


def view_of(ref, level, b, p, k):
    return ref.at[pl.ds(pl.multiple_of(base(level, b, p) + 8 * k, 8), 24), :]


def here_of(ref, level, b, p, k):
    return view_of(ref, level, b, p, k)[8:16, :]


def put(ref, level, b, p, k, value):
    ref[pl.ds(pl.multiple_of(base(level, b, p) + PAD + 8 * k, 8), 8), :] = value


def vertical(ref, level, b, p, k):
    count = planes_of(level)
    above = view_of(ref, level, b - 1, p, k)[8:16, :] if b > 0 else view_of(ref, level, count - 1, p, k)[7:15, :]
    below = view_of(ref, level, b + 1, p, k)[8:16, :] if b < count - 1 else view_of(ref, level, 0, p, k)[9:17, :]
    return above + below


def beside_main(ref, coef, level, b, p, k):
    count = planes_of(level)
    step = 2**level
    lane = iota((8, 128), 1)
    east, west = coefs_of(coef, level, p)
    if p < count - 1:
        right = here_of(ref, level, b, p + 1, k)
    else:
        first, side = here_of(ref, level, b, 0, k), here_of(ref, level, b, count, k)
        right = jnp.where(lane < 120, turn(first, -8), turn(first, -9))
        right = jnp.where(lane == 127, turn(side, -1), right)
    if p > 0:
        left = here_of(ref, level, b, p - 1, k)
    else:
        last, side = here_of(ref, level, b, count - 1, k), here_of(ref, level, b, count, k)
        left = jnp.where(lane >= 8, turn(last, 8), turn(last, 9))
        left = jnp.where(lane == 0, turn(side, step), left)
    return (vertical(ref, level, b, p, k) + east * right) + west * left


def beside_side(ref, coef, level, b, k):
    count = planes_of(level)
    step = 2**level
    lane = iota((8, 128), 1)
    east, west = coefs_of(coef, level, count)
    side = here_of(ref, level, b, count, k)
    first, last = here_of(ref, level, b, 0, k), here_of(ref, level, b, count - 1, k)
    right = jnp.where(lane == 128 - step, turn(first, 128 - step), turn(side, -step))
    left = jnp.where(lane == 0, turn(last, 1), turn(side, step))
    return (vertical(ref, level, b, count, k) + east * right) + west * left


def odd_side(level, b):
    return ((lax.shift_right_logical(iota((8, 128), 1), level) + b) & 1) == 1


def inside_factors(k):
    gz, row, gz_count, row_count = place()
    low = jnp.where(gz == 0, 4, 0)
    high = jnp.where(gz == gz_count - 1, SPAN - 4, SPAN)
    at = iota((8, 128), 0) + 8 * k
    main = jnp.where((at >= low) & (at < high), 1.0, 0.0).astype(F32)
    lane = iota((8, 128), 1)
    first = jnp.where(row == row_count - 1, 64, 0)
    after = jnp.where(row == 0, 64, 128)
    return main, jnp.where((lane >= first) & (lane < after), main, 0.0)


def chunks(level, body):
    def write(stores):
        for ref, at, b, p, k, value in stores:
            put(ref, at, b, p, k, value)

    if level == 0:
        pl.loop(0, SPAN // 8)(lambda k: write(body(k)))
    else:
        write([store for k in range(SPAN // 8) for store in body(k)])


def down_level(level, source, black, coarse, coef):
    count = planes_of(level)
    step = 2**level
    keep = (lax.shift_right_logical(iota((8, 128), 1), level) & 1) == 0

    def sweep(k):
        main, side = inside_factors(k)
        main, side = 0.25 * main, 0.25 * side
        stores = []
        for b in range(count):
            beside = beside_side(source, coef, level, b, k)
            value = (here_of(source, level, b, count, k) + 0.25 * beside) * side
            stores.append((black, level, b, count, k, jnp.where(odd_side(level, b), value, 0.0)))
            for p in range(1 - b % 2, count, 2):
                beside = beside_main(source, coef, level, b, p, k)
                value = (here_of(source, level, b, p, k) + 0.25 * beside) * main
                stores.append((black, level, b, p, k, value))
        return stores

    def restrict(k):
        main, side = inside_factors(k)
        stores = []
        for b in range(0, count, 2):
            even = beside_side(black, coef, level, b, k)
            odd = turn(beside_side(black, coef, level, b + 1, k), -step)
            value = jnp.where(keep, (even + odd) * side, 0.0)
            stores.append((coarse, level + 1, b // 2, count // 2, k, value))
            for p in range(0, count, 2):
                value = beside_main(black, coef, level, b, p, k) + beside_main(black, coef, level, b + 1, p + 1, k)
                stores.append((coarse, level + 1, b // 2, p // 2, k, value * main))
        return stores

    chunks(level, sweep)
    chunks(level, restrict)


def up_level(level, source, black, error, coef):
    count = planes_of(level)
    step = 2**level
    moved = (lax.shift_right_logical(iota((8, 128), 1), level) & 1) == 1

    def correct(k):
        stores = []
        for b in range(count):
            value = here_of(error, level + 1, b // 2, count // 2, k)
            value = jnp.where(moved, turn(value, step), value)
            value = here_of(black, level, b, count, k) + value
            stores.append((black, level, b, count, k, jnp.where(odd_side(level, b), value, 0.0)))
            for p in range(1 - b % 2, count, 2):
                value = here_of(error, level + 1, b // 2, p // 2, k)
                stores.append((black, level, b, p, k, here_of(black, level, b, p, k) + value))
        return stores

    def sweep(colour, k):
        main, side = inside_factors(k)
        main, side = 0.25 * main, 0.25 * side
        stores = []
        for b in range(count):
            beside = beside_side(black, coef, level, b, k)
            value = (here_of(source, level, b, count, k) + beside) * side
            mine = odd_side(level, b + 1 - colour)
            stores.append((black, level, b, count, k, jnp.where(mine, value, here_of(black, level, b, count, k))))
            for p in range((b + colour) % 2, count, 2):
                beside = beside_main(black, coef, level, b, p, k)
                stores.append((black, level, b, p, k, (here_of(source, level, b, p, k) + beside) * main))
        return stores

    chunks(level, correct)
    chunks(level, functools.partial(sweep, 0))
    chunks(level, functools.partial(sweep, 1))


def zero_pads(refs):
    for level, ref in refs:
        for b in range(planes_of(level)):
            for p in range(planes_of(level) + 1):
                at = base(level, b, p)
                ref[at : at + PAD, :] = jnp.zeros((PAD, 128), F32)
                ref[at + PAD + SPAN : at + TALL, :] = jnp.zeros((PAD, 128), F32)


def picked(x, pick):
    return jnp.take_along_axis(x, pick, axis=1)


def exchanged(tiles):
    tiles = list(tiles)
    lane = iota(tiles[0].shape, 1)
    for bit in range(3):
        far = 2**bit
        low = (lax.shift_right_logical(lane, bit) & 1) == 0
        for k in range(8):
            if not k & far:
                a, c = tiles[k], tiles[k + far]
                tiles[k] = jnp.where(low, a, turn(c, far))
                tiles[k + far] = jnp.where(low, turn(a, -far), c)
    return tiles


def two_sum(a, b):
    total = a + b
    part = total - a
    return total, (a - (total - part)) + (b - part)


def halves(a):
    wide = a * 4097.0
    high = wide - (wide - a)
    return high, a - high


def two_prod(a, b):
    total = a * b
    ah, al = halves(a)
    bh, bl = halves(b)
    return total, ((ah * bh - total) + ah * bl + al * bh) + al * bl


def dd_add(a, b):
    total, rest = two_sum(a[0], b[0])
    rest = rest + (a[1] + b[1])
    high = total + rest
    return high, rest - (high - total)


def dd_mul(a, b):
    total, rest = two_prod(a[0], b[0])
    rest = rest + (a[0] * b[1] + a[1] * b[0])
    high = total + rest
    return high, rest - (high - total)


BAND = 32


def first_kernel(
    vort_hbm, swirl_first, swirl_last, part, to_east, to_west, planes, s0, s1, s2, s3, b0, b1, b2, coef, vort, arrived
):
    copies = []
    for band in range(ROWS // BAND):
        rows = pl.ds(BAND * band, BAND)
        copies.append(pltpu.make_async_copy(vort_hbm.at[rows, :], vort.at[rows, :], arrived.at[band]))
        copies[-1].start()
    fill_coefs(coef)
    zero_pads(((0, s0), (1, s1), (2, s2), (0, b0), (1, b1), (2, b2)))
    low = iota((BAND, 128), 1) < 64
    for b in range(8):
        for p in range(8):
            at = base(0, b, p) + PAD
            s0[at : at + 4, :] = jnp.zeros((4, 128), F32)
            s0[at + 28 : at + 32, :] = jnp.zeros((4, 128), F32)
        at = base(0, b, 8) + PAD
        s0[at : at + SPAN, :] = jnp.zeros((SPAN, 128), F32)
    for band in range(ROWS // BAND):
        copies[band].wait()
        rows = slice(BAND * band, BAND * band + BAND)
        tiles = [vort[rows, 128 * k : 128 * k + 128] for k in range(8)]
        to_east[rows, :] = jnp.where(low, turn(swirl_last[rows, :], 64), tiles[7])
        to_west[rows, :] = jnp.where(low, tiles[0], turn(swirl_first[rows, :], 64))
        for p, tile in enumerate(exchanged(tiles)):
            for part_of in range(BAND // 8):
                g = BAND // 8 * band + part_of
                s0[pl.ds(base(0, 0, p) + PAD + 4 + g, 8, stride=9 * TALL), :] = tile[8 * part_of : 8 * part_of + 8]
    for b in range(8):
        for p in range(8):
            at = base(0, b, p) + PAD + 4
            planes[24 * (8 * b + p) : 24 * (8 * b + p) + 24, :] = s0[at : at + 24, :]
    down_level(0, s0, b0, s1, coef)
    down_level(1, s1, b1, s2, coef)
    down_level(2, s2, b2, s3, coef)

    scale = 1.0 / float(4**LEVELS)
    main = s3[PAD : PAD + SPAN, :] * scale
    side = s3[TALL + PAD : TALL + PAD + SPAN, :] * scale
    lane = iota((SPAN, 128), 1)
    main = picked(main, 8 * (lane & 15) + lax.shift_right_logical(lane, 4))
    side = jnp.where((lane < 8) | (lane >= 120), picked(side, 8 * (lane & 15)), 0.0)
    part[:, :128] = main
    part[:, 128:] = side
    high = lane >= 64
    to_east[ROWS:, :] = jnp.where(high, main, side)
    to_west[ROWS:, :] = jnp.where(high, side, main)


def level_scratch():
    sources = [pltpu.VMEM((plane_rows(level), 128), F32) for level in range(LEVELS + 1)]
    blacks = [pltpu.VMEM((plane_rows(level), 128), F32) for level in range(LEVELS)]
    return sources + blacks + [pltpu.VMEM((COEF_ROWS, 128), F32)]


def vmem():
    return pl.BlockSpec(memory_space=pltpu.VMEM)


def shaped(*dims):
    return jax.ShapeDtypeStruct(dims, F32)


def params(mebibytes):
    return dict(compiler_params=pltpu.CompilerParams(vmem_limit_bytes=mebibytes * 2**20))


def run_first(vort, swirl):
    return pl.pallas_call(
        first_kernel,
        grid=(1,),
        out_shape=(shaped(32, 256), shaped(ROWS + 32, 128), shaped(ROWS + 32, 128), shaped(64 * 24, 128)),
        in_specs=[
            pl.BlockSpec(memory_space=pl.ANY),
            pl.BlockSpec((ROWS, 128), lambda t: (0, 0)),
            pl.BlockSpec((ROWS, 128), lambda t: (0, COLS // 128 - 1)),
        ],
        out_specs=[vmem()] * 4,
        scratch_shapes=level_scratch() + [pltpu.VMEM((ROWS, COLS), F32), pltpu.SemaphoreType.DMA((ROWS // BAND,))],
        name="down_own",
        **params(56),
    )(vort, swirl, swirl)


def second_kernel(part, from_west, from_east, planes, vort_top, vort_end, swirl_top, swirl_end, base_top, base_end, whole, to_next, to_prev):
    high = iota((32, 128), 1) >= 64
    west, east = from_west[ROWS:, :], from_east[ROWS:, :]
    main = part[:, :128] + jnp.where(high, east, west)
    side = part[:, 128:] + jnp.where(high, west, east)
    whole[:, :128] = main
    whole[:, 128:] = side
    low = iota((4, 128), 1) < 64
    ends = ((to_next, 20, 7, slice(16, 32), vort_end, swirl_end, base_end), (to_prev, 0, 0, slice(0, 16), vort_top, swirl_top, base_top))
    for dest, g, edge, rows, vort, swirl, back in ends:
        for b in range(8):
            for p in range(8):
                at = 4 * (9 * b + p)
                dest[at : at + 4, :] = planes[24 * (8 * b + p) + g : 24 * (8 * b + p) + g + 4, :]
            at = 4 * (9 * b + 8)
            beyond = (from_east[pl.ds(8 * g + b, 4, stride=8), :], from_west[pl.ds(8 * g + b, 4, stride=8), :])
            dest[at : at + 4, :] = jnp.where(low, beyond[0], beyond[1])
        for tile in range(COLS // 128):
            lanes = slice(128 * tile, 128 * tile + 128)
            row = swirl[edge : edge + 1, lanes]
            dest[320 + tile : 321 + tile, :] = row
            dest[328 + tile : 329 + tile, :] = 2.0 * back[edge : edge + 1, lanes] * row
            dest[336 + tile : 337 + tile, :] = vort[edge : edge + 1, lanes]
        dest[288:304, :] = main[rows]
        dest[304:320, :] = side[rows]


def run_second(part, from_west, from_east, planes, vort, swirl, back):
    top = pl.BlockSpec((8, COLS), lambda t: (0, 0))
    end = pl.BlockSpec((8, COLS), lambda t: (ROWS // 8 - 1, 0))
    return pl.pallas_call(
        second_kernel,
        grid=(1,),
        out_shape=(shaped(32, 256), shaped(344, 128), shaped(344, 128)),
        in_specs=[vmem()] * 4 + [top, end] * 3,
        out_specs=[vmem()] * 3,
        name="pack_gz",
        **params(40),
    )(part, from_west, from_east, planes, vort, vort, swirl, swirl, back, back)


def third_kernel(whole, from_prev, from_next, basis, message, grid, gram_high, gram_low):
    gz, row, gz_count, row_count = place()
    grid[...] = jnp.zeros((48, 256), F32)
    grid[8:40, :] = whole[...]
    grid[0:16, :128] += from_prev[288:304, :]
    grid[0:16, 128:] += from_prev[304:320, :]
    grid[32:48, :128] += from_next[288:304, :]
    grid[32:48, 128:] += from_next[304:320, :]

    lane = iota((48, 256), 1)
    cols = jnp.where(lane < 192, lane, lane - 256)
    width = COLS >> LEVELS
    at = iota((48, 256), 0) - 12
    inside = lanes_inside(cols, width, row, row_count)
    low = jnp.where(gz == 0, 0, -64)
    high = jnp.where(gz == gz_count - 1, ROWS >> LEVELS, 128)
    inside = inside & (at >= low) & (at < high)
    spacing = float(2**LEVELS)
    radius = spacing * ((cols + row * width).astype(F32) + 0.5) + 16.0
    term = (1.5 * spacing) / radius
    east = jnp.where(inside, 0.25 + 0.25 * term, 0.0)
    west = jnp.where(inside, 0.25 - 0.25 * term, 0.0)
    quarter = jnp.where(inside, 0.25, 0.0)

    def average(x):
        total = quarter * (pltpu.roll(x, 1, 0) + pltpu.roll(x, 47, 0))
        total = total + east * pltpu.roll(x, 255, 1)
        return total + west * pltpu.roll(x, 1, 1)

    source = jnp.where(inside, grid[...], 0.0)
    older = source - average(source)
    newer = average(older)
    vectors = [source, older, newer]
    for _ in range(BASIS - 3):
        older, newer = newer, 2.0 * average(newer) - older
        vectors.append(newer)
    at = iota((32, 128), 0)
    own = (at >= 4) & (at < 28)
    parts = []
    for k in range(BASIS):
        if k < ITERS:
            basis[32 * k : 32 * k + 32, :] = vectors[k][8:40]
        masked = jnp.where(own, vectors[k][8:40, :128], 0.0)
        parts.append((masked,) + halves(masked))
    for slot, (i, j) in enumerate(PAIRS):
        a, ah, al = parts[i]
        b, bh, bl = parts[j]
        product = a * b
        error = ((ah * bh - product) + ah * bl + al * bh) + al * bl
        top, first = two_sum(product[0:8], product[8:16])
        bottom, second = two_sum(product[16:24], product[24:32])
        total, third = two_sum(top, bottom)
        rest = (error[0:8] + error[8:16]) + (error[16:24] + error[24:32])
        gram_high[8 * slot : 8 * slot + 8, :] = total
        gram_low[8 * slot : 8 * slot + 8, :] = rest + (first + second + third)
    gram_high[8 * len(PAIRS) :, :] = jnp.zeros((8 * (SLOTS - len(PAIRS)), 128), F32)
    gram_low[8 * len(PAIRS) :, :] = jnp.zeros((8 * (SLOTS - len(PAIRS)), 128), F32)
    total = None
    for s in range(8):
        term = (gram_high[pl.ds(s, SLOTS, stride=8), :], gram_low[pl.ds(s, SLOTS, stride=8), :])
        total = term if total is None else dd_add(total, term)
    for by in (64, 32, 16, 8, 4, 2, 1):
        total = dd_add(total, tuple(pltpu.roll(t, by, 1) for t in total))
    slot = iota((SLOTS, 128), 0)
    lane = iota((SLOTS, 128), 1)
    keep = lane < 0
    for number, (i, j) in enumerate(PAIRS):
        keep = keep | ((slot == number) & ((lane == BASIS * i + j) | (lane == BASIS * j + i)))
    rows = [jnp.sum(jnp.where(keep, t, 0.0), axis=0, keepdims=True) for t in total]
    odd = (iota(message.shape, 0) & 1) == 1
    message[...] = jnp.where(odd, rows[1], rows[0])


def run_third(whole, from_prev, from_next, devices):
    return pl.pallas_call(
        third_kernel,
        out_shape=(shaped(32 * ITERS, 256), shaped(2 * devices, 128)),
        in_specs=[vmem()] * 3,
        out_specs=[vmem()] * 2,
        scratch_shapes=[pltpu.VMEM((48, 256), F32), pltpu.VMEM((8 * SLOTS, 128), F32), pltpu.VMEM((8 * SLOTS, 128), F32)],
        name="basis_gram",
        **params(40),
    )(whole, from_prev, from_next)


def sum_of(terms):
    terms = list(terms)
    while len(terms) > 1:
        added = []
        for left, right in zip(terms[::2], terms[1::2]):
            total, rest = two_sum(left[0], right[0])
            added.append((total, rest + (left[1] + right[1])))
        terms = added + terms[len(terms) // 2 * 2 :]
    return terms[0]


def tidy(pair):
    high = pair[0] + pair[1]
    return high, pair[1] - (high - pair[0])


def coarse_coefs(grams, held, cells):
    devices = grams.shape[0] // 2
    gram = (grams[pl.ds(0, devices, stride=2), :], grams[pl.ds(1, devices, stride=2), :])
    while gram[0].shape[0] > 8:
        half = gram[0].shape[0] // 2
        gram = dd_add(tuple(g[:half] for g in gram), tuple(g[half:] for g in gram))
    for by in (4, 2, 1):
        gram = dd_add(gram, tuple(pltpu.roll(g, by, 0) for g in gram))

    lane = iota((16, 128), 0)
    gram = tuple(jnp.concatenate([g, g], axis=0) for g in gram)
    columns = []
    for j in range(BASIS):
        pick = jnp.minimum(lane * BASIS + j, BASIS * BASIS - 1)
        high, low = (jnp.where(lane < BASIS, picked(g, pick), 0.0) for g in gram)
        columns.append((high, low) + halves(high))

    index = iota((16, 128), 0)
    below = jnp.where(index == 0, 0.0, jnp.where(index == 1, -1.0, jnp.where(index == 2, 1.0, 0.5)))
    below = jnp.where(index < BASIS, below, 0.0)
    above = jnp.where((index > 0) & (index < BASIS - 1), 0.5, 0.0)
    same = jnp.where((index > 0) & (index < BASIS), 1.0, 0.0)

    def image(a):
        moved = sum_of([tuple(below * pltpu.roll(t, 1, 0) for t in a), tuple(above * pltpu.roll(t, 15, 0) for t in a)])
        return tidy(sum_of([tuple(same * t for t in a), tuple(-t for t in moved)]))

    a = (jnp.where(index == 0, 1.0, 0.0), jnp.zeros((16, 128), F32))
    solved = jnp.zeros((16, 128), F32)
    tiny = float(4 ** (2 * LEVELS)) / 16.0 * cells * 1e-12
    for _ in range(ITERS):
        b = image(a)
        held[0:16, :] = b[0]
        held[16:32, :] = b[1]
        terms = []
        for j, (high, low, upper, lower) in enumerate(columns):
            at_j = jnp.broadcast_to(held[j : j + 1, :], (16, 128))
            rest_j = jnp.broadcast_to(held[16 + j : 17 + j, :], (16, 128))
            jh, jl = halves(at_j)
            product = high * at_j
            rest = ((upper * jh - product) + upper * jl + lower * jh) + lower * jl
            terms.append((product, rest + (high * rest_j + low * at_j)))
        image_gram = tidy(sum_of(terms))
        forms = []
        for left in (a, b):
            high, rest = two_prod(left[0], image_gram[0])
            form = (high, rest + (left[0] * image_gram[1] + left[1] * image_gram[0]))
            form = sum_of([tuple(t[:8] for t in form), tuple(t[8:] for t in form)])
            for by in (4, 2, 1):
                form = sum_of([form, tuple(pltpu.roll(t, by, 0) for t in form)])
            forms.append(form[0] + form[1])
        alpha = forms[0] / (forms[1] + tiny)
        alpha = jnp.concatenate([alpha, alpha], axis=0)
        solved = solved + alpha * a[0]
        high, rest = two_prod(alpha, b[0])
        a = tidy(sum_of([a, (-high, -(rest + alpha * b[1]))]))
    return solved * (float(4**LEVELS) * 0.25)


def fourth_kernel(
    grams, basis, planes, from_west, from_east, from_prev, from_next, out,
    s0, s1, s2, s3, b0, b1, b2, coef, held, *, cells,
):
    fill_coefs(coef)
    zero_pads(((0, s0), (1, s1), (2, s2), (0, b0), (1, b1), (2, b2)))
    low = iota((24, 128), 1) < 64
    for b in range(8):
        for p in range(9):
            at = base(0, b, p) + PAD
            edge = 4 * (9 * b + p)
            s0[at : at + 4, :] = from_prev[edge : edge + 4, :]
            s0[at + 28 : at + 32, :] = from_next[edge : edge + 4, :]
            if p < 8:
                s0[at + 4 : at + 28, :] = planes[24 * (8 * b + p) : 24 * (8 * b + p) + 24, :]
            else:
                beyond = (from_east[pl.ds(b, 24, stride=8), :], from_west[pl.ds(b, 24, stride=8), :])
                s0[at + 4 : at + 28, :] = jnp.where(low, beyond[0], beyond[1])
    down_level(0, s0, b0, s1, coef)
    down_level(1, s1, b1, s2, coef)
    down_level(2, s2, b2, s3, coef)

    solved = coarse_coefs(grams, held, cells)
    value = jnp.zeros((32, 256), F32)
    for k in range(ITERS):
        value = value + solved[k : k + 1, 0:1] * basis[32 * k : 32 * k + 32, :]
    lane = iota((SPAN, 128), 1)
    side = value[:, 128:]
    far = lax.shift_right_logical(lane, 3)
    s3[PAD : PAD + SPAN, :] = picked(value[:, :128], 16 * (lane & 7) + far)
    s3[TALL + PAD : TALL + PAD + SPAN, :] = picked(side, jnp.where(lane < 64, far, far + 112))
    up_level(2, s2, b2, s3, coef)
    up_level(1, s1, b1, b2, coef)
    up_level(0, s0, b0, b1, coef)
    for band in range(ROWS // BAND):
        tiles = []
        for p in range(8):
            at = base(0, 0, p) + PAD + 4 + BAND // 8 * band
            tiles.append(jnp.concatenate([b0[pl.ds(at + g, 8, stride=9 * TALL), :] for g in range(BAND // 8)], axis=0))
        for k, tile in enumerate(exchanged(tiles)):
            out[BAND * band : BAND * band + BAND, 128 * k : 128 * k + 128] = tile


def run_fourth(grams, basis, planes, from_west, from_east, from_prev, from_next):
    cells = float((ROWS >> LEVELS) * (COLS >> LEVELS) * lax.axis_size("gz") * lax.axis_size("row"))
    return pl.pallas_call(
        functools.partial(fourth_kernel, cells=cells),
        out_shape=shaped(ROWS, COLS),
        in_specs=[vmem()] * 7,
        out_specs=vmem(),
        scratch_shapes=level_scratch() + [pltpu.VMEM((32, 128), F32)],
        name="v_cycle",
        **params(40),
    )(grams, basis, planes, from_west, from_east, from_prev, from_next)


def rates_kernel(
    swirl, vort, back, from_west, from_east, from_prev, from_next, vel_r, vel_z, swirl_coef, vort_coef, swirl_out, vort_out
):
    tile = pl.program_id(0)
    lane = iota((ROWS, 128), 1)
    at = iota((ROWS, 128), 0)
    start = pl.multiple_of(128 * tile, 128)
    lanes = pl.ds(start, 128)
    before = pl.ds(pl.multiple_of(jnp.maximum(start - 128, 0), 128), 128)
    after = pl.ds(pl.multiple_of(jnp.minimum(start + 128, COLS - 128), 128), 128)

    def slope_r(ref, west, east):
        here = ref[:, lanes]
        left = jnp.where(tile == 0, west, pltpu.roll(ref[:, before], 1, 1))
        right = jnp.where(tile == COLS // 128 - 1, east, pltpu.roll(ref[:, after], 127, 1))
        ahead = jnp.where(lane == 127, right, pltpu.roll(here, 127, 1))
        behind = jnp.where(lane == 0, left, pltpu.roll(here, 1, 1))
        return (ahead - behind) * 0.5

    def slope_z(here, top, bottom):
        ahead = jnp.where(at == ROWS - 1, bottom, pltpu.roll(here, ROWS - 1, 0))
        behind = jnp.where(at == 0, top, pltpu.roll(here, 1, 0))
        return (ahead - behind) * 0.5

    west, east = from_west[:ROWS, :], from_east[:ROWS, :]
    u_r = slope_r(swirl, turn(west, 65), turn(east, 63))
    w_r = slope_r(vort, pltpu.roll(west, 1, 1), pltpu.roll(east, 127, 1))
    u, w = swirl[:, lanes], vort[:, lanes]
    product = 2.0 * back[:, lanes] * u
    u_z = slope_z(u, from_prev[pl.ds(320 + tile, 1), :], from_next[pl.ds(320 + tile, 1), :])
    p_z = slope_z(product, from_prev[pl.ds(328 + tile, 1), :], from_next[pl.ds(328 + tile, 1), :])
    w_z = slope_z(w, from_prev[pl.ds(336 + tile, 1), :], from_next[pl.ds(336 + tile, 1), :])
    swirl_out[...] = swirl_coef[...] * u - vel_r[...] * u_r - vel_z[...] * u_z
    vort_out[...] = vort_coef[...] * w - vel_r[...] * w_r - vel_z[...] * w_z + p_z


def run_rates(swirl, vort, back, from_west, from_east, from_prev, from_next, vel_r, vel_z, swirl_coef, vort_coef):
    block = pl.BlockSpec((ROWS, 128), lambda t: (0, t))

    def whole(shape):
        return pl.BlockSpec(shape, lambda t: (0, 0))

    big = whole((ROWS, COLS))
    return pl.pallas_call(
        rates_kernel,
        grid=(COLS // 128,),
        out_shape=(shaped(ROWS, COLS), shaped(ROWS, COLS)),
        in_specs=[big] * 3 + [whole((ROWS + 32, 128))] * 2 + [whole((344, 128))] * 2 + [block] * 4,
        out_specs=[block] * 2,
        name="rates",
        cost_estimate=pl.CostEstimate(flops=30 * ROWS * COLS, bytes_accessed=36 * ROWS * COLS, transcendentals=0),
        **params(60),
    )(swirl, vort, back, from_west, from_east, from_prev, from_next, vel_r, vel_z, swirl_coef, vort_coef)


def both_ways(axis, up, down):
    count = lax.axis_size(axis)
    ahead = [(i, i + 1) for i in range(count - 1)]
    back = [(i + 1, i) for i in range(count - 1)]
    return lax.ppermute(up, axis, ahead), lax.ppermute(down, axis, back)


def per_device(swirl, vorticity, base_swirl, vel_r, vel_z, swirl_coef, vort_coef):
    devices = lax.axis_size("gz") * lax.axis_size("row")
    part, to_east, to_west, planes = run_first(vorticity, swirl)
    from_west, from_east = both_ways("row", to_east, to_west)
    whole, to_next, to_prev = run_second(part, from_west, from_east, planes, vorticity, swirl, base_swirl)
    from_prev, from_next = both_ways("gz", to_next, to_prev)
    basis, message = run_third(whole, from_prev, from_next, devices)
    grams = lax.all_to_all(message, AXES, 0, 0, tiled=True)
    potential = run_fourth(grams, basis, planes, from_west, from_east, from_prev, from_next)
    swirl_rate, vort_rate = run_rates(
        swirl, vorticity, base_swirl, from_west, from_east, from_prev, from_next, vel_r, vel_z, swirl_coef, vort_coef
    )
    return swirl_rate, vort_rate, potential


def solution(mesh):
    spec = P("gz", "row")
    return jax.shard_map(per_device, mesh=mesh, in_specs=(spec,) * 7, out_specs=(spec,) * 3, check_vma=False)
```

```python
import functools

import jax
import jax.numpy as jnp
from jax import lax
from jax.experimental import pallas as pl
from jax.experimental.pallas import tpu as pltpu
from jax.sharding import PartitionSpec as P

LEVELS = 3
ITERS = 10
BASIS = ITERS + 1
PAIRS = [(i, j) for i in range(BASIS) for j in range(i, BASIS)]
SLOTS = 72
AXES = ("gz", "row")

ROWS, COLS = 192, 1024
SPAN = 32
PAD = 8
TALL = SPAN + 2 * PAD
F32 = jnp.float32


def iota(shape, dim):
    return lax.broadcasted_iota(jnp.int32, shape, dim)


def place():
    return lax.axis_index("gz"), lax.axis_index("row"), lax.axis_size("gz"), lax.axis_size("row")


def lanes_inside(cols, width, row, row_count):
    low = jnp.where(row == 0, 0, -width)
    high = jnp.where(row == row_count - 1, width, 2 * width)
    return (cols >= low) & (cols < high)


def planes_of(level):
    return 8 >> level


def plane_rows(level):
    return planes_of(level) * (planes_of(level) + 1) * TALL


def base(level, b, p):
    return (b * (planes_of(level) + 1) + p) * TALL


COEF_AT = [0, 9, 14]
COEF_ROWS = 2 * 8 * 17


def main_q():
    lane = iota((8, 128), 1)
    return 16 * (lane & 7) + lax.shift_right_logical(lane, 3)


def side_cols():
    lane = iota((8, 128), 1)
    return jnp.where(lane < 64, lane + COLS, lane - 128)


def fill_coefs(coef):
    _, row, _, _ = place()
    for level in range(LEVELS):
        count = planes_of(level)
        spacing = float(2**level)
        for p in range(count + 1):
            if p < count:
                cols = count * main_q() + p
            else:
                cols = lax.shift_right_arithmetic(side_cols(), level)
            cols = cols + row * (COLS >> level)
            term = (1.5 * spacing) / (spacing * (cols.astype(F32) + 0.5) + 16.0)
            at = 16 * (COEF_AT[level] + p)
            coef[at : at + 8, :] = 1.0 + term
            coef[at + 8 : at + 16, :] = 1.0 - term


def coefs_of(coef, level, p):
    at = 16 * (COEF_AT[level] + p)
    return coef[at : at + 8, :], coef[at + 8 : at + 16, :]


def turn(x, by):
    return pltpu.roll(x, by % 128, 1)


def view_of(ref, level, b, p, k):
    return ref.at[pl.ds(pl.multiple_of(base(level, b, p) + 8 * k, 8), 24), :]


def here_of(ref, level, b, p, k):
    return view_of(ref, level, b, p, k)[8:16, :]


def put(ref, level, b, p, k, value):
    ref[pl.ds(pl.multiple_of(base(level, b, p) + PAD + 8 * k, 8), 8), :] = value


def vertical(ref, level, b, p, k):
    count = planes_of(level)
    above = view_of(ref, level, b - 1, p, k)[8:16, :] if b > 0 else view_of(ref, level, count - 1, p, k)[7:15, :]
    below = view_of(ref, level, b + 1, p, k)[8:16, :] if b < count - 1 else view_of(ref, level, 0, p, k)[9:17, :]
    return above + below


def beside_main(ref, coef, level, b, p, k):
    count = planes_of(level)
    step = 2**level
    lane = iota((8, 128), 1)
    east, west = coefs_of(coef, level, p)
    if p < count - 1:
        right = here_of(ref, level, b, p + 1, k)
    else:
        first, side = here_of(ref, level, b, 0, k), here_of(ref, level, b, count, k)
        right = jnp.where(lane < 120, turn(first, -8), turn(first, -9))
        right = jnp.where(lane == 127, turn(side, -1), right)
    if p > 0:
        left = here_of(ref, level, b, p - 1, k)
    else:
        last, side = here_of(ref, level, b, count - 1, k), here_of(ref, level, b, count, k)
        left = jnp.where(lane >= 8, turn(last, 8), turn(last, 9))
        left = jnp.where(lane == 0, turn(side, step), left)
    return (vertical(ref, level, b, p, k) + east * right) + west * left


def beside_side(ref, coef, level, b, k):
    count = planes_of(level)
    step = 2**level
    lane = iota((8, 128), 1)
    east, west = coefs_of(coef, level, count)
    side = here_of(ref, level, b, count, k)
    first, last = here_of(ref, level, b, 0, k), here_of(ref, level, b, count - 1, k)
    right = jnp.where(lane == 128 - step, turn(first, 128 - step), turn(side, -step))
    left = jnp.where(lane == 0, turn(last, 1), turn(side, step))
    return (vertical(ref, level, b, count, k) + east * right) + west * left


def odd_side(level, b):
    return ((lax.shift_right_logical(iota((8, 128), 1), level) + b) & 1) == 1


def inside_factors(k):
    gz, row, gz_count, row_count = place()
    low = jnp.where(gz == 0, 4, 0)
    high = jnp.where(gz == gz_count - 1, SPAN - 4, SPAN)
    at = iota((8, 128), 0) + 8 * k
    main = jnp.where((at >= low) & (at < high), 1.0, 0.0).astype(F32)
    lane = iota((8, 128), 1)
    first = jnp.where(row == row_count - 1, 64, 0)
    after = jnp.where(row == 0, 64, 128)
    return main, jnp.where((lane >= first) & (lane < after), main, 0.0)


def chunks(level, body):
    def write(stores):
        for ref, at, b, p, k, value in stores:
            put(ref, at, b, p, k, value)

    if level == 0:
        pl.loop(0, SPAN // 8)(lambda k: write(body(k)))
    else:
        write([store for k in range(SPAN // 8) for store in body(k)])


def down_level(level, source, black, coarse, coef):
    count = planes_of(level)
    step = 2**level
    keep = (lax.shift_right_logical(iota((8, 128), 1), level) & 1) == 0

    def sweep(k):
        main, side = inside_factors(k)
        main, side = 0.25 * main, 0.25 * side
        stores = []
        for b in range(count):
            beside = beside_side(source, coef, level, b, k)
            value = (here_of(source, level, b, count, k) + 0.25 * beside) * side
            stores.append((black, level, b, count, k, jnp.where(odd_side(level, b), value, 0.0)))
            for p in range(1 - b % 2, count, 2):
                beside = beside_main(source, coef, level, b, p, k)
                value = (here_of(source, level, b, p, k) + 0.25 * beside) * main
                stores.append((black, level, b, p, k, value))
        return stores

    def restrict(k):
        main, side = inside_factors(k)
        stores = []
        for b in range(0, count, 2):
            even = beside_side(black, coef, level, b, k)
            odd = turn(beside_side(black, coef, level, b + 1, k), -step)
            value = jnp.where(keep, (even + odd) * side, 0.0)
            stores.append((coarse, level + 1, b // 2, count // 2, k, value))
            for p in range(0, count, 2):
                value = beside_main(black, coef, level, b, p, k) + beside_main(black, coef, level, b + 1, p + 1, k)
                stores.append((coarse, level + 1, b // 2, p // 2, k, value * main))
        return stores

    chunks(level, sweep)
    chunks(level, restrict)


def up_level(level, source, black, error, field, coef):
    count = planes_of(level)
    step = 2**level
    moved = (lax.shift_right_logical(iota((8, 128), 1), level) & 1) == 1

    def correct(k):
        stores = []
        for b in range(count):
            value = here_of(error, level + 1, b // 2, count // 2, k)
            value = jnp.where(moved, turn(value, step), value)
            value = here_of(black, level, b, count, k) + value
            stores.append((field, level, b, count, k, jnp.where(odd_side(level, b), value, 0.0)))
            for p in range(1 - b % 2, count, 2):
                value = here_of(error, level + 1, b // 2, p // 2, k)
                stores.append((field, level, b, p, k, here_of(black, level, b, p, k) + value))
        return stores

    def sweep(colour, k):
        main, side = inside_factors(k)
        main, side = 0.25 * main, 0.25 * side
        stores = []
        for b in range(count):
            beside = beside_side(field, coef, level, b, k)
            value = (here_of(source, level, b, count, k) + beside) * side
            mine = odd_side(level, b + 1 - colour)
            stores.append((field, level, b, count, k, jnp.where(mine, value, here_of(field, level, b, count, k))))
            for p in range((b + colour) % 2, count, 2):
                beside = beside_main(field, coef, level, b, p, k)
                stores.append((field, level, b, p, k, (here_of(source, level, b, p, k) + beside) * main))
        return stores

    chunks(level, correct)
    chunks(level, functools.partial(sweep, 0))
    chunks(level, functools.partial(sweep, 1))


def zero_pads(refs):
    for level, ref in refs:
        for b in range(planes_of(level)):
            for p in range(planes_of(level) + 1):
                at = base(level, b, p)
                ref[at : at + PAD, :] = jnp.zeros((PAD, 128), F32)
                ref[at + PAD + SPAN : at + TALL, :] = jnp.zeros((PAD, 128), F32)


def picked(x, pick):
    return jnp.take_along_axis(x, pick, axis=1)


def exchanged(tiles):
    tiles = list(tiles)
    lane = iota(tiles[0].shape, 1)
    for bit in range(3):
        far = 2**bit
        low = (lax.shift_right_logical(lane, bit) & 1) == 0
        for k in range(8):
            if not k & far:
                a, c = tiles[k], tiles[k + far]
                tiles[k] = jnp.where(low, a, turn(c, far))
                tiles[k + far] = jnp.where(low, turn(a, -far), c)
    return tiles


def two_sum(a, b):
    total = a + b
    part = total - a
    return total, (a - (total - part)) + (b - part)


def halves(a):
    wide = a * 4097.0
    high = wide - (wide - a)
    return high, a - high


def two_prod(a, b):
    total = a * b
    ah, al = halves(a)
    bh, bl = halves(b)
    return total, ((ah * bh - total) + ah * bl + al * bh) + al * bl


def dd_add(a, b):
    total, rest = two_sum(a[0], b[0])
    rest = rest + (a[1] + b[1])
    high = total + rest
    return high, rest - (high - total)


def dd_mul(a, b):
    total, rest = two_prod(a[0], b[0])
    rest = rest + (a[0] * b[1] + a[1] * b[0])
    high = total + rest
    return high, rest - (high - total)


BAND = 32
FOLD = ROWS // 4


def pack_edges(vort, swirl_first, swirl_last, to_east, to_west):
    lane = iota((FOLD, 128), 1)
    eastward = westward = None
    for run in range(4):
        rows = slice(FOLD * run, FOLD * run + FOLD)
        last = jnp.where(lane == 96, turn(swirl_last[rows, :], 97), vort[rows, COLS - 128 :])
        first = jnp.where(lane == 31, turn(swirl_first[rows, :], 31), vort[rows, :128])
        last, first = turn(last, 32 * run + 32), turn(first, 32 * run)
        mine = lax.shift_right_logical(lane, 5) == run
        eastward = last if run == 0 else jnp.where(mine, last, eastward)
        westward = first if run == 0 else jnp.where(mine, first, westward)
    to_east[:FOLD, :] = eastward
    to_west[:FOLD, :] = westward


def unpack_edges(from_west, from_east, beyond):
    lane = iota((FOLD, 128), 1)
    west, east = from_west[:FOLD, :], from_east[:FOLD, :]
    for run in range(4):
        value = jnp.where(lane >= 96, turn(west, 96 - 32 * run), 0.0)
        beyond[FOLD * run : FOLD * run + FOLD, :] = jnp.where(lane < 32, turn(east, -32 * run), value)


def first_kernel(
    vort_hbm, swirl_hbm, back_hbm, part, to_east, to_west, planes, row_top, row_end,
    s0, s1, s2, s3, b0, b1, b2, coef, vort, arrived, swirl_first, swirl_last, ends, ends_arrived,
):
    copies, extras = [], []
    for band in range(ROWS // BAND):
        rows = pl.ds(BAND * band, BAND)
        copies.append(pltpu.make_async_copy(vort_hbm.at[rows, :], vort.at[rows, :], arrived.at[band]))
        copies[-1].start()
    pieces = [(swirl_hbm.at[:, pl.ds(0, 128)], swirl_first), (swirl_hbm.at[:, pl.ds(COLS - 128, 128)], swirl_last)]
    for number, array in enumerate((swirl_hbm, back_hbm)):
        for end, first in enumerate((0, ROWS - 8)):
            pieces.append((array.at[pl.ds(first, 8), :], ends.at[2 * number + end]))
    for number, (src, dst) in enumerate(pieces):
        extras.append(pltpu.make_async_copy(src, dst, ends_arrived.at[number]))
        extras[-1].start()
    fill_coefs(coef)
    zero_pads(((0, s0), (1, s1), (2, s2), (0, b0), (1, b1), (2, b2)))
    for b in range(8):
        for p in range(8):
            at = base(0, b, p) + PAD
            s0[at : at + 4, :] = jnp.zeros((4, 128), F32)
            s0[at + 28 : at + 32, :] = jnp.zeros((4, 128), F32)
        at = base(0, b, 8) + PAD
        s0[at : at + SPAN, :] = jnp.zeros((SPAN, 128), F32)
    for band in range(ROWS // BAND):
        copies[band].wait()
        rows = slice(BAND * band, BAND * band + BAND)
        tiles = [vort[rows, 128 * k : 128 * k + 128] for k in range(8)]
        for p, tile in enumerate(exchanged(tiles)):
            for part_of in range(BAND // 8):
                g = BAND // 8 * band + part_of
                s0[pl.ds(base(0, 0, p) + PAD + 4 + g, 8, stride=9 * TALL), :] = tile[8 * part_of : 8 * part_of + 8]
    for extra in extras:
        extra.wait()
    pack_edges(vort, swirl_first, swirl_last, to_east, to_west)
    for end, (dest, row, edge) in enumerate(((row_top, 0, 0), (row_end, ROWS - 1, 7))):
        for tile in range(COLS // 128):
            lanes = slice(128 * tile, 128 * tile + 128)
            swirl = ends[end, edge : edge + 1, lanes]
            dest[tile : tile + 1, :] = swirl
            dest[8 + tile : 9 + tile, :] = 2.0 * ends[2 + end, edge : edge + 1, lanes] * swirl
            dest[16 + tile : 17 + tile, :] = vort[row : row + 1, lanes]
    for b in range(8):
        for p in range(8):
            at = base(0, b, p) + PAD + 4
            planes[24 * (8 * b + p) : 24 * (8 * b + p) + 24, :] = s0[at : at + 24, :]
    down_level(0, s0, b0, s1, coef)
    down_level(1, s1, b1, s2, coef)
    down_level(2, s2, b2, s3, coef)

    scale = 1.0 / float(4**LEVELS)
    main = s3[PAD : PAD + SPAN, :] * scale
    side = s3[TALL + PAD : TALL + PAD + SPAN, :] * scale
    lane = iota((SPAN, 128), 1)
    main = picked(main, 8 * (lane & 15) + lax.shift_right_logical(lane, 4))
    side = jnp.where((lane < 8) | (lane >= 120), picked(side, 8 * (lane & 15)), 0.0)
    part[:, :128] = main
    part[:, 128:] = side
    high = lane >= 64
    to_east[FOLD:, :] = jnp.where(high, main, side)
    to_west[FOLD:, :] = jnp.where(high, side, main)


def level_scratch():
    sources = [pltpu.VMEM((plane_rows(level), 128), F32) for level in range(LEVELS + 1)]
    blacks = [pltpu.VMEM((plane_rows(level), 128), F32) for level in range(LEVELS)]
    return sources + blacks + [pltpu.VMEM((COEF_ROWS, 128), F32)]


def vmem():
    return pl.BlockSpec(memory_space=pltpu.VMEM)


def hbm():
    return pl.BlockSpec(memory_space=pltpu.HBM)


def fixed(x):
    return pltpu.with_memory_space_constraint(x, pltpu.HBM)


def shaped(*dims):
    return jax.ShapeDtypeStruct(dims, F32)


def params(mebibytes):
    return dict(compiler_params=pltpu.CompilerParams(vmem_limit_bytes=mebibytes * 2**20))


def run_first(vort, swirl, back):
    return pl.pallas_call(
        first_kernel,
        out_shape=(shaped(32, 256), shaped(FOLD + 32, 128), shaped(FOLD + 32, 128), shaped(64 * 24, 128))
        + (shaped(24, 128),) * 2,
        in_specs=[hbm()] * 3,
        out_specs=[vmem()] * 6,
        scratch_shapes=level_scratch()
        + [pltpu.VMEM((ROWS, COLS), F32), pltpu.SemaphoreType.DMA((ROWS // BAND,))]
        + [pltpu.VMEM((ROWS, 128), F32)] * 2
        + [pltpu.VMEM((4, 8, COLS), F32), pltpu.SemaphoreType.DMA((6,))],
        name="down_own",
        **params(24),
    )(fixed(vort), fixed(swirl), fixed(back))


OUTER = 288


def second_kernel(part, from_west, from_east, planes, row_top, row_end, whole, beyond, to_next, to_prev):
    high = iota((32, 128), 1) >= 64
    west, east = from_west[FOLD:, :], from_east[FOLD:, :]
    main = part[:, :128] + jnp.where(high, east, west)
    side = part[:, 128:] + jnp.where(high, west, east)
    whole[:, :128] = main
    whole[:, 128:] = side
    unpack_edges(from_west, from_east, beyond)
    for dest, g, rows, row in ((to_next, 20, slice(16, 32), row_end), (to_prev, 0, slice(0, 16), row_top)):
        for b in range(8):
            for p in range(8):
                at = 4 * (9 * b + p)
                dest[at : at + 4, :] = planes[24 * (8 * b + p) + g : 24 * (8 * b + p) + g + 4, :]
            at = 4 * (9 * b + 8)
            dest[at : at + 4, :] = beyond[pl.ds(8 * g + b, 4, stride=8), :]
        dest[OUTER : OUTER + 16, :] = main[rows]
        dest[OUTER + 16 : OUTER + 32, :] = side[rows]
        dest[OUTER + 32 :, :] = row[...]


def run_second(part, from_west, from_east, planes, row_top, row_end):
    return pl.pallas_call(
        second_kernel,
        out_shape=(shaped(32, 256), shaped(ROWS, 128), shaped(OUTER + 56, 128), shaped(OUTER + 56, 128)),
        in_specs=[vmem()] * 6,
        out_specs=[vmem()] * 4,
        name="pack_gz",
        **params(24),
    )(part, from_west, from_east, planes, row_top, row_end)


def third_kernel(whole, from_prev, from_next, basis_out, message, grid, gram_high, gram_low, basis, moved):
    gz, row, gz_count, row_count = place()
    grid[...] = jnp.zeros((48, 256), F32)
    grid[8:40, :] = whole[...]
    grid[0:16, :128] += from_prev[OUTER : OUTER + 16, :]
    grid[0:16, 128:] += from_prev[OUTER + 16 : OUTER + 32, :]
    grid[32:48, :128] += from_next[OUTER : OUTER + 16, :]
    grid[32:48, 128:] += from_next[OUTER + 16 : OUTER + 32, :]

    lane = iota((48, 256), 1)
    cols = jnp.where(lane < 192, lane, lane - 256)
    width = COLS >> LEVELS
    at = iota((48, 256), 0) - 12
    inside = lanes_inside(cols, width, row, row_count)
    low = jnp.where(gz == 0, 0, -64)
    high = jnp.where(gz == gz_count - 1, ROWS >> LEVELS, 128)
    inside = inside & (at >= low) & (at < high)
    spacing = float(2**LEVELS)
    radius = spacing * ((cols + row * width).astype(F32) + 0.5) + 16.0
    term = (1.5 * spacing) / radius
    east = jnp.where(inside, 0.25 + 0.25 * term, 0.0)
    west = jnp.where(inside, 0.25 - 0.25 * term, 0.0)
    quarter = jnp.where(inside, 0.25, 0.0)

    def average(x):
        total = quarter * (pltpu.roll(x, 1, 0) + pltpu.roll(x, 47, 0))
        total = total + east * pltpu.roll(x, 255, 1)
        return total + west * pltpu.roll(x, 1, 1)

    source = jnp.where(inside, grid[...], 0.0)
    older = source - average(source)
    newer = average(older)
    vectors = [source, older, newer]
    for _ in range(BASIS - 3):
        older, newer = newer, 2.0 * average(newer) - older
        vectors.append(newer)
    at = iota((32, 128), 0)
    own = (at >= 4) & (at < 28)
    parts = []
    for k in range(BASIS):
        if k < ITERS:
            basis[32 * k : 32 * k + 32, :] = vectors[k][8:40]
        masked = jnp.where(own, vectors[k][8:40, :128], 0.0)
        parts.append((masked,) + halves(masked))
    copy = pltpu.make_async_copy(basis, basis_out, moved)
    copy.start()
    for slot, (i, j) in enumerate(PAIRS):
        a, ah, al = parts[i]
        b, bh, bl = parts[j]
        product = a * b
        error = ((ah * bh - product) + ah * bl + al * bh) + al * bl
        top, first = two_sum(product[0:8], product[8:16])
        bottom, second = two_sum(product[16:24], product[24:32])
        total, third = two_sum(top, bottom)
        rest = (error[0:8] + error[8:16]) + (error[16:24] + error[24:32])
        gram_high[8 * slot : 8 * slot + 8, :] = total
        gram_low[8 * slot : 8 * slot + 8, :] = rest + (first + second + third)
    gram_high[8 * len(PAIRS) :, :] = jnp.zeros((8 * (SLOTS - len(PAIRS)), 128), F32)
    gram_low[8 * len(PAIRS) :, :] = jnp.zeros((8 * (SLOTS - len(PAIRS)), 128), F32)
    total = None
    for s in range(8):
        term = (gram_high[pl.ds(s, SLOTS, stride=8), :], gram_low[pl.ds(s, SLOTS, stride=8), :])
        total = term if total is None else dd_add(total, term)
    for by in (64, 32, 16, 8, 4, 2, 1):
        total = dd_add(total, tuple(pltpu.roll(t, by, 1) for t in total))
    slot = iota((SLOTS, 128), 0)
    lane = iota((SLOTS, 128), 1)
    keep = lane < 0
    for number, (i, j) in enumerate(PAIRS):
        keep = keep | ((slot == number) & ((lane == BASIS * i + j) | (lane == BASIS * j + i)))
    rows = [jnp.sum(jnp.where(keep, t, 0.0), axis=0, keepdims=True) for t in total]
    odd = (iota(message.shape, 0) & 1) == 1
    message[...] = jnp.where(odd, rows[1], rows[0])
    copy.wait()


def run_third(whole, from_prev, from_next, devices):
    return pl.pallas_call(
        third_kernel,
        out_shape=(pltpu.HBM((32 * ITERS, 256), F32), shaped(2 * devices, 128)),
        in_specs=[vmem()] * 3,
        out_specs=[hbm(), vmem()],
        scratch_shapes=[pltpu.VMEM((48, 256), F32)]
        + [pltpu.VMEM((8 * SLOTS, 128), F32)] * 2
        + [pltpu.VMEM((32 * ITERS, 256), F32), pltpu.SemaphoreType.DMA],
        name="basis_gram",
        **params(24),
    )(whole, from_prev, from_next)


def sum_of(terms):
    terms = list(terms)
    while len(terms) > 1:
        added = []
        for left, right in zip(terms[::2], terms[1::2]):
            total, rest = two_sum(left[0], right[0])
            added.append((total, rest + (left[1] + right[1])))
        terms = added + terms[len(terms) // 2 * 2 :]
    return terms[0]


def tidy(pair):
    high = pair[0] + pair[1]
    return high, pair[1] - (high - pair[0])


def coarse_coefs(grams, held, cells):
    devices = grams.shape[0] // 2
    gram = (grams[pl.ds(0, devices, stride=2), :], grams[pl.ds(1, devices, stride=2), :])
    while gram[0].shape[0] > 8:
        half = gram[0].shape[0] // 2
        gram = dd_add(tuple(g[:half] for g in gram), tuple(g[half:] for g in gram))
    for by in (4, 2, 1):
        gram = dd_add(gram, tuple(pltpu.roll(g, by, 0) for g in gram))

    lane = iota((16, 128), 0)
    gram = tuple(jnp.concatenate([g, g], axis=0) for g in gram)
    columns = []
    for j in range(BASIS):
        pick = jnp.minimum(lane * BASIS + j, BASIS * BASIS - 1)
        high, low = (jnp.where(lane < BASIS, picked(g, pick), 0.0) for g in gram)
        columns.append((high, low) + halves(high))

    index = iota((16, 128), 0)
    below = jnp.where(index == 0, 0.0, jnp.where(index == 1, -1.0, jnp.where(index == 2, 1.0, 0.5)))
    below = jnp.where(index < BASIS, below, 0.0)
    above = jnp.where((index > 0) & (index < BASIS - 1), 0.5, 0.0)
    same = jnp.where((index > 0) & (index < BASIS), 1.0, 0.0)

    def image(a):
        moved = sum_of([tuple(below * pltpu.roll(t, 1, 0) for t in a), tuple(above * pltpu.roll(t, 15, 0) for t in a)])
        return tidy(sum_of([tuple(same * t for t in a), tuple(-t for t in moved)]))

    a = (jnp.where(index == 0, 1.0, 0.0), jnp.zeros((16, 128), F32))
    solved = jnp.zeros((16, 128), F32)
    tiny = float(4 ** (2 * LEVELS)) / 16.0 * cells * 1e-12
    for _ in range(ITERS):
        b = image(a)
        held[0:16, :] = b[0]
        held[16:32, :] = b[1]
        terms = []
        for j, (high, low, upper, lower) in enumerate(columns):
            at_j = jnp.broadcast_to(held[j : j + 1, :], (16, 128))
            rest_j = jnp.broadcast_to(held[16 + j : 17 + j, :], (16, 128))
            jh, jl = halves(at_j)
            product = high * at_j
            rest = ((upper * jh - product) + upper * jl + lower * jh) + lower * jl
            terms.append((product, rest + (high * rest_j + low * at_j)))
        image_gram = tidy(sum_of(terms))
        forms = []
        for left in (a, b):
            high, rest = two_prod(left[0], image_gram[0])
            form = (high, rest + (left[0] * image_gram[1] + left[1] * image_gram[0]))
            form = sum_of([tuple(t[:8] for t in form), tuple(t[8:] for t in form)])
            for by in (4, 2, 1):
                form = sum_of([form, tuple(pltpu.roll(t, by, 0) for t in form)])
            forms.append(form[0] + form[1])
        alpha = forms[0] / (forms[1] + tiny)
        alpha = jnp.concatenate([alpha, alpha], axis=0)
        solved = solved + alpha * a[0]
        high, rest = two_prod(alpha, b[0])
        a = tidy(sum_of([a, (-high, -(rest + alpha * b[1]))]))
    return solved * (float(4**LEVELS) * 0.25)


def out_copies(pairs, moved):
    return [pltpu.make_async_copy(src, dst, moved.at[at]) for at, (src, dst) in enumerate(pairs)]


LEVEL_ROWS = [plane_rows(level) for level in range(LEVELS)]


def down_kernel(
    planes_hbm, beyond_hbm, prev_hbm, next_hbm, s0_out, b0_out, s1_out, b1_out, s2_out, b2_out,
    s0, s1, s2, s3, b0, b1, b2, coef, planes, beyond, from_prev, from_next, arrived, moved,
):
    outer = pl.ds(0, OUTER)
    reads = out_copies(
        [(planes_hbm, planes), (beyond_hbm, beyond), (prev_hbm.at[outer, :], from_prev), (next_hbm.at[outer, :], from_next)],
        arrived,
    )
    writes = out_copies([(s0, s0_out), (b0, b0_out), (s1, s1_out), (b1, b1_out), (s2, s2_out), (b2, b2_out)], moved)
    for read in reads:
        read.start()
    fill_coefs(coef)
    zero_pads(((0, s0), (1, s1), (2, s2), (0, b0), (1, b1), (2, b2)))
    for read in reads:
        read.wait()
    for b in range(8):
        for p in range(9):
            at = base(0, b, p) + PAD
            edge = 4 * (9 * b + p)
            s0[at : at + 4, :] = from_prev[edge : edge + 4, :]
            s0[at + 28 : at + 32, :] = from_next[edge : edge + 4, :]
            if p < 8:
                s0[at + 4 : at + 28, :] = planes[24 * (8 * b + p) : 24 * (8 * b + p) + 24, :]
            else:
                s0[at + 4 : at + 28, :] = beyond[pl.ds(b, 24, stride=8), :]
    writes[0].start()
    down_level(0, s0, b0, s1, coef)
    writes[1].start()
    writes[2].start()
    down_level(1, s1, b1, s2, coef)
    writes[3].start()
    writes[4].start()
    down_level(2, s2, b2, s3, coef)
    writes[5].start()
    for write in writes:
        write.wait()


def run_down(planes, beyond, from_prev, from_next):
    held = [(64 * 24, 128), (ROWS, 128), (OUTER, 128), (OUTER, 128)]
    return pl.pallas_call(
        down_kernel,
        out_shape=tuple(pltpu.HBM((LEVEL_ROWS[level], 128), F32) for level in (0, 0, 1, 1, 2, 2)),
        in_specs=[hbm()] * 4,
        out_specs=[hbm()] * 6,
        scratch_shapes=level_scratch()
        + [pltpu.VMEM(dims, F32) for dims in held]
        + [pltpu.SemaphoreType.DMA((4,)), pltpu.SemaphoreType.DMA((6,))],
        name="down_all",
        cost_estimate=pl.CostEstimate(flops=40 * ROWS * COLS, bytes_accessed=30 * ROWS * COLS, transcendentals=0),
        **params(24),
    )(*[fixed(x) for x in (planes, beyond, from_prev, from_next)])


def fourth_kernel(
    grams, basis_hbm, s0_hbm, b0_hbm, s1_hbm, b1_hbm, s2_hbm, b2_hbm, out,
    s0, s1, s2, s3, b0, b1, b2, coef, held, basis, moved, *, cells,
):
    reads = out_copies(
        [(basis_hbm, basis), (s2_hbm, s2), (b2_hbm, b2), (s1_hbm, s1), (b1_hbm, b1), (s0_hbm, s0), (b0_hbm, b0)], moved
    )
    for read in reads:
        read.start()
    fill_coefs(coef)
    solved = coarse_coefs(grams, held, cells)
    for read in reads[:3]:
        read.wait()
    value = jnp.zeros((32, 256), F32)
    for k in range(ITERS):
        value = value + solved[k : k + 1, 0:1] * basis[32 * k : 32 * k + 32, :]
    lane = iota((SPAN, 128), 1)
    side = value[:, 128:]
    far = lax.shift_right_logical(lane, 3)
    s3[PAD : PAD + SPAN, :] = picked(value[:, :128], 16 * (lane & 7) + far)
    s3[TALL + PAD : TALL + PAD + SPAN, :] = picked(side, jnp.where(lane < 64, far, far + 112))
    up_level(2, s2, b2, s3, b2, coef)
    for read in reads[3:5]:
        read.wait()
    up_level(1, s1, b1, b2, b1, coef)
    for read in reads[5:]:
        read.wait()
    up_level(0, s0, b0, b1, b0, coef)
    for band in range(ROWS // BAND):
        tiles = []
        for p in range(8):
            at = base(0, 0, p) + PAD + 4 + BAND // 8 * band
            tiles.append(jnp.concatenate([b0[pl.ds(at + g, 8, stride=9 * TALL), :] for g in range(BAND // 8)], axis=0))
        for k, tile in enumerate(exchanged(tiles)):
            out[BAND * band : BAND * band + BAND, 128 * k : 128 * k + 128] = tile


def run_fourth(grams, basis, levels):
    cells = float((ROWS >> LEVELS) * (COLS >> LEVELS) * lax.axis_size("gz") * lax.axis_size("row"))
    held = [(32, 128), (32 * ITERS, 256)]
    return pl.pallas_call(
        functools.partial(fourth_kernel, cells=cells),
        out_shape=shaped(ROWS, COLS),
        in_specs=[vmem()] + [hbm()] * 7,
        out_specs=vmem(),
        scratch_shapes=level_scratch() + [pltpu.VMEM(dims, F32) for dims in held] + [pltpu.SemaphoreType.DMA((7,))],
        name="v_cycle",
        **params(24),
    )(grams, *[fixed(x) for x in (basis, *levels)])


STRIP = 32


def rates_kernel(
    swirl, swirl_up, swirl_down, vort, vort_up, vort_down, back, back_up, back_down, beyond,
    u_prev, p_prev, w_prev, u_next, p_next, w_next, vel_r, vel_z, swirl_coef, vort_coef, swirl_out, vort_out,
):
    strip = pl.program_id(0)
    lane = iota((STRIP, 128), 1)
    at = iota((STRIP, 128), 0)
    tiles = COLS // 128
    outside = beyond[...]

    above, below = strip > 0, strip < ROWS // STRIP - 1

    def slopes(ref, top, bottom, west, east, tile):
        lanes = slice(128 * tile, 128 * tile + 128)
        here = ref[:, lanes]
        left = west if tile == 0 else turn(ref[:, 128 * tile - 128 : 128 * tile], 1)
        right = east if tile == tiles - 1 else turn(ref[:, 128 * tile + 128 : 128 * tile + 256], -1)
        along_r = jnp.where(lane == 127, right, turn(here, -1)) - jnp.where(lane == 0, left, turn(here, 1))
        return here, along_r * 0.5, slope_z(here, top, bottom)

    def slope_z(here, top, bottom):
        ahead = jnp.where(at == STRIP - 1, bottom, pltpu.roll(here, STRIP - 1, 0))
        behind = jnp.where(at == 0, top, pltpu.roll(here, 1, 0))
        return (ahead - behind) * 0.5

    for tile in range(tiles):
        lanes = slice(128 * tile, 128 * tile + 128)
        own = slice(tile, tile + 1)
        u_top = jnp.where(above, swirl_up[7:8, lanes], u_prev[own, :])
        u_bottom = jnp.where(below, swirl_down[0:1, lanes], u_next[own, :])
        w_top = jnp.where(above, vort_up[7:8, lanes], w_prev[own, :])
        w_bottom = jnp.where(below, vort_down[0:1, lanes], w_next[own, :])
        p_top = jnp.where(above, 2.0 * back_up[7:8, lanes] * u_top, p_prev[own, :])
        p_bottom = jnp.where(below, 2.0 * back_down[0:1, lanes] * u_bottom, p_next[own, :])
        u, u_r, u_z = slopes(swirl, u_top, u_bottom, turn(outside, 32), turn(outside, 96), tile)
        w, w_r, w_z = slopes(vort, w_top, w_bottom, turn(outside, 1), turn(outside, -1), tile)
        p_z = slope_z(2.0 * back[:, lanes] * u, p_top, p_bottom)
        swirl_out[:, lanes] = swirl_coef[:, lanes] * u - vel_r[:, lanes] * u_r - vel_z[:, lanes] * u_z
        vort_out[:, lanes] = vort_coef[:, lanes] * w - vel_r[:, lanes] * w_r - vel_z[:, lanes] * w_z + p_z


def run_rates(swirl, vort, back, beyond, from_prev, from_next, vel_r, vel_z, swirl_coef, vort_coef):
    per = STRIP // 8
    block = pl.BlockSpec((STRIP, COLS), lambda t: (t, 0))
    up = pl.BlockSpec((8, COLS), lambda t: (jnp.maximum(per * t - 1, 0), 0))
    down = pl.BlockSpec((8, COLS), lambda t: (jnp.minimum(per * t + per, ROWS // 8 - 1), 0))
    singles = [pl.BlockSpec((8, 128), functools.partial(lambda at, t: (at, 0), OUTER // 8 + 4 + k)) for k in range(3)]
    return pl.pallas_call(
        rates_kernel,
        grid=(ROWS // STRIP,),
        out_shape=(shaped(ROWS, COLS), shaped(ROWS, COLS)),
        in_specs=[block, up, down] * 3 + [pl.BlockSpec((STRIP, 128), lambda t: (t, 0))] + singles * 2 + [block] * 4,
        out_specs=[block] * 2,
        name="rates",
        cost_estimate=pl.CostEstimate(flops=30 * ROWS * COLS, bytes_accessed=36 * ROWS * COLS, transcendentals=0),
        **params(16),
    )(*[fixed(x) for x in (swirl,) * 3 + (vort,) * 3 + (back,) * 3], fixed(beyond), *[fixed(x) for x in (from_prev,) * 3 + (from_next,) * 3 + (vel_r, vel_z, swirl_coef, vort_coef)])


def both_ways(axis, up, down):
    count = lax.axis_size(axis)
    ahead = [(i, i + 1) for i in range(count - 1)]
    back = [(i + 1, i) for i in range(count - 1)]
    return lax.ppermute(up, axis, ahead), lax.ppermute(down, axis, back)


def per_device(swirl, vorticity, base_swirl, vel_r, vel_z, swirl_coef, vort_coef):
    devices = lax.axis_size("gz") * lax.axis_size("row")
    part, to_east, to_west, planes, row_top, row_end = run_first(vorticity, swirl, base_swirl)
    from_west, from_east = both_ways("row", to_east, to_west)
    whole, beyond, to_next, to_prev = run_second(part, from_west, from_east, planes, row_top, row_end)
    from_prev, from_next = both_ways("gz", to_next, to_prev)
    basis, message = run_third(whole, from_prev, from_next, devices)
    grams = lax.all_to_all(message, AXES, 0, 0, tiled=True)
    levels = run_down(planes, beyond, from_prev, from_next)
    swirl_rate, vort_rate = run_rates(
        swirl, vorticity, base_swirl, beyond, from_prev, from_next, vel_r, vel_z, swirl_coef, vort_coef
    )
    potential = run_fourth(grams, basis, levels)
    return swirl_rate, vort_rate, potential


def solution(mesh):
    spec = P("gz", "row")
    return jax.shard_map(per_device, mesh=mesh, in_specs=(spec,) * 7, out_specs=(spec,) * 3, check_vma=False)
```

```python
import functools

import jax
import jax.numpy as jnp
from jax import lax
from jax.experimental import pallas as pl
from jax.experimental.pallas import tpu as pltpu
from jax.sharding import PartitionSpec as P

LEVELS = 3
ITERS = 10
BASIS = ITERS + 1
PAIRS = [(i, j) for i in range(BASIS) for j in range(i, BASIS)]
SLOTS = 72
AXES = ("gz", "row")

ROWS, COLS = 192, 1024
SPAN = 32
PAD = 8
TALL = SPAN + 2 * PAD
F32 = jnp.float32


def iota(shape, dim):
    return lax.broadcasted_iota(jnp.int32, shape, dim)


def place():
    return lax.axis_index("gz"), lax.axis_index("row"), lax.axis_size("gz"), lax.axis_size("row")


def is_odd(axis):
    return lax.axis_index(axis) % 2 == 1


def chosen(axis, first, second):
    at, count, odd = lax.axis_index(axis), lax.axis_size(axis), is_odd(axis)
    before = jnp.where(at > 0, jnp.where(odd, first, second), 0.0)
    return before, jnp.where(at < count - 1, jnp.where(odd, second, first), 0.0)


def lanes_inside(cols, width, row, row_count):
    low = jnp.where(row == 0, 0, -width)
    high = jnp.where(row == row_count - 1, width, 2 * width)
    return (cols >= low) & (cols < high)


def planes_of(level):
    return 8 >> level


def plane_rows(level):
    return planes_of(level) * (planes_of(level) + 1) * TALL


def base(level, b, p):
    return (b * (planes_of(level) + 1) + p) * TALL


COEF_AT = [0, 9, 14]
COEF_ROWS = 2 * 8 * 17


def main_q():
    lane = iota((8, 128), 1)
    return 16 * (lane & 7) + lax.shift_right_logical(lane, 3)


def side_cols():
    lane = iota((8, 128), 1)
    return jnp.where(lane < 64, lane + COLS, lane - 128)


def fill_coefs(coef):
    _, row, _, _ = place()
    for level in range(LEVELS):
        count = planes_of(level)
        spacing = float(2**level)
        for p in range(count + 1):
            if p < count:
                cols = count * main_q() + p
            else:
                cols = lax.shift_right_arithmetic(side_cols(), level)
            cols = cols + row * (COLS >> level)
            term = (1.5 * spacing) / (spacing * (cols.astype(F32) + 0.5) + 16.0)
            at = 16 * (COEF_AT[level] + p)
            coef[at : at + 8, :] = 1.0 + term
            coef[at + 8 : at + 16, :] = 1.0 - term


def coefs_of(coef, level, p):
    at = 16 * (COEF_AT[level] + p)
    return coef[at : at + 8, :], coef[at + 8 : at + 16, :]


def turn(x, by):
    return pltpu.roll(x, by % 128, 1)


def view_of(ref, level, b, p, k):
    return ref.at[pl.ds(pl.multiple_of(base(level, b, p) + 8 * k, 8), 24), :]


def here_of(ref, level, b, p, k):
    return view_of(ref, level, b, p, k)[8:16, :]


def put(ref, level, b, p, k, value):
    ref[pl.ds(pl.multiple_of(base(level, b, p) + PAD + 8 * k, 8), 8), :] = value


def vertical(ref, level, b, p, k):
    count = planes_of(level)
    above = view_of(ref, level, b - 1, p, k)[8:16, :] if b > 0 else view_of(ref, level, count - 1, p, k)[7:15, :]
    below = view_of(ref, level, b + 1, p, k)[8:16, :] if b < count - 1 else view_of(ref, level, 0, p, k)[9:17, :]
    return above + below


def beside_main(ref, coef, level, b, p, k):
    count = planes_of(level)
    step = 2**level
    lane = iota((8, 128), 1)
    east, west = coefs_of(coef, level, p)
    if p < count - 1:
        right = here_of(ref, level, b, p + 1, k)
    else:
        first, side = here_of(ref, level, b, 0, k), here_of(ref, level, b, count, k)
        right = jnp.where(lane < 120, turn(first, -8), turn(first, -9))
        right = jnp.where(lane == 127, turn(side, -1), right)
    if p > 0:
        left = here_of(ref, level, b, p - 1, k)
    else:
        last, side = here_of(ref, level, b, count - 1, k), here_of(ref, level, b, count, k)
        left = jnp.where(lane >= 8, turn(last, 8), turn(last, 9))
        left = jnp.where(lane == 0, turn(side, step), left)
    return (vertical(ref, level, b, p, k) + east * right) + west * left


def beside_side(ref, coef, level, b, k):
    count = planes_of(level)
    step = 2**level
    lane = iota((8, 128), 1)
    east, west = coefs_of(coef, level, count)
    side = here_of(ref, level, b, count, k)
    first, last = here_of(ref, level, b, 0, k), here_of(ref, level, b, count - 1, k)
    right = jnp.where(lane == 128 - step, turn(first, 128 - step), turn(side, -step))
    left = jnp.where(lane == 0, turn(last, 1), turn(side, step))
    return (vertical(ref, level, b, count, k) + east * right) + west * left


def odd_side(level, b):
    return ((lax.shift_right_logical(iota((8, 128), 1), level) + b) & 1) == 1


def inside_factors(k):
    gz, row, gz_count, row_count = place()
    low = jnp.where(gz == 0, 4, 0)
    high = jnp.where(gz == gz_count - 1, SPAN - 4, SPAN)
    at = iota((8, 128), 0) + 8 * k
    main = jnp.where((at >= low) & (at < high), 1.0, 0.0).astype(F32)
    lane = iota((8, 128), 1)
    first = jnp.where(row == row_count - 1, 64, 0)
    after = jnp.where(row == 0, 64, 128)
    return main, jnp.where((lane >= first) & (lane < after), main, 0.0)


def chunks(level, body):
    def write(stores):
        for ref, at, b, p, k, value in stores:
            put(ref, at, b, p, k, value)

    if level == 0:
        pl.loop(0, SPAN // 8)(lambda k: write(body(k)))
    else:
        write([store for k in range(SPAN // 8) for store in body(k)])


def down_level(level, source, black, coarse, coef):
    count = planes_of(level)
    step = 2**level
    keep = (lax.shift_right_logical(iota((8, 128), 1), level) & 1) == 0

    def sweep(k):
        main, side = inside_factors(k)
        main, side = 0.25 * main, 0.25 * side
        stores = []
        for b in range(count):
            beside = beside_side(source, coef, level, b, k)
            value = (here_of(source, level, b, count, k) + 0.25 * beside) * side
            stores.append((black, level, b, count, k, jnp.where(odd_side(level, b), value, 0.0)))
            for p in range(1 - b % 2, count, 2):
                beside = beside_main(source, coef, level, b, p, k)
                value = (here_of(source, level, b, p, k) + 0.25 * beside) * main
                stores.append((black, level, b, p, k, value))
        return stores

    def restrict(k):
        main, side = inside_factors(k)
        stores = []
        for b in range(0, count, 2):
            even = beside_side(black, coef, level, b, k)
            odd = turn(beside_side(black, coef, level, b + 1, k), -step)
            value = jnp.where(keep, (even + odd) * side, 0.0)
            stores.append((coarse, level + 1, b // 2, count // 2, k, value))
            for p in range(0, count, 2):
                value = beside_main(black, coef, level, b, p, k) + beside_main(black, coef, level, b + 1, p + 1, k)
                stores.append((coarse, level + 1, b // 2, p // 2, k, value * main))
        return stores

    chunks(level, sweep)
    chunks(level, restrict)


def up_level(level, source, black, error, field, coef):
    count = planes_of(level)
    step = 2**level
    moved = (lax.shift_right_logical(iota((8, 128), 1), level) & 1) == 1

    def correct(k):
        stores = []
        for b in range(count):
            value = here_of(error, level + 1, b // 2, count // 2, k)
            value = jnp.where(moved, turn(value, step), value)
            value = here_of(black, level, b, count, k) + value
            stores.append((field, level, b, count, k, jnp.where(odd_side(level, b), value, 0.0)))
            for p in range(1 - b % 2, count, 2):
                value = here_of(error, level + 1, b // 2, p // 2, k)
                stores.append((field, level, b, p, k, here_of(black, level, b, p, k) + value))
        return stores

    def sweep(colour, k):
        main, side = inside_factors(k)
        main, side = 0.25 * main, 0.25 * side
        stores = []
        for b in range(count):
            beside = beside_side(field, coef, level, b, k)
            value = (here_of(source, level, b, count, k) + beside) * side
            mine = odd_side(level, b + 1 - colour)
            stores.append((field, level, b, count, k, jnp.where(mine, value, here_of(field, level, b, count, k))))
            for p in range((b + colour) % 2, count, 2):
                beside = beside_main(field, coef, level, b, p, k)
                stores.append((field, level, b, p, k, (here_of(source, level, b, p, k) + beside) * main))
        return stores

    chunks(level, correct)
    chunks(level, functools.partial(sweep, 0))
    chunks(level, functools.partial(sweep, 1))


def zero_pads(refs):
    for level, ref in refs:
        for b in range(planes_of(level)):
            for p in range(planes_of(level) + 1):
                at = base(level, b, p)
                ref[at : at + PAD, :] = jnp.zeros((PAD, 128), F32)
                ref[at + PAD + SPAN : at + TALL, :] = jnp.zeros((PAD, 128), F32)


def picked(x, pick):
    return jnp.take_along_axis(x, pick, axis=1)


def exchanged(tiles):
    tiles = list(tiles)
    lane = iota(tiles[0].shape, 1)
    for bit in range(3):
        far = 2**bit
        low = (lax.shift_right_logical(lane, bit) & 1) == 0
        for k in range(8):
            if not k & far:
                a, c = tiles[k], tiles[k + far]
                tiles[k] = jnp.where(low, a, turn(c, far))
                tiles[k + far] = jnp.where(low, turn(a, -far), c)
    return tiles


def two_sum(a, b):
    total = a + b
    part = total - a
    return total, (a - (total - part)) + (b - part)


def halves(a):
    wide = a * 4097.0
    high = wide - (wide - a)
    return high, a - high


def two_prod(a, b):
    total = a * b
    ah, al = halves(a)
    bh, bl = halves(b)
    return total, ((ah * bh - total) + ah * bl + al * bh) + al * bl


def dd_add(a, b):
    total, rest = two_sum(a[0], b[0])
    rest = rest + (a[1] + b[1])
    high = total + rest
    return high, rest - (high - total)


def dd_mul(a, b):
    total, rest = two_prod(a[0], b[0])
    rest = rest + (a[0] * b[1] + a[1] * b[0])
    high = total + rest
    return high, rest - (high - total)


BAND = 32
FOLD = ROWS // 4


def pack_edges(vort, swirl_first, swirl_last):
    lane = iota((FOLD, 128), 1)
    eastward = westward = None
    for run in range(4):
        rows = slice(FOLD * run, FOLD * run + FOLD)
        last = jnp.where(lane == 96, turn(swirl_last[rows, :], 97), vort[rows, COLS - 128 :])
        first = jnp.where(lane == 31, turn(swirl_first[rows, :], 31), vort[rows, :128])
        last, first = turn(last, 32 * run + 32), turn(first, 32 * run)
        mine = lax.shift_right_logical(lane, 5) == run
        eastward = last if run == 0 else jnp.where(mine, last, eastward)
        westward = first if run == 0 else jnp.where(mine, first, westward)
    return eastward, westward


def unpack_edges(west, east, beyond):
    lane = iota((FOLD, 128), 1)
    for run in range(4):
        value = jnp.where(lane >= 96, turn(west, 96 - 32 * run), 0.0)
        beyond[FOLD * run : FOLD * run + FOLD, :] = jnp.where(lane < 32, turn(east, -32 * run), value)


def first_kernel(
    vort_hbm, swirl_hbm, back_hbm, part, swap_a, swap_b, planes, row_top, row_end,
    s0, s1, s2, s3, b0, b1, b2, coef, vort, arrived, swirl_first, swirl_last, ends, ends_arrived,
):
    copies, extras = [], []
    for band in range(ROWS // BAND):
        rows = pl.ds(BAND * band, BAND)
        copies.append(pltpu.make_async_copy(vort_hbm.at[rows, :], vort.at[rows, :], arrived.at[band]))
        copies[-1].start()
    pieces = [(swirl_hbm.at[:, pl.ds(0, 128)], swirl_first), (swirl_hbm.at[:, pl.ds(COLS - 128, 128)], swirl_last)]
    for number, array in enumerate((swirl_hbm, back_hbm)):
        for end, first in enumerate((0, ROWS - 8)):
            pieces.append((array.at[pl.ds(first, 8), :], ends.at[2 * number + end]))
    for number, (src, dst) in enumerate(pieces):
        extras.append(pltpu.make_async_copy(src, dst, ends_arrived.at[number]))
        extras[-1].start()
    fill_coefs(coef)
    zero_pads(((0, s0), (1, s1), (2, s2), (0, b0), (1, b1), (2, b2)))
    for b in range(8):
        for p in range(8):
            at = base(0, b, p) + PAD
            s0[at : at + 4, :] = jnp.zeros((4, 128), F32)
            s0[at + 28 : at + 32, :] = jnp.zeros((4, 128), F32)
        at = base(0, b, 8) + PAD
        s0[at : at + SPAN, :] = jnp.zeros((SPAN, 128), F32)
    for band in range(ROWS // BAND):
        copies[band].wait()
        rows = slice(BAND * band, BAND * band + BAND)
        tiles = [vort[rows, 128 * k : 128 * k + 128] for k in range(8)]
        for p, tile in enumerate(exchanged(tiles)):
            for part_of in range(BAND // 8):
                g = BAND // 8 * band + part_of
                s0[pl.ds(base(0, 0, p) + PAD + 4 + g, 8, stride=9 * TALL), :] = tile[8 * part_of : 8 * part_of + 8]
    for extra in extras:
        extra.wait()
    odd = is_odd("row")
    eastward, westward = pack_edges(vort, swirl_first, swirl_last)
    swap_a[:FOLD, :] = jnp.where(odd, westward, eastward)
    swap_b[:FOLD, :] = jnp.where(odd, eastward, westward)
    for end, (dest, row, edge) in enumerate(((row_top, 0, 0), (row_end, ROWS - 1, 7))):
        for tile in range(COLS // 128):
            lanes = slice(128 * tile, 128 * tile + 128)
            swirl = ends[end, edge : edge + 1, lanes]
            dest[tile : tile + 1, :] = swirl
            dest[8 + tile : 9 + tile, :] = 2.0 * ends[2 + end, edge : edge + 1, lanes] * swirl
            dest[16 + tile : 17 + tile, :] = vort[row : row + 1, lanes]
    for b in range(8):
        for p in range(8):
            at = base(0, b, p) + PAD + 4
            planes[24 * (8 * b + p) : 24 * (8 * b + p) + 24, :] = s0[at : at + 24, :]
    down_level(0, s0, b0, s1, coef)
    down_level(1, s1, b1, s2, coef)
    down_level(2, s2, b2, s3, coef)

    scale = 1.0 / float(4**LEVELS)
    main = s3[PAD : PAD + SPAN, :] * scale
    side = s3[TALL + PAD : TALL + PAD + SPAN, :] * scale
    lane = iota((SPAN, 128), 1)
    main = picked(main, 8 * (lane & 15) + lax.shift_right_logical(lane, 4))
    side = jnp.where((lane < 8) | (lane >= 120), picked(side, 8 * (lane & 15)), 0.0)
    part[:, :128] = main
    part[:, 128:] = side
    high = lane >= 64
    eastward, westward = jnp.where(high, main, side), jnp.where(high, side, main)
    swap_a[FOLD:, :] = jnp.where(odd, westward, eastward)
    swap_b[FOLD:, :] = jnp.where(odd, eastward, westward)


def level_scratch():
    sources = [pltpu.VMEM((plane_rows(level), 128), F32) for level in range(LEVELS + 1)]
    blacks = [pltpu.VMEM((plane_rows(level), 128), F32) for level in range(LEVELS)]
    return sources + blacks + [pltpu.VMEM((COEF_ROWS, 128), F32)]


def vmem():
    return pl.BlockSpec(memory_space=pltpu.VMEM)


def hbm():
    return pl.BlockSpec(memory_space=pltpu.HBM)


def fixed(x):
    return pltpu.with_memory_space_constraint(x, pltpu.HBM)


def shaped(*dims):
    return jax.ShapeDtypeStruct(dims, F32)


def params(mebibytes):
    return dict(compiler_params=pltpu.CompilerParams(vmem_limit_bytes=mebibytes * 2**20))


def run_first(vort, swirl, back):
    return pl.pallas_call(
        first_kernel,
        out_shape=(shaped(32, 256), shaped(FOLD + 32, 128), shaped(FOLD + 32, 128), shaped(64 * 24, 128))
        + (shaped(24, 128),) * 2,
        in_specs=[hbm()] * 3,
        out_specs=[vmem()] * 6,
        scratch_shapes=level_scratch()
        + [pltpu.VMEM((ROWS, COLS), F32), pltpu.SemaphoreType.DMA((ROWS // BAND,))]
        + [pltpu.VMEM((ROWS, 128), F32)] * 2
        + [pltpu.VMEM((4, 8, COLS), F32), pltpu.SemaphoreType.DMA((6,))],
        name="down_own",
        **params(24),
    )(fixed(vort), fixed(swirl), fixed(back))


OUTER = 288


def second_kernel(part, swap_a, swap_b, planes, row_top, row_end, whole, beyond, out_a, out_b, to_next, to_prev):
    high = iota((32, 128), 1) >= 64
    from_west, from_east = chosen("row", swap_a[...], swap_b[...])
    west, east = from_west[FOLD:], from_east[FOLD:]
    main = part[:, :128] + jnp.where(high, east, west)
    side = part[:, 128:] + jnp.where(high, west, east)
    whole[:, :128] = main
    whole[:, 128:] = side
    unpack_edges(from_west[:FOLD], from_east[:FOLD], beyond)
    for dest, g, rows, row in ((to_next, 20, slice(16, 32), row_end), (to_prev, 0, slice(0, 16), row_top)):
        for b in range(8):
            for p in range(8):
                at = 4 * (9 * b + p)
                dest[at : at + 4, :] = planes[24 * (8 * b + p) + g : 24 * (8 * b + p) + g + 4, :]
            at = 4 * (9 * b + 8)
            dest[at : at + 4, :] = beyond[pl.ds(8 * g + b, 4, stride=8), :]
        dest[OUTER : OUTER + 16, :] = main[rows]
        dest[OUTER + 16 : OUTER + 32, :] = side[rows]
        dest[OUTER + 32 :, :] = row[...]
    odd = is_odd("gz")
    out_a[...] = jnp.where(odd, to_prev[...], to_next[...])
    out_b[...] = jnp.where(odd, to_next[...], to_prev[...])


def run_second(part, swap_a, swap_b, planes, row_top, row_end):
    return pl.pallas_call(
        second_kernel,
        out_shape=(shaped(32, 256), shaped(ROWS, 128), shaped(OUTER + 56, 128), shaped(OUTER + 56, 128)),
        in_specs=[vmem()] * 6,
        out_specs=[vmem()] * 4,
        scratch_shapes=[pltpu.VMEM((OUTER + 56, 128), F32)] * 2,
        name="pack_gz",
        **params(24),
    )(part, swap_a, swap_b, planes, row_top, row_end)


def third_kernel(whole, swap_a, swap_b, basis_out, message, grid, gram_high, gram_low, basis, moved):
    gz, row, gz_count, row_count = place()
    grid[...] = jnp.zeros((48, 256), F32)
    grid[8:40, :] = whole[...]
    from_prev, from_next = chosen("gz", swap_a[OUTER : OUTER + 32, :], swap_b[OUTER : OUTER + 32, :])
    grid[0:16, :128] += from_prev[:16]
    grid[0:16, 128:] += from_prev[16:]
    grid[32:48, :128] += from_next[:16]
    grid[32:48, 128:] += from_next[16:]

    lane = iota((48, 256), 1)
    cols = jnp.where(lane < 192, lane, lane - 256)
    width = COLS >> LEVELS
    at = iota((48, 256), 0) - 12
    inside = lanes_inside(cols, width, row, row_count)
    low = jnp.where(gz == 0, 0, -64)
    high = jnp.where(gz == gz_count - 1, ROWS >> LEVELS, 128)
    inside = inside & (at >= low) & (at < high)
    spacing = float(2**LEVELS)
    radius = spacing * ((cols + row * width).astype(F32) + 0.5) + 16.0
    term = (1.5 * spacing) / radius
    east = jnp.where(inside, 0.25 + 0.25 * term, 0.0)
    west = jnp.where(inside, 0.25 - 0.25 * term, 0.0)
    quarter = jnp.where(inside, 0.25, 0.0)

    def average(x):
        total = quarter * (pltpu.roll(x, 1, 0) + pltpu.roll(x, 47, 0))
        total = total + east * pltpu.roll(x, 255, 1)
        return total + west * pltpu.roll(x, 1, 1)

    source = jnp.where(inside, grid[...], 0.0)
    older = source - average(source)
    newer = average(older)
    vectors = [source, older, newer]
    for _ in range(BASIS - 3):
        older, newer = newer, 2.0 * average(newer) - older
        vectors.append(newer)
    at = iota((32, 128), 0)
    own = (at >= 4) & (at < 28)
    parts = []
    for k in range(BASIS):
        if k < ITERS:
            basis[32 * k : 32 * k + 32, :] = vectors[k][8:40]
        masked = jnp.where(own, vectors[k][8:40, :128], 0.0)
        parts.append((masked,) + halves(masked))
    copy = pltpu.make_async_copy(basis, basis_out, moved)
    copy.start()
    for slot, (i, j) in enumerate(PAIRS):
        a, ah, al = parts[i]
        b, bh, bl = parts[j]
        product = a * b
        error = ((ah * bh - product) + ah * bl + al * bh) + al * bl
        top, first = two_sum(product[0:8], product[8:16])
        bottom, second = two_sum(product[16:24], product[24:32])
        total, third = two_sum(top, bottom)
        rest = (error[0:8] + error[8:16]) + (error[16:24] + error[24:32])
        gram_high[8 * slot : 8 * slot + 8, :] = total
        gram_low[8 * slot : 8 * slot + 8, :] = rest + (first + second + third)
    gram_high[8 * len(PAIRS) :, :] = jnp.zeros((8 * (SLOTS - len(PAIRS)), 128), F32)
    gram_low[8 * len(PAIRS) :, :] = jnp.zeros((8 * (SLOTS - len(PAIRS)), 128), F32)
    total = None
    for s in range(8):
        term = (gram_high[pl.ds(s, SLOTS, stride=8), :], gram_low[pl.ds(s, SLOTS, stride=8), :])
        total = term if total is None else dd_add(total, term)
    for by in (64, 32, 16, 8, 4, 2, 1):
        total = dd_add(total, tuple(pltpu.roll(t, by, 1) for t in total))
    lane = iota((SLOTS, 128), 1)
    i = lane // BASIS
    j = lane - BASIS * i
    i, j = jnp.minimum(i, j), jnp.maximum(i, j)
    keep = (iota((SLOTS, 128), 0) == BASIS * i - i * (i - 1) // 2 + j - i) & (lane < BASIS * BASIS)
    rows = [jnp.sum(jnp.where(keep, t, 0.0), axis=0, keepdims=True) for t in total]
    odd = (iota(message.shape, 0) & 1) == 1
    message[...] = jnp.where(odd, rows[1], rows[0])
    copy.wait()


def run_third(whole, swap_a, swap_b, devices):
    return pl.pallas_call(
        third_kernel,
        out_shape=(pltpu.HBM((32 * ITERS, 256), F32), shaped(2 * devices, 128)),
        in_specs=[vmem()] * 3,
        out_specs=[hbm(), vmem()],
        scratch_shapes=[pltpu.VMEM((48, 256), F32)]
        + [pltpu.VMEM((8 * SLOTS, 128), F32)] * 2
        + [pltpu.VMEM((32 * ITERS, 256), F32), pltpu.SemaphoreType.DMA],
        name="basis_gram",
        **params(24),
    )(whole, swap_a, swap_b)


def sum_of(terms):
    terms = list(terms)
    while len(terms) > 1:
        added = []
        for left, right in zip(terms[::2], terms[1::2]):
            total, rest = two_sum(left[0], right[0])
            added.append((total, rest + (left[1] + right[1])))
        terms = added + terms[len(terms) // 2 * 2 :]
    return terms[0]


def tidy(pair):
    high = pair[0] + pair[1]
    return high, pair[1] - (high - pair[0])


def coarse_coefs(grams, held, cells):
    devices = grams.shape[0] // 2
    gram = (grams[pl.ds(0, devices, stride=2), :], grams[pl.ds(1, devices, stride=2), :])
    while gram[0].shape[0] > 8:
        half = gram[0].shape[0] // 2
        gram = dd_add(tuple(g[:half] for g in gram), tuple(g[half:] for g in gram))
    for by in (4, 2, 1):
        gram = dd_add(gram, tuple(pltpu.roll(g, by, 0) for g in gram))

    lane = iota((16, 128), 0)
    gram = tuple(jnp.concatenate([g, g], axis=0) for g in gram)
    columns = []
    for j in range(BASIS):
        pick = jnp.minimum(lane * BASIS + j, BASIS * BASIS - 1)
        high, low = (jnp.where(lane < BASIS, picked(g, pick), 0.0) for g in gram)
        columns.append((high, low) + halves(high))

    index = iota((16, 128), 0)
    below = jnp.where(index == 0, 0.0, jnp.where(index == 1, -1.0, jnp.where(index == 2, 1.0, 0.5)))
    below = jnp.where(index < BASIS, below, 0.0)
    above = jnp.where((index > 0) & (index < BASIS - 1), 0.5, 0.0)
    same = jnp.where((index > 0) & (index < BASIS), 1.0, 0.0)

    def image(a):
        moved = sum_of([tuple(below * pltpu.roll(t, 1, 0) for t in a), tuple(above * pltpu.roll(t, 15, 0) for t in a)])
        return tidy(sum_of([tuple(same * t for t in a), tuple(-t for t in moved)]))

    a = (jnp.where(index == 0, 1.0, 0.0), jnp.zeros((16, 128), F32))
    solved = jnp.zeros((16, 128), F32)
    tiny = float(4 ** (2 * LEVELS)) / 16.0 * cells * 1e-12
    for _ in range(ITERS):
        b = image(a)
        held[0:16, :] = b[0]
        held[16:32, :] = b[1]
        terms = []
        for j, (high, low, upper, lower) in enumerate(columns):
            at_j = jnp.broadcast_to(held[j : j + 1, :], (16, 128))
            rest_j = jnp.broadcast_to(held[16 + j : 17 + j, :], (16, 128))
            jh, jl = halves(at_j)
            product = high * at_j
            rest = ((upper * jh - product) + upper * jl + lower * jh) + lower * jl
            terms.append((product, rest + (high * rest_j + low * at_j)))
        image_gram = tidy(sum_of(terms))
        forms = []
        for left in (a, b):
            high, rest = two_prod(left[0], image_gram[0])
            form = (high, rest + (left[0] * image_gram[1] + left[1] * image_gram[0]))
            form = sum_of([tuple(t[:8] for t in form), tuple(t[8:] for t in form)])
            for by in (4, 2, 1):
                form = sum_of([form, tuple(pltpu.roll(t, by, 0) for t in form)])
            forms.append(form[0] + form[1])
        alpha = forms[0] / (forms[1] + tiny)
        alpha = jnp.concatenate([alpha, alpha], axis=0)
        solved = solved + alpha * a[0]
        high, rest = two_prod(alpha, b[0])
        a = tidy(sum_of([a, (-high, -(rest + alpha * b[1]))]))
    return solved * (float(4**LEVELS) * 0.25)


def out_copies(pairs, moved):
    return [pltpu.make_async_copy(src, dst, moved.at[at]) for at, (src, dst) in enumerate(pairs)]


LEVEL_ROWS = [plane_rows(level) for level in range(LEVELS)]


def down_kernel(
    planes_hbm, beyond_hbm, a_hbm, b_hbm, s0_out, b0_out, s1_out, b1_out, s2_out, b2_out,
    s0, s1, s2, s3, b0, b1, b2, coef, planes, beyond, swap_a, swap_b, arrived, moved,
):
    outer = pl.ds(0, OUTER)
    reads = out_copies(
        [(planes_hbm, planes), (beyond_hbm, beyond), (a_hbm.at[outer, :], swap_a), (b_hbm.at[outer, :], swap_b)],
        arrived,
    )
    writes = out_copies([(s0, s0_out), (b0, b0_out), (s1, s1_out), (b1, b1_out), (s2, s2_out), (b2, b2_out)], moved)
    for read in reads:
        read.start()
    fill_coefs(coef)
    zero_pads(((0, s0), (1, s1), (2, s2), (0, b0), (1, b1), (2, b2)))
    for read in reads:
        read.wait()
    for b in range(8):
        for p in range(9):
            at = base(0, b, p) + PAD
            edge = 4 * (9 * b + p)
            from_prev, from_next = chosen("gz", swap_a[edge : edge + 4, :], swap_b[edge : edge + 4, :])
            s0[at : at + 4, :] = from_prev
            s0[at + 28 : at + 32, :] = from_next
            if p < 8:
                s0[at + 4 : at + 28, :] = planes[24 * (8 * b + p) : 24 * (8 * b + p) + 24, :]
            else:
                s0[at + 4 : at + 28, :] = beyond[pl.ds(b, 24, stride=8), :]
    writes[0].start()
    down_level(0, s0, b0, s1, coef)
    writes[1].start()
    writes[2].start()
    down_level(1, s1, b1, s2, coef)
    writes[3].start()
    writes[4].start()
    down_level(2, s2, b2, s3, coef)
    writes[5].start()
    for write in writes:
        write.wait()


def run_down(planes, beyond, swap_a, swap_b):
    held = [(64 * 24, 128), (ROWS, 128), (OUTER, 128), (OUTER, 128)]
    return pl.pallas_call(
        down_kernel,
        out_shape=tuple(pltpu.HBM((LEVEL_ROWS[level], 128), F32) for level in (0, 0, 1, 1, 2, 2)),
        in_specs=[hbm()] * 4,
        out_specs=[hbm()] * 6,
        scratch_shapes=level_scratch()
        + [pltpu.VMEM(dims, F32) for dims in held]
        + [pltpu.SemaphoreType.DMA((4,)), pltpu.SemaphoreType.DMA((6,))],
        name="down_all",
        cost_estimate=pl.CostEstimate(flops=40 * ROWS * COLS, bytes_accessed=30 * ROWS * COLS, transcendentals=0),
        **params(24),
    )(*[fixed(x) for x in (planes, beyond, swap_a, swap_b)])


def fourth_kernel(
    grams, basis_hbm, s0_hbm, b0_hbm, s1_hbm, b1_hbm, s2_hbm, b2_hbm, out,
    s0, s1, s2, s3, b0, b1, b2, coef, held, basis, moved, *, cells,
):
    reads = out_copies(
        [(basis_hbm, basis), (s2_hbm, s2), (b2_hbm, b2), (s1_hbm, s1), (b1_hbm, b1), (s0_hbm, s0), (b0_hbm, b0)], moved
    )
    for read in reads:
        read.start()
    fill_coefs(coef)
    solved = coarse_coefs(grams, held, cells)
    for read in reads[:3]:
        read.wait()
    value = jnp.zeros((32, 256), F32)
    for k in range(ITERS):
        value = value + solved[k : k + 1, 0:1] * basis[32 * k : 32 * k + 32, :]
    lane = iota((SPAN, 128), 1)
    side = value[:, 128:]
    far = lax.shift_right_logical(lane, 3)
    s3[PAD : PAD + SPAN, :] = picked(value[:, :128], 16 * (lane & 7) + far)
    s3[TALL + PAD : TALL + PAD + SPAN, :] = picked(side, jnp.where(lane < 64, far, far + 112))
    up_level(2, s2, b2, s3, b2, coef)
    for read in reads[3:5]:
        read.wait()
    up_level(1, s1, b1, b2, b1, coef)
    for read in reads[5:]:
        read.wait()
    up_level(0, s0, b0, b1, b0, coef)
    for band in range(ROWS // BAND):
        tiles = []
        for p in range(8):
            at = base(0, 0, p) + PAD + 4 + BAND // 8 * band
            tiles.append(jnp.concatenate([b0[pl.ds(at + g, 8, stride=9 * TALL), :] for g in range(BAND // 8)], axis=0))
        for k, tile in enumerate(exchanged(tiles)):
            out[BAND * band : BAND * band + BAND, 128 * k : 128 * k + 128] = tile


def run_fourth(grams, basis, levels):
    cells = float((ROWS >> LEVELS) * (COLS >> LEVELS) * lax.axis_size("gz") * lax.axis_size("row"))
    held = [(32, 128), (32 * ITERS, 256)]
    return pl.pallas_call(
        functools.partial(fourth_kernel, cells=cells),
        out_shape=shaped(ROWS, COLS),
        in_specs=[vmem()] + [hbm()] * 7,
        out_specs=vmem(),
        scratch_shapes=level_scratch() + [pltpu.VMEM(dims, F32) for dims in held] + [pltpu.SemaphoreType.DMA((7,))],
        name="v_cycle",
        **params(24),
    )(grams, *[fixed(x) for x in (basis, *levels)])


STRIP = 32


def rates_kernel(
    swirl, swirl_up, swirl_down, vort, vort_up, vort_down, back, back_up, back_down, beyond,
    u_a, p_a, w_a, u_b, p_b, w_b, vel_r, vel_z, swirl_coef, vort_coef, swirl_out, vort_out,
):
    strip = pl.program_id(0)
    lane = iota((STRIP, 128), 1)
    at = iota((STRIP, 128), 0)
    tiles = COLS // 128
    outside = beyond[...]

    u_prev, u_next = chosen("gz", u_a[...], u_b[...])
    p_prev, p_next = chosen("gz", p_a[...], p_b[...])
    w_prev, w_next = chosen("gz", w_a[...], w_b[...])
    above, below = strip > 0, strip < ROWS // STRIP - 1

    def slopes(ref, top, bottom, west, east, tile):
        lanes = slice(128 * tile, 128 * tile + 128)
        here = ref[:, lanes]
        left = west if tile == 0 else turn(ref[:, 128 * tile - 128 : 128 * tile], 1)
        right = east if tile == tiles - 1 else turn(ref[:, 128 * tile + 128 : 128 * tile + 256], -1)
        along_r = jnp.where(lane == 127, right, turn(here, -1)) - jnp.where(lane == 0, left, turn(here, 1))
        return here, along_r * 0.5, slope_z(here, top, bottom)

    def slope_z(here, top, bottom):
        ahead = jnp.where(at == STRIP - 1, bottom, pltpu.roll(here, STRIP - 1, 0))
        behind = jnp.where(at == 0, top, pltpu.roll(here, 1, 0))
        return (ahead - behind) * 0.5

    for tile in range(tiles):
        lanes = slice(128 * tile, 128 * tile + 128)
        own = slice(tile, tile + 1)
        u_top = jnp.where(above, swirl_up[7:8, lanes], u_prev[own])
        u_bottom = jnp.where(below, swirl_down[0:1, lanes], u_next[own])
        w_top = jnp.where(above, vort_up[7:8, lanes], w_prev[own])
        w_bottom = jnp.where(below, vort_down[0:1, lanes], w_next[own])
        p_top = jnp.where(above, 2.0 * back_up[7:8, lanes] * u_top, p_prev[own])
        p_bottom = jnp.where(below, 2.0 * back_down[0:1, lanes] * u_bottom, p_next[own])
        u, u_r, u_z = slopes(swirl, u_top, u_bottom, turn(outside, 32), turn(outside, 96), tile)
        w, w_r, w_z = slopes(vort, w_top, w_bottom, turn(outside, 1), turn(outside, -1), tile)
        p_z = slope_z(2.0 * back[:, lanes] * u, p_top, p_bottom)
        swirl_out[:, lanes] = swirl_coef[:, lanes] * u - vel_r[:, lanes] * u_r - vel_z[:, lanes] * u_z
        vort_out[:, lanes] = vort_coef[:, lanes] * w - vel_r[:, lanes] * w_r - vel_z[:, lanes] * w_z + p_z


def run_rates(swirl, vort, back, beyond, swap_a, swap_b, vel_r, vel_z, swirl_coef, vort_coef):
    per = STRIP // 8
    block = pl.BlockSpec((STRIP, COLS), lambda t: (t, 0))
    up = pl.BlockSpec((8, COLS), lambda t: (jnp.maximum(per * t - 1, 0), 0))
    down = pl.BlockSpec((8, COLS), lambda t: (jnp.minimum(per * t + per, ROWS // 8 - 1), 0))
    singles = [pl.BlockSpec((8, 128), functools.partial(lambda at, t: (at, 0), OUTER // 8 + 4 + k)) for k in range(3)]
    return pl.pallas_call(
        rates_kernel,
        grid=(ROWS // STRIP,),
        out_shape=(shaped(ROWS, COLS), shaped(ROWS, COLS)),
        in_specs=[block, up, down] * 3 + [pl.BlockSpec((STRIP, 128), lambda t: (t, 0))] + singles * 2 + [block] * 4,
        out_specs=[block] * 2,
        name="rates",
        cost_estimate=pl.CostEstimate(flops=30 * ROWS * COLS, bytes_accessed=36 * ROWS * COLS, transcendentals=0),
        **params(16),
    )(*[fixed(x) for x in (swirl,) * 3 + (vort,) * 3 + (back,) * 3], fixed(beyond), *[fixed(x) for x in (swap_a,) * 3 + (swap_b,) * 3 + (vel_r, vel_z, swirl_coef, vort_coef)])


def swapped(axis, first, second):
    count = lax.axis_size(axis)
    pairs = [(i, i ^ 1) for i in range(count)]
    others = [(i, (i + 1) % count if i % 2 else (i - 1) % count) for i in range(count)]
    return lax.ppermute(first, axis, pairs), lax.ppermute(second, axis, others)


def per_device(swirl, vorticity, base_swirl, vel_r, vel_z, swirl_coef, vort_coef):
    devices = lax.axis_size("gz") * lax.axis_size("row")
    part, *swaps, planes, row_top, row_end = run_first(vorticity, swirl, base_swirl)
    swaps = swapped("row", *swaps)
    whole, beyond, *swaps = run_second(part, *swaps, planes, row_top, row_end)
    swaps = swapped("gz", *swaps)
    basis, message = run_third(whole, *swaps, devices)
    grams = lax.all_to_all(message, AXES, 0, 0, tiled=True)
    levels = run_down(planes, beyond, *swaps)
    swirl_rate, vort_rate = run_rates(swirl, vorticity, base_swirl, beyond, *swaps, vel_r, vel_z, swirl_coef, vort_coef)
    potential = run_fourth(grams, basis, levels)
    return swirl_rate, vort_rate, potential


def solution(mesh):
    spec = P("gz", "row")
    return jax.shard_map(per_device, mesh=mesh, in_specs=(spec,) * 7, out_specs=(spec,) * 3, check_vma=False)
```

```python
import functools

import jax
import jax.numpy as jnp
from jax import lax
from jax.experimental import pallas as pl
from jax.experimental.pallas import tpu as pltpu
from jax.sharding import PartitionSpec as P

LEVELS = 3
ITERS = 10
BASIS = ITERS + 1
PAIRS = [(i, j) for i in range(BASIS) for j in range(i, BASIS)]
SLOTS = 72
AXES = ("gz", "row")

ROWS, COLS = 192, 1024
SPAN = 32
PAD = 8
TALL = SPAN + 2 * PAD
F32 = jnp.float32


def iota(shape, dim):
    return lax.broadcasted_iota(jnp.int32, shape, dim)


def place():
    return lax.axis_index("gz"), lax.axis_index("row"), lax.axis_size("gz"), lax.axis_size("row")


def is_odd(axis):
    return lax.axis_index(axis) % 2 == 1


def chosen(axis, first, second):
    at, count, odd = lax.axis_index(axis), lax.axis_size(axis), is_odd(axis)
    before = jnp.where(at > 0, jnp.where(odd, first, second), 0.0)
    return before, jnp.where(at < count - 1, jnp.where(odd, second, first), 0.0)


def lanes_inside(cols, width, row, row_count):
    low = jnp.where(row == 0, 0, -width)
    high = jnp.where(row == row_count - 1, width, 2 * width)
    return (cols >= low) & (cols < high)


def planes_of(level):
    return 8 >> level


def plane_rows(level):
    return planes_of(level) * (planes_of(level) + 1) * TALL


def base(level, b, p):
    return (b * (planes_of(level) + 1) + p) * TALL


COEF_AT = [0, 9, 14]
COEF_ROWS = 2 * 8 * 17


def main_q():
    lane = iota((8, 128), 1)
    return 16 * (lane & 7) + lax.shift_right_logical(lane, 3)


def side_cols():
    lane = iota((8, 128), 1)
    return jnp.where(lane < 64, lane + COLS, lane - 128)


def fill_coefs(coef):
    _, row, _, _ = place()
    for level in range(LEVELS):
        count = planes_of(level)
        spacing = float(2**level)
        for p in range(count + 1):
            if p < count:
                cols = count * main_q() + p
            else:
                cols = lax.shift_right_arithmetic(side_cols(), level)
            cols = cols + row * (COLS >> level)
            term = (1.5 * spacing) / (spacing * (cols.astype(F32) + 0.5) + 16.0)
            at = 16 * (COEF_AT[level] + p)
            coef[at : at + 8, :] = 1.0 + term
            coef[at + 8 : at + 16, :] = 1.0 - term


def coefs_of(coef, level, p):
    at = 16 * (COEF_AT[level] + p)
    return coef[at : at + 8, :], coef[at + 8 : at + 16, :]


def turn(x, by):
    return pltpu.roll(x, by % 128, 1)


def view_of(ref, level, b, p, k):
    return ref.at[pl.ds(pl.multiple_of(base(level, b, p) + 8 * k, 8), 24), :]


def here_of(ref, level, b, p, k):
    return view_of(ref, level, b, p, k)[8:16, :]


def put(ref, level, b, p, k, value):
    ref[pl.ds(pl.multiple_of(base(level, b, p) + PAD + 8 * k, 8), 8), :] = value


def vertical(ref, level, b, p, k):
    count = planes_of(level)
    above = view_of(ref, level, b - 1, p, k)[8:16, :] if b > 0 else view_of(ref, level, count - 1, p, k)[7:15, :]
    below = view_of(ref, level, b + 1, p, k)[8:16, :] if b < count - 1 else view_of(ref, level, 0, p, k)[9:17, :]
    return above + below


def beside_main(ref, coef, level, b, p, k):
    count = planes_of(level)
    step = 2**level
    lane = iota((8, 128), 1)
    east, west = coefs_of(coef, level, p)
    if p < count - 1:
        right = here_of(ref, level, b, p + 1, k)
    else:
        first, side = here_of(ref, level, b, 0, k), here_of(ref, level, b, count, k)
        right = jnp.where(lane < 120, turn(first, -8), turn(first, -9))
        right = jnp.where(lane == 127, turn(side, -1), right)
    if p > 0:
        left = here_of(ref, level, b, p - 1, k)
    else:
        last, side = here_of(ref, level, b, count - 1, k), here_of(ref, level, b, count, k)
        left = jnp.where(lane >= 8, turn(last, 8), turn(last, 9))
        left = jnp.where(lane == 0, turn(side, step), left)
    return (vertical(ref, level, b, p, k) + east * right) + west * left


def beside_side(ref, coef, level, b, k):
    count = planes_of(level)
    step = 2**level
    lane = iota((8, 128), 1)
    east, west = coefs_of(coef, level, count)
    side = here_of(ref, level, b, count, k)
    first, last = here_of(ref, level, b, 0, k), here_of(ref, level, b, count - 1, k)
    right = jnp.where(lane == 128 - step, turn(first, 128 - step), turn(side, -step))
    left = jnp.where(lane == 0, turn(last, 1), turn(side, step))
    return (vertical(ref, level, b, count, k) + east * right) + west * left


def odd_side(level, b):
    return ((lax.shift_right_logical(iota((8, 128), 1), level) + b) & 1) == 1


def inside_factors(k):
    gz, row, gz_count, row_count = place()
    low = jnp.where(gz == 0, 4, 0)
    high = jnp.where(gz == gz_count - 1, SPAN - 4, SPAN)
    at = iota((8, 128), 0) + 8 * k
    main = jnp.where((at >= low) & (at < high), 1.0, 0.0).astype(F32)
    lane = iota((8, 128), 1)
    first = jnp.where(row == row_count - 1, 64, 0)
    after = jnp.where(row == 0, 64, 128)
    return main, jnp.where((lane >= first) & (lane < after), main, 0.0)


def chunks(level, body):
    def write(stores):
        for ref, at, b, p, k, value in stores:
            put(ref, at, b, p, k, value)

    if level == 0:
        pl.loop(0, SPAN // 8)(lambda k: write(body(k)))
    else:
        write([store for k in range(SPAN // 8) for store in body(k)])


def down_level(level, source, black, coarse, coef):
    count = planes_of(level)
    step = 2**level
    keep = (lax.shift_right_logical(iota((8, 128), 1), level) & 1) == 0

    def sweep(k):
        main, side = inside_factors(k)
        main, side = 0.25 * main, 0.25 * side
        stores = []
        for b in range(count):
            beside = beside_side(source, coef, level, b, k)
            value = (here_of(source, level, b, count, k) + 0.25 * beside) * side
            stores.append((black, level, b, count, k, jnp.where(odd_side(level, b), value, 0.0)))
            for p in range(1 - b % 2, count, 2):
                beside = beside_main(source, coef, level, b, p, k)
                value = (here_of(source, level, b, p, k) + 0.25 * beside) * main
                stores.append((black, level, b, p, k, value))
        return stores

    def restrict(k):
        main, side = inside_factors(k)
        stores = []
        for b in range(0, count, 2):
            even = beside_side(black, coef, level, b, k)
            odd = turn(beside_side(black, coef, level, b + 1, k), -step)
            value = jnp.where(keep, (even + odd) * side, 0.0)
            stores.append((coarse, level + 1, b // 2, count // 2, k, value))
            for p in range(0, count, 2):
                value = beside_main(black, coef, level, b, p, k) + beside_main(black, coef, level, b + 1, p + 1, k)
                stores.append((coarse, level + 1, b // 2, p // 2, k, value * main))
        return stores

    chunks(level, sweep)
    chunks(level, restrict)


PACKED_SOURCE = 72 * SPAN
PACKED_BLACK = 40 * SPAN


def packed_source(b, p):
    return (9 * b + p) * SPAN


def packed_black(b, p):
    return (5 * b + (p // 2 if p < 8 else 4)) * SPAN


def up_level(level, source, black, error, field, coef):
    count = planes_of(level)
    step = 2**level
    moved = (lax.shift_right_logical(iota((8, 128), 1), level) & 1) == 1

    def source_at(b, p, k):
        if level > 0:
            return here_of(source, level, b, p, k)
        return source[pl.ds(pl.multiple_of(packed_source(b, p) + 8 * k, 8), 8), :]

    def black_at(b, p, k):
        if level > 0:
            return here_of(black, level, b, p, k)
        return black[pl.ds(pl.multiple_of(packed_black(b, p) + 8 * k, 8), 8), :]

    def correct(k):
        stores = []
        for b in range(count):
            value = here_of(error, level + 1, b // 2, count // 2, k)
            value = jnp.where(moved, turn(value, step), value)
            value = black_at(b, count, k) + value
            stores.append((field, level, b, count, k, jnp.where(odd_side(level, b), value, 0.0)))
            for p in range(1 - b % 2, count, 2):
                value = here_of(error, level + 1, b // 2, p // 2, k)
                stores.append((field, level, b, p, k, black_at(b, p, k) + value))
        return stores

    def sweep(colour, k):
        main, side = inside_factors(k)
        main, side = 0.25 * main, 0.25 * side
        stores = []
        for b in range(count):
            beside = beside_side(field, coef, level, b, k)
            value = (source_at(b, count, k) + beside) * side
            mine = odd_side(level, b + 1 - colour)
            stores.append((field, level, b, count, k, jnp.where(mine, value, here_of(field, level, b, count, k))))
            for p in range((b + colour) % 2, count, 2):
                beside = beside_main(field, coef, level, b, p, k)
                stores.append((field, level, b, p, k, (source_at(b, p, k) + beside) * main))
        return stores

    chunks(level, correct)
    chunks(level, functools.partial(sweep, 0))
    chunks(level, functools.partial(sweep, 1))


def zero_pads(refs):
    for level, ref in refs:
        for b in range(planes_of(level)):
            for p in range(planes_of(level) + 1):
                at = base(level, b, p)
                ref[at : at + PAD, :] = jnp.zeros((PAD, 128), F32)
                ref[at + PAD + SPAN : at + TALL, :] = jnp.zeros((PAD, 128), F32)


def picked(x, pick):
    return jnp.take_along_axis(x, pick, axis=1)


def exchanged(tiles):
    tiles = list(tiles)
    lane = iota(tiles[0].shape, 1)
    for bit in range(3):
        far = 2**bit
        low = (lax.shift_right_logical(lane, bit) & 1) == 0
        for k in range(8):
            if not k & far:
                a, c = tiles[k], tiles[k + far]
                tiles[k] = jnp.where(low, a, turn(c, far))
                tiles[k + far] = jnp.where(low, turn(a, -far), c)
    return tiles


def two_sum(a, b):
    total = a + b
    part = total - a
    return total, (a - (total - part)) + (b - part)


def halves(a):
    wide = a * 4097.0
    high = wide - (wide - a)
    return high, a - high


def two_prod(a, b):
    total = a * b
    ah, al = halves(a)
    bh, bl = halves(b)
    return total, ((ah * bh - total) + ah * bl + al * bh) + al * bl


def dd_add(a, b):
    total, rest = two_sum(a[0], b[0])
    rest = rest + (a[1] + b[1])
    high = total + rest
    return high, rest - (high - total)


def dd_mul(a, b):
    total, rest = two_prod(a[0], b[0])
    rest = rest + (a[0] * b[1] + a[1] * b[0])
    high = total + rest
    return high, rest - (high - total)


BAND = 32
FOLD = ROWS // 4


def pack_edges(vort, swirl_first, swirl_last):
    lane = iota((FOLD, 128), 1)
    eastward = westward = None
    for run in range(4):
        rows = slice(FOLD * run, FOLD * run + FOLD)
        last = jnp.where(lane == 96, turn(swirl_last[rows, :], 97), vort[rows, COLS - 128 :])
        first = jnp.where(lane == 31, turn(swirl_first[rows, :], 31), vort[rows, :128])
        last, first = turn(last, 32 * run + 32), turn(first, 32 * run)
        mine = lax.shift_right_logical(lane, 5) == run
        eastward = last if run == 0 else jnp.where(mine, last, eastward)
        westward = first if run == 0 else jnp.where(mine, first, westward)
    return eastward, westward


def unpack_edges(west, east, beyond):
    lane = iota((FOLD, 128), 1)
    for run in range(4):
        value = jnp.where(lane >= 96, turn(west, 96 - 32 * run), 0.0)
        beyond[FOLD * run : FOLD * run + FOLD, :] = jnp.where(lane < 32, turn(east, -32 * run), value)


def first_kernel(
    vort_hbm, swirl_hbm, back_hbm, part, swap_a, swap_b, planes, row_top, row_end,
    s0, s1, s2, s3, b0, b1, b2, coef, vort, arrived, swirl_first, swirl_last, ends, ends_arrived,
):
    copies, extras = [], []
    for band in range(ROWS // BAND):
        rows = pl.ds(BAND * band, BAND)
        copies.append(pltpu.make_async_copy(vort_hbm.at[rows, :], vort.at[rows, :], arrived.at[band]))
        copies[-1].start()
    pieces = [(swirl_hbm.at[:, pl.ds(0, 128)], swirl_first), (swirl_hbm.at[:, pl.ds(COLS - 128, 128)], swirl_last)]
    for number, array in enumerate((swirl_hbm, back_hbm)):
        for end, first in enumerate((0, ROWS - 8)):
            pieces.append((array.at[pl.ds(first, 8), :], ends.at[2 * number + end]))
    for number, (src, dst) in enumerate(pieces):
        extras.append(pltpu.make_async_copy(src, dst, ends_arrived.at[number]))
        extras[-1].start()
    fill_coefs(coef)
    zero_pads(((0, s0), (1, s1), (2, s2), (0, b0), (1, b1), (2, b2)))
    for b in range(8):
        for p in range(8):
            at = base(0, b, p) + PAD
            s0[at : at + 4, :] = jnp.zeros((4, 128), F32)
            s0[at + 28 : at + 32, :] = jnp.zeros((4, 128), F32)
        at = base(0, b, 8) + PAD
        s0[at : at + SPAN, :] = jnp.zeros((SPAN, 128), F32)
    for band in range(ROWS // BAND):
        copies[band].wait()
        rows = slice(BAND * band, BAND * band + BAND)
        tiles = [vort[rows, 128 * k : 128 * k + 128] for k in range(8)]
        for p, tile in enumerate(exchanged(tiles)):
            for part_of in range(BAND // 8):
                g = BAND // 8 * band + part_of
                s0[pl.ds(base(0, 0, p) + PAD + 4 + g, 8, stride=9 * TALL), :] = tile[8 * part_of : 8 * part_of + 8]
    for extra in extras:
        extra.wait()
    odd = is_odd("row")
    eastward, westward = pack_edges(vort, swirl_first, swirl_last)
    swap_a[:FOLD, :] = jnp.where(odd, westward, eastward)
    swap_b[:FOLD, :] = jnp.where(odd, eastward, westward)
    for end, (dest, row, edge) in enumerate(((row_top, 0, 0), (row_end, ROWS - 1, 7))):
        for tile in range(COLS // 128):
            lanes = slice(128 * tile, 128 * tile + 128)
            swirl = ends[end, edge : edge + 1, lanes]
            dest[tile : tile + 1, :] = swirl
            dest[8 + tile : 9 + tile, :] = 2.0 * ends[2 + end, edge : edge + 1, lanes] * swirl
            dest[16 + tile : 17 + tile, :] = vort[row : row + 1, lanes]
    for b in range(8):
        for p in range(8):
            at = base(0, b, p) + PAD + 4
            planes[24 * (8 * b + p) : 24 * (8 * b + p) + 24, :] = s0[at : at + 24, :]
    down_level(0, s0, b0, s1, coef)
    down_level(1, s1, b1, s2, coef)
    down_level(2, s2, b2, s3, coef)

    scale = 1.0 / float(4**LEVELS)
    main = s3[PAD : PAD + SPAN, :] * scale
    side = s3[TALL + PAD : TALL + PAD + SPAN, :] * scale
    lane = iota((SPAN, 128), 1)
    main = picked(main, 8 * (lane & 15) + lax.shift_right_logical(lane, 4))
    side = jnp.where((lane < 8) | (lane >= 120), picked(side, 8 * (lane & 15)), 0.0)
    part[:, :128] = main
    part[:, 128:] = side
    high = lane >= 64
    eastward, westward = jnp.where(high, main, side), jnp.where(high, side, main)
    swap_a[FOLD:, :] = jnp.where(odd, westward, eastward)
    swap_b[FOLD:, :] = jnp.where(odd, eastward, westward)


def level_scratch():
    sources = [pltpu.VMEM((plane_rows(level), 128), F32) for level in range(LEVELS + 1)]
    blacks = [pltpu.VMEM((plane_rows(level), 128), F32) for level in range(LEVELS)]
    return sources + blacks + [pltpu.VMEM((COEF_ROWS, 128), F32)]


def vmem():
    return pl.BlockSpec(memory_space=pltpu.VMEM)


def out_copies(pairs, moved):
    return [pltpu.make_async_copy(src, dst, moved.at[at]) for at, (src, dst) in enumerate(pairs)]


def hbm():
    return pl.BlockSpec(memory_space=pltpu.HBM)


def fixed(x):
    return pltpu.with_memory_space_constraint(x, pltpu.HBM)


def shaped(*dims):
    return jax.ShapeDtypeStruct(dims, F32)


def params(mebibytes):
    return dict(compiler_params=pltpu.CompilerParams(vmem_limit_bytes=mebibytes * 2**20))


def run_first(vort, swirl, back):
    return pl.pallas_call(
        first_kernel,
        out_shape=(shaped(32, 256), shaped(FOLD + 32, 128), shaped(FOLD + 32, 128), shaped(64 * 24, 128))
        + (shaped(24, 128),) * 2,
        in_specs=[hbm()] * 3,
        out_specs=[vmem()] * 6,
        scratch_shapes=level_scratch()
        + [pltpu.VMEM((ROWS, COLS), F32), pltpu.SemaphoreType.DMA((ROWS // BAND,))]
        + [pltpu.VMEM((ROWS, 128), F32)] * 2
        + [pltpu.VMEM((4, 8, COLS), F32), pltpu.SemaphoreType.DMA((6,))],
        name="down_own",
        **params(24),
    )(fixed(vort), fixed(swirl), fixed(back))


OUTER = 288


def second_kernel(part, swap_a, swap_b, planes, row_top, row_end, whole, out_a, out_b, to_next, to_prev, beyond):
    high = iota((32, 128), 1) >= 64
    from_west, from_east = chosen("row", swap_a[...], swap_b[...])
    west, east = from_west[FOLD:], from_east[FOLD:]
    main = part[:, :128] + jnp.where(high, east, west)
    side = part[:, 128:] + jnp.where(high, west, east)
    whole[:, :128] = main
    whole[:, 128:] = side
    unpack_edges(from_west[:FOLD], from_east[:FOLD], beyond)
    for dest, g, rows, row in ((to_next, 20, slice(16, 32), row_end), (to_prev, 0, slice(0, 16), row_top)):
        for b in range(8):
            for p in range(8):
                at = 4 * (9 * b + p)
                dest[at : at + 4, :] = planes[24 * (8 * b + p) + g : 24 * (8 * b + p) + g + 4, :]
            at = 4 * (9 * b + 8)
            dest[at : at + 4, :] = beyond[pl.ds(8 * g + b, 4, stride=8), :]
        dest[OUTER : OUTER + 16, :] = main[rows]
        dest[OUTER + 16 : OUTER + 32, :] = side[rows]
        dest[OUTER + 32 :, :] = row[...]
    odd = is_odd("gz")
    out_a[...] = jnp.where(odd, to_prev[...], to_next[...])
    out_b[...] = jnp.where(odd, to_next[...], to_prev[...])


def run_second(part, swap_a, swap_b, planes, row_top, row_end):
    return pl.pallas_call(
        second_kernel,
        out_shape=(shaped(32, 256), shaped(OUTER + 56, 128), shaped(OUTER + 56, 128)),
        in_specs=[vmem()] * 6,
        out_specs=[vmem()] * 3,
        scratch_shapes=[pltpu.VMEM((OUTER + 56, 128), F32)] * 2 + [pltpu.VMEM((ROWS, 128), F32)],
        name="pack_gz",
        **params(24),
    )(part, swap_a, swap_b, planes, row_top, row_end)


def third_kernel(
    whole, swap_a, swap_b, basis_out, message, grid, gram_high, gram_low, basis, moved
):
    copies = out_copies([(basis, basis_out)], moved)
    gz, row, gz_count, row_count = place()
    grid[...] = jnp.zeros((48, 256), F32)
    grid[8:40, :] = whole[...]
    from_prev, from_next = chosen("gz", swap_a[OUTER : OUTER + 32, :], swap_b[OUTER : OUTER + 32, :])
    grid[0:16, :128] += from_prev[:16]
    grid[0:16, 128:] += from_prev[16:]
    grid[32:48, :128] += from_next[:16]
    grid[32:48, 128:] += from_next[16:]

    lane = iota((48, 256), 1)
    cols = jnp.where(lane < 192, lane, lane - 256)
    width = COLS >> LEVELS
    at = iota((48, 256), 0) - 12
    inside = lanes_inside(cols, width, row, row_count)
    low = jnp.where(gz == 0, 0, -64)
    high = jnp.where(gz == gz_count - 1, ROWS >> LEVELS, 128)
    inside = inside & (at >= low) & (at < high)
    spacing = float(2**LEVELS)
    radius = spacing * ((cols + row * width).astype(F32) + 0.5) + 16.0
    term = (1.5 * spacing) / radius
    east = jnp.where(inside, 0.25 + 0.25 * term, 0.0)
    west = jnp.where(inside, 0.25 - 0.25 * term, 0.0)
    quarter = jnp.where(inside, 0.25, 0.0)

    def average(x):
        total = quarter * (pltpu.roll(x, 1, 0) + pltpu.roll(x, 47, 0))
        total = total + east * pltpu.roll(x, 255, 1)
        return total + west * pltpu.roll(x, 1, 1)

    source = jnp.where(inside, grid[...], 0.0)
    older = source - average(source)
    newer = average(older)
    vectors = [source, older, newer]
    for _ in range(BASIS - 3):
        older, newer = newer, 2.0 * average(newer) - older
        vectors.append(newer)
    at = iota((32, 128), 0)
    own = (at >= 4) & (at < 28)
    parts = []
    for k in range(BASIS):
        if k < ITERS:
            basis[32 * k : 32 * k + 32, :] = vectors[k][8:40]
        masked = jnp.where(own, vectors[k][8:40, :128], 0.0)
        parts.append((masked,) + halves(masked))
    copies[0].start()
    for slot, (i, j) in enumerate(PAIRS):
        a, ah, al = parts[i]
        b, bh, bl = parts[j]
        product = a * b
        error = ((ah * bh - product) + ah * bl + al * bh) + al * bl
        top, first = two_sum(product[0:8], product[8:16])
        bottom, second = two_sum(product[16:24], product[24:32])
        total, third = two_sum(top, bottom)
        rest = (error[0:8] + error[8:16]) + (error[16:24] + error[24:32])
        gram_high[8 * slot : 8 * slot + 8, :] = total
        gram_low[8 * slot : 8 * slot + 8, :] = rest + (first + second + third)
    gram_high[8 * len(PAIRS) :, :] = jnp.zeros((8 * (SLOTS - len(PAIRS)), 128), F32)
    gram_low[8 * len(PAIRS) :, :] = jnp.zeros((8 * (SLOTS - len(PAIRS)), 128), F32)
    total = None
    for s in range(8):
        term = (gram_high[pl.ds(s, SLOTS, stride=8), :], gram_low[pl.ds(s, SLOTS, stride=8), :])
        total = term if total is None else dd_add(total, term)
    for by in (64, 32, 16, 8, 4, 2, 1):
        total = dd_add(total, tuple(pltpu.roll(t, by, 1) for t in total))
    lane = iota((SLOTS, 128), 1)
    i = lane // BASIS
    j = lane - BASIS * i
    i, j = jnp.minimum(i, j), jnp.maximum(i, j)
    keep = (iota((SLOTS, 128), 0) == BASIS * i - i * (i - 1) // 2 + j - i) & (lane < BASIS * BASIS)
    rows = [jnp.sum(jnp.where(keep, t, 0.0), axis=0, keepdims=True) for t in total]
    odd = (iota(message.shape, 0) & 1) == 1
    message[...] = jnp.where(odd, rows[1], rows[0])
    for copy in copies:
        copy.wait()


def run_third(whole, swaps, devices):
    return pl.pallas_call(
        third_kernel,
        out_shape=(pltpu.HBM((32 * ITERS, 256), F32), shaped(2 * devices, 128)),
        in_specs=[vmem()] * 3,
        out_specs=[hbm(), vmem()],
        scratch_shapes=[pltpu.VMEM((48, 256), F32)]
        + [pltpu.VMEM((8 * SLOTS, 128), F32)] * 2
        + [pltpu.VMEM((32 * ITERS, 256), F32), pltpu.SemaphoreType.DMA((1,))],
        name="basis_gram",
        **params(24),
    )(whole, *swaps)


def sum_of(terms):
    terms = list(terms)
    while len(terms) > 1:
        added = []
        for left, right in zip(terms[::2], terms[1::2]):
            total, rest = two_sum(left[0], right[0])
            added.append((total, rest + (left[1] + right[1])))
        terms = added + terms[len(terms) // 2 * 2 :]
    return terms[0]


def tidy(pair):
    high = pair[0] + pair[1]
    return high, pair[1] - (high - pair[0])


def coarse_coefs(grams, held, cells):
    devices = grams.shape[0] // 2
    gram = (grams[pl.ds(0, devices, stride=2), :], grams[pl.ds(1, devices, stride=2), :])
    while gram[0].shape[0] > 8:
        half = gram[0].shape[0] // 2
        gram = dd_add(tuple(g[:half] for g in gram), tuple(g[half:] for g in gram))
    for by in (4, 2, 1):
        gram = dd_add(gram, tuple(pltpu.roll(g, by, 0) for g in gram))

    lane = iota((16, 128), 0)
    gram = tuple(jnp.concatenate([g, g], axis=0) for g in gram)
    columns = []
    for j in range(BASIS):
        pick = jnp.minimum(lane * BASIS + j, BASIS * BASIS - 1)
        high, low = (jnp.where(lane < BASIS, picked(g, pick), 0.0) for g in gram)
        columns.append((high, low) + halves(high))

    index = iota((16, 128), 0)
    below = jnp.where(index == 0, 0.0, jnp.where(index == 1, -1.0, jnp.where(index == 2, 1.0, 0.5)))
    below = jnp.where(index < BASIS, below, 0.0)
    above = jnp.where((index > 0) & (index < BASIS - 1), 0.5, 0.0)
    same = jnp.where((index > 0) & (index < BASIS), 1.0, 0.0)

    def image(a):
        moved = sum_of([tuple(below * pltpu.roll(t, 1, 0) for t in a), tuple(above * pltpu.roll(t, 15, 0) for t in a)])
        return tidy(sum_of([tuple(same * t for t in a), tuple(-t for t in moved)]))

    a = (jnp.where(index == 0, 1.0, 0.0), jnp.zeros((16, 128), F32))
    solved = jnp.zeros((16, 128), F32)
    tiny = float(4 ** (2 * LEVELS)) / 16.0 * cells * 1e-12
    for _ in range(ITERS):
        b = image(a)
        held[0:16, :] = b[0]
        held[16:32, :] = b[1]
        terms = []
        for j, (high, low, upper, lower) in enumerate(columns):
            at_j = jnp.broadcast_to(held[j : j + 1, :], (16, 128))
            rest_j = jnp.broadcast_to(held[16 + j : 17 + j, :], (16, 128))
            jh, jl = halves(at_j)
            product = high * at_j
            rest = ((upper * jh - product) + upper * jl + lower * jh) + lower * jl
            terms.append((product, rest + (high * rest_j + low * at_j)))
        image_gram = tidy(sum_of(terms))
        forms = []
        for left in (a, b):
            high, rest = two_prod(left[0], image_gram[0])
            form = (high, rest + (left[0] * image_gram[1] + left[1] * image_gram[0]))
            form = sum_of([tuple(t[:8] for t in form), tuple(t[8:] for t in form)])
            for by in (4, 2, 1):
                form = sum_of([form, tuple(pltpu.roll(t, by, 0) for t in form)])
            forms.append(form[0] + form[1])
        alpha = forms[0] / (forms[1] + tiny)
        alpha = jnp.concatenate([alpha, alpha], axis=0)
        solved = solved + alpha * a[0]
        high, rest = two_prod(alpha, b[0])
        a = tidy(sum_of([a, (-high, -(rest + alpha * b[1]))]))
    return solved * (float(4**LEVELS) * 0.25)


LEVEL_ROWS = [PACKED_SOURCE, PACKED_BLACK] + [plane_rows(level) for level in (1, 1, 2, 2)]


def down_kernel(
    planes_hbm, row_a_hbm, row_b_hbm, a_hbm, b_hbm, s0_out, b0_out, s1_out, b1_out, s2_out, b2_out,
    s0, s1, s2, s3, b0, b1, b2, coef, planes, row_a, row_b, swap_a, swap_b, beyond, s0_packed, b0_packed, arrived, moved,
):
    outer = pl.ds(0, OUTER)
    reads = out_copies(
        [(row_a_hbm, row_a), (row_b_hbm, row_b), (planes_hbm, planes), (a_hbm.at[outer, :], swap_a), (b_hbm.at[outer, :], swap_b)],
        arrived,
    )
    writes = out_copies([(s0_packed, s0_out), (b0_packed, b0_out), (s1, s1_out), (b1, b1_out), (s2, s2_out), (b2, b2_out)], moved)
    for read in reads:
        read.start()
    fill_coefs(coef)
    zero_pads(((0, s0), (1, s1), (2, s2), (0, b0), (1, b1), (2, b2)))
    for read in reads:
        read.wait()
    unpack_edges(*chosen("row", row_a[:FOLD, :], row_b[:FOLD, :]), beyond)
    for b in range(8):
        for p in range(9):
            at = base(0, b, p) + PAD
            edge = 4 * (9 * b + p)
            from_prev, from_next = chosen("gz", swap_a[edge : edge + 4, :], swap_b[edge : edge + 4, :])
            s0[at : at + 4, :] = from_prev
            s0[at + 28 : at + 32, :] = from_next
            if p < 8:
                s0[at + 4 : at + 28, :] = planes[24 * (8 * b + p) : 24 * (8 * b + p) + 24, :]
            else:
                s0[at + 4 : at + 28, :] = beyond[pl.ds(b, 24, stride=8), :]
            s0_packed[packed_source(b, p) : packed_source(b, p) + SPAN, :] = s0[at : at + SPAN, :]
    writes[0].start()
    down_level(0, s0, b0, s1, coef)
    for b in range(8):
        for p in list(range(1 - b % 2, 8, 2)) + [8]:
            at = base(0, b, p) + PAD
            b0_packed[packed_black(b, p) : packed_black(b, p) + SPAN, :] = b0[at : at + SPAN, :]
    writes[1].start()
    writes[2].start()
    down_level(1, s1, b1, s2, coef)
    writes[3].start()
    writes[4].start()
    down_level(2, s2, b2, s3, coef)
    writes[5].start()
    for write in writes:
        write.wait()


def run_down(planes, rows, swaps):
    held = [(64 * 24, 128), (FOLD + 32, 128), (FOLD + 32, 128), (OUTER, 128), (OUTER, 128), (ROWS, 128), (PACKED_SOURCE, 128), (PACKED_BLACK, 128)]
    return pl.pallas_call(
        down_kernel,
        out_shape=tuple(pltpu.HBM((rows, 128), F32) for rows in LEVEL_ROWS),
        in_specs=[hbm()] * 5,
        out_specs=[hbm()] * 6,
        scratch_shapes=level_scratch()
        + [pltpu.VMEM(dims, F32) for dims in held]
        + [pltpu.SemaphoreType.DMA((5,)), pltpu.SemaphoreType.DMA((6,))],
        name="down_all",
        cost_estimate=pl.CostEstimate(flops=40 * ROWS * COLS, bytes_accessed=30 * ROWS * COLS, transcendentals=0),
        **params(24),
    )(*[fixed(x) for x in (planes, *rows, *swaps)])


def fourth_kernel(
    grams, basis_hbm, s0_hbm, b0_hbm, s1_hbm, b1_hbm, s2_hbm, b2_hbm, out,
    s0, s1, s2, s3, b0, b1, b2, v0, coef, held, basis, moved, final, left, *, cells,
):
    reads = out_copies(
        [(basis_hbm, basis), (s2_hbm, s2), (b2_hbm, b2), (s1_hbm, s1), (b1_hbm, b1), (s0_hbm, s0), (b0_hbm, b0)], moved
    )
    for read in reads:
        read.start()
    fill_coefs(coef)
    zero_pads(((0, v0),))
    solved = coarse_coefs(grams, held, cells)
    for read in reads[:3]:
        read.wait()
    value = jnp.zeros((32, 256), F32)
    for k in range(ITERS):
        value = value + solved[k : k + 1, 0:1] * basis[32 * k : 32 * k + 32, :]
    lane = iota((SPAN, 128), 1)
    side = value[:, 128:]
    far = lax.shift_right_logical(lane, 3)
    s3[PAD : PAD + SPAN, :] = picked(value[:, :128], 16 * (lane & 7) + far)
    s3[TALL + PAD : TALL + PAD + SPAN, :] = picked(side, jnp.where(lane < 64, far, far + 112))
    up_level(2, s2, b2, s3, b2, coef)
    for read in reads[3:5]:
        read.wait()
    up_level(1, s1, b1, b2, b1, coef)
    for read in reads[5:]:
        read.wait()
    up_level(0, s0, b0, b1, v0, coef)
    writes = []
    for band in range(ROWS // BAND):
        tiles = []
        for p in range(8):
            at = base(0, 0, p) + PAD + 4 + BAND // 8 * band
            tiles.append(jnp.concatenate([v0[pl.ds(at + g, 8, stride=9 * TALL), :] for g in range(BAND // 8)], axis=0))
        for k, tile in enumerate(exchanged(tiles)):
            final[BAND * band : BAND * band + BAND, 128 * k : 128 * k + 128] = tile
        rows = pl.ds(BAND * band, BAND)
        writes.append(pltpu.make_async_copy(final.at[rows, :], out.at[rows, :], left.at[band]))
        writes[-1].start()
    for write in writes:
        write.wait()


def run_fourth(grams, basis, levels):
    cells = float((ROWS >> LEVELS) * (COLS >> LEVELS) * lax.axis_size("gz") * lax.axis_size("row"))
    tall = [PACKED_SOURCE, *(plane_rows(level) for level in (1, 2, 3)), PACKED_BLACK]
    tall += [plane_rows(level) for level in (1, 2, 0)] + [COEF_ROWS]
    fields = [pltpu.VMEM((rows, 128), F32) for rows in tall]
    held = [(32, 128), (32 * ITERS, 256)]
    return pl.pallas_call(
        functools.partial(fourth_kernel, cells=cells),
        out_shape=shaped(ROWS, COLS),
        in_specs=[vmem()] + [hbm()] * 7,
        out_specs=hbm(),
        scratch_shapes=fields + [pltpu.VMEM(dims, F32) for dims in held]
        + [pltpu.SemaphoreType.DMA((7,)), pltpu.VMEM((ROWS, COLS), F32), pltpu.SemaphoreType.DMA((ROWS // BAND,))],
        name="v_cycle",
        **params(24),
    )(grams, *[fixed(x) for x in (basis, *levels)])


STRIP = FOLD


def rates_kernel(
    swirl, swirl_up, swirl_down, vort, vort_up, vort_down, back, back_up, back_down, row_a, row_b,
    u_a, p_a, w_a, u_b, p_b, w_b, vel_r, vel_z, swirl_coef, vort_coef, swirl_out, vort_out,
):
    strip = pl.program_id(0)
    lane = iota((STRIP, 128), 1)
    at = iota((STRIP, 128), 0)
    tiles = COLS // 128
    west, east = chosen("row", row_a[...], row_b[...])
    west, east = pltpu.roll(west, (224 - 32 * strip) % 128, 1), pltpu.roll(east, (128 - 32 * strip) % 128, 1)

    u_prev, u_next = chosen("gz", u_a[...], u_b[...])
    p_prev, p_next = chosen("gz", p_a[...], p_b[...])
    w_prev, w_next = chosen("gz", w_a[...], w_b[...])
    above, below = strip > 0, strip < ROWS // STRIP - 1

    def slopes(ref, top, bottom, west, east, tile):
        lanes = slice(128 * tile, 128 * tile + 128)
        here = ref[:, lanes]
        left = west if tile == 0 else turn(ref[:, 128 * tile - 128 : 128 * tile], 1)
        right = east if tile == tiles - 1 else turn(ref[:, 128 * tile + 128 : 128 * tile + 256], -1)
        along_r = jnp.where(lane == 127, right, turn(here, -1)) - jnp.where(lane == 0, left, turn(here, 1))
        return here, along_r * 0.5, slope_z(here, top, bottom)

    def slope_z(here, top, bottom):
        ahead = jnp.where(at == STRIP - 1, bottom, pltpu.roll(here, STRIP - 1, 0))
        behind = jnp.where(at == 0, top, pltpu.roll(here, 1, 0))
        return (ahead - behind) * 0.5

    for tile in range(tiles):
        lanes = slice(128 * tile, 128 * tile + 128)
        own = slice(tile, tile + 1)
        u_top = jnp.where(above, swirl_up[7:8, lanes], u_prev[own])
        u_bottom = jnp.where(below, swirl_down[0:1, lanes], u_next[own])
        w_top = jnp.where(above, vort_up[7:8, lanes], w_prev[own])
        w_bottom = jnp.where(below, vort_down[0:1, lanes], w_next[own])
        p_top = jnp.where(above, 2.0 * back_up[7:8, lanes] * u_top, p_prev[own])
        p_bottom = jnp.where(below, 2.0 * back_down[0:1, lanes] * u_bottom, p_next[own])
        u, u_r, u_z = slopes(swirl, u_top, u_bottom, turn(west, 32), turn(east, 96), tile)
        w, w_r, w_z = slopes(vort, w_top, w_bottom, turn(west, 1), turn(east, -1), tile)
        p_z = slope_z(2.0 * back[:, lanes] * u, p_top, p_bottom)
        swirl_out[:, lanes] = swirl_coef[:, lanes] * u - vel_r[:, lanes] * u_r - vel_z[:, lanes] * u_z
        vort_out[:, lanes] = vort_coef[:, lanes] * w - vel_r[:, lanes] * w_r - vel_z[:, lanes] * w_z + p_z


def run_rates(swirl, vort, back, rows, swap_a, swap_b, vel_r, vel_z, swirl_coef, vort_coef):
    per = STRIP // 8
    block = pl.BlockSpec((STRIP, COLS), lambda t: (t, 0))
    up = pl.BlockSpec((8, COLS), lambda t: (jnp.maximum(per * t - 1, 0), 0))
    down = pl.BlockSpec((8, COLS), lambda t: (jnp.minimum(per * t + per, ROWS // 8 - 1), 0))
    singles = [pl.BlockSpec((8, 128), functools.partial(lambda at, t: (at, 0), OUTER // 8 + 4 + k)) for k in range(3)]
    return pl.pallas_call(
        rates_kernel,
        grid=(ROWS // STRIP,),
        out_shape=(shaped(ROWS, COLS), shaped(ROWS, COLS)),
        in_specs=[block, up, down] * 3 + [pl.BlockSpec((FOLD, 128), lambda t: (0, 0))] * 2 + singles * 2 + [block] * 4,
        out_specs=[block] * 2,
        name="rates",
        cost_estimate=pl.CostEstimate(flops=30 * ROWS * COLS, bytes_accessed=36 * ROWS * COLS, transcendentals=0),
        **params(16),
    )(*[fixed(x) for x in (swirl,) * 3 + (vort,) * 3 + (back,) * 3], *[fixed(x) for x in (*rows,) + (swap_a,) * 3 + (swap_b,) * 3 + (vel_r, vel_z, swirl_coef, vort_coef)])


def swapped(axis, first, second):
    count = lax.axis_size(axis)
    pairs = [(i, i ^ 1) for i in range(count)]
    others = [(i, (i + 1) % count if i % 2 else (i - 1) % count) for i in range(count)]
    return lax.ppermute(first, axis, pairs), lax.ppermute(second, axis, others)


def per_device(swirl, vorticity, base_swirl, vel_r, vel_z, swirl_coef, vort_coef):
    devices = lax.axis_size("gz") * lax.axis_size("row")
    part, *swaps, planes, row_top, row_end = run_first(vorticity, swirl, base_swirl)
    rows = swapped("row", *swaps)
    whole, *swaps = run_second(part, *rows, planes, row_top, row_end)
    swaps = swapped("gz", *swaps)
    basis, message = run_third(whole, swaps, devices)
    grams = lax.all_to_all(message, AXES, 0, 0, tiled=True)
    levels = run_down(planes, rows, swaps)
    swirl_rate, vort_rate = run_rates(swirl, vorticity, base_swirl, rows, *swaps, vel_r, vel_z, swirl_coef, vort_coef)
    potential = run_fourth(grams, basis, levels)
    return swirl_rate, vort_rate, potential


def solution(mesh):
    spec = P("gz", "row")
    return jax.shard_map(per_device, mesh=mesh, in_specs=(spec,) * 7, out_specs=(spec,) * 3, check_vma=False)
```

```python
import functools

import jax
import jax.numpy as jnp
from jax import lax
from jax.experimental import pallas as pl
from jax.experimental.pallas import tpu as pltpu
from jax.sharding import PartitionSpec as P

LEVELS = 3
ITERS = 10
BASIS = ITERS + 1
PAIRS = [(i, j) for i in range(BASIS) for j in range(i, BASIS)]
SLOTS = 72
AXES = ("gz", "row")

ROWS, COLS = 192, 1024
SPAN = 32
PAD = 8
TALL = SPAN + 2 * PAD
F32 = jnp.float32


def iota(shape, dim):
    return lax.broadcasted_iota(jnp.int32, shape, dim)


def place():
    return lax.axis_index("gz"), lax.axis_index("row"), lax.axis_size("gz"), lax.axis_size("row")


def is_odd(axis):
    return lax.axis_index(axis) % 2 == 1


def chosen(axis, first, second):
    at, count, odd = lax.axis_index(axis), lax.axis_size(axis), is_odd(axis)
    before = jnp.where(at > 0, jnp.where(odd, first, second), 0.0)
    return before, jnp.where(at < count - 1, jnp.where(odd, second, first), 0.0)


def lanes_inside(cols, width, row, row_count):
    low = jnp.where(row == 0, 0, -width)
    high = jnp.where(row == row_count - 1, width, 2 * width)
    return (cols >= low) & (cols < high)


def planes_of(level):
    return 8 >> level


def plane_rows(level):
    return planes_of(level) * (planes_of(level) + 1) * TALL


def base(level, b, p):
    return (b * (planes_of(level) + 1) + p) * TALL


COEF_AT = [0, 9, 14]
COEF_ROWS = 2 * 8 * 17


def main_q():
    lane = iota((8, 128), 1)
    return 16 * (lane & 7) + lax.shift_right_logical(lane, 3)


def side_cols():
    lane = iota((8, 128), 1)
    return jnp.where(lane < 64, lane + COLS, lane - 128)


def fill_coefs(coef):
    _, row, _, _ = place()
    for level in range(LEVELS):
        count = planes_of(level)
        spacing = float(2**level)
        for p in range(count + 1):
            if p < count:
                cols = count * main_q() + p
            else:
                cols = lax.shift_right_arithmetic(side_cols(), level)
            cols = cols + row * (COLS >> level)
            term = (1.5 * spacing) / (spacing * (cols.astype(F32) + 0.5) + 16.0)
            at = 16 * (COEF_AT[level] + p)
            coef[at : at + 8, :] = 1.0 + term
            coef[at + 8 : at + 16, :] = 1.0 - term


def coefs_of(coef, level, p):
    at = 16 * (COEF_AT[level] + p)
    return coef[at : at + 8, :], coef[at + 8 : at + 16, :]


def turn(x, by):
    return pltpu.roll(x, by % 128, 1)


def view_of(ref, level, b, p, k):
    return ref.at[pl.ds(pl.multiple_of(base(level, b, p) + 8 * k, 8), 24), :]


def here_of(ref, level, b, p, k):
    return view_of(ref, level, b, p, k)[8:16, :]


def put(ref, level, b, p, k, value):
    ref[pl.ds(pl.multiple_of(base(level, b, p) + PAD + 8 * k, 8), 8), :] = value


def vertical(ref, level, b, p, k):
    count = planes_of(level)
    above = view_of(ref, level, b - 1, p, k)[8:16, :] if b > 0 else view_of(ref, level, count - 1, p, k)[7:15, :]
    below = view_of(ref, level, b + 1, p, k)[8:16, :] if b < count - 1 else view_of(ref, level, 0, p, k)[9:17, :]
    return above + below


def beside_main(ref, coef, level, b, p, k):
    count = planes_of(level)
    step = 2**level
    lane = iota((8, 128), 1)
    east, west = coefs_of(coef, level, p)
    if p < count - 1:
        right = here_of(ref, level, b, p + 1, k)
    else:
        first, side = here_of(ref, level, b, 0, k), here_of(ref, level, b, count, k)
        right = jnp.where(lane < 120, turn(first, -8), turn(first, -9))
        right = jnp.where(lane == 127, turn(side, -1), right)
    if p > 0:
        left = here_of(ref, level, b, p - 1, k)
    else:
        last, side = here_of(ref, level, b, count - 1, k), here_of(ref, level, b, count, k)
        left = jnp.where(lane >= 8, turn(last, 8), turn(last, 9))
        left = jnp.where(lane == 0, turn(side, step), left)
    return (vertical(ref, level, b, p, k) + east * right) + west * left


def beside_side(ref, coef, level, b, k):
    count = planes_of(level)
    step = 2**level
    lane = iota((8, 128), 1)
    east, west = coefs_of(coef, level, count)
    side = here_of(ref, level, b, count, k)
    first, last = here_of(ref, level, b, 0, k), here_of(ref, level, b, count - 1, k)
    right = jnp.where(lane == 128 - step, turn(first, 128 - step), turn(side, -step))
    left = jnp.where(lane == 0, turn(last, 1), turn(side, step))
    return (vertical(ref, level, b, count, k) + east * right) + west * left


def odd_side(level, b):
    return ((lax.shift_right_logical(iota((8, 128), 1), level) + b) & 1) == 1


def inside_factors(k):
    gz, row, gz_count, row_count = place()
    low = jnp.where(gz == 0, 4, 0)
    high = jnp.where(gz == gz_count - 1, SPAN - 4, SPAN)
    at = iota((8, 128), 0) + 8 * k
    main = jnp.where((at >= low) & (at < high), 1.0, 0.0).astype(F32)
    lane = iota((8, 128), 1)
    first = jnp.where(row == row_count - 1, 64, 0)
    after = jnp.where(row == 0, 64, 128)
    return main, jnp.where((lane >= first) & (lane < after), main, 0.0)


def chunks(level, body):
    def write(stores):
        for ref, at, b, p, k, value in stores:
            put(ref, at, b, p, k, value)

    if level == 0:
        pl.loop(0, SPAN // 8)(lambda k: write(body(k)))
    else:
        write([store for k in range(SPAN // 8) for store in body(k)])


def down_level(level, source, black, coarse, coef):
    count = planes_of(level)
    step = 2**level
    keep = (lax.shift_right_logical(iota((8, 128), 1), level) & 1) == 0

    def sweep(k):
        main, side = inside_factors(k)
        main, side = 0.25 * main, 0.25 * side
        stores = []
        for b in range(count):
            beside = beside_side(source, coef, level, b, k)
            value = (here_of(source, level, b, count, k) + 0.25 * beside) * side
            stores.append((black, level, b, count, k, jnp.where(odd_side(level, b), value, 0.0)))
            for p in range(1 - b % 2, count, 2):
                beside = beside_main(source, coef, level, b, p, k)
                value = (here_of(source, level, b, p, k) + 0.25 * beside) * main
                stores.append((black, level, b, p, k, value))
        return stores

    def restrict(k):
        main, side = inside_factors(k)
        stores = []
        for b in range(0, count, 2):
            even = beside_side(black, coef, level, b, k)
            odd = turn(beside_side(black, coef, level, b + 1, k), -step)
            value = jnp.where(keep, (even + odd) * side, 0.0)
            stores.append((coarse, level + 1, b // 2, count // 2, k, value))
            for p in range(0, count, 2):
                value = beside_main(black, coef, level, b, p, k) + beside_main(black, coef, level, b + 1, p + 1, k)
                stores.append((coarse, level + 1, b // 2, p // 2, k, value * main))
        return stores

    chunks(level, sweep)
    chunks(level, restrict)


PACKED_SOURCE = 72 * SPAN
PACKED_BLACK = 40 * SPAN


def packed_source(b, p):
    return (9 * b + p) * SPAN


def packed_black(b, p):
    return (5 * b + (p // 2 if p < 8 else 4)) * SPAN


def up_level(level, source, black, error, field, coef):
    count = planes_of(level)
    step = 2**level
    moved = (lax.shift_right_logical(iota((8, 128), 1), level) & 1) == 1

    def source_at(b, p, k):
        if level > 0:
            return here_of(source, level, b, p, k)
        return source[pl.ds(pl.multiple_of(packed_source(b, p) + 8 * k, 8), 8), :]

    def black_at(b, p, k):
        if level > 0:
            return here_of(black, level, b, p, k)
        return black[pl.ds(pl.multiple_of(packed_black(b, p) + 8 * k, 8), 8), :]

    def correct(k):
        stores = []
        for b in range(count):
            value = here_of(error, level + 1, b // 2, count // 2, k)
            value = jnp.where(moved, turn(value, step), value)
            value = black_at(b, count, k) + value
            stores.append((field, level, b, count, k, jnp.where(odd_side(level, b), value, 0.0)))
            for p in range(1 - b % 2, count, 2):
                value = here_of(error, level + 1, b // 2, p // 2, k)
                stores.append((field, level, b, p, k, black_at(b, p, k) + value))
        return stores

    def sweep(colour, k):
        main, side = inside_factors(k)
        main, side = 0.25 * main, 0.25 * side
        stores = []
        for b in range(count):
            beside = beside_side(field, coef, level, b, k)
            value = (source_at(b, count, k) + beside) * side
            mine = odd_side(level, b + 1 - colour)
            stores.append((field, level, b, count, k, jnp.where(mine, value, here_of(field, level, b, count, k))))
            for p in range((b + colour) % 2, count, 2):
                beside = beside_main(field, coef, level, b, p, k)
                stores.append((field, level, b, p, k, (source_at(b, p, k) + beside) * main))
        return stores

    chunks(level, correct)
    chunks(level, functools.partial(sweep, 0))
    chunks(level, functools.partial(sweep, 1))


def zero_pads(refs):
    for level, ref in refs:
        for b in range(planes_of(level)):
            for p in range(planes_of(level) + 1):
                at = base(level, b, p)
                ref[at : at + PAD, :] = jnp.zeros((PAD, 128), F32)
                ref[at + PAD + SPAN : at + TALL, :] = jnp.zeros((PAD, 128), F32)


def picked(x, pick):
    return jnp.take_along_axis(x, pick, axis=1)


def exchanged(tiles):
    tiles = list(tiles)
    lane = iota(tiles[0].shape, 1)
    for bit in range(3):
        far = 2**bit
        low = (lax.shift_right_logical(lane, bit) & 1) == 0
        for k in range(8):
            if not k & far:
                a, c = tiles[k], tiles[k + far]
                tiles[k] = jnp.where(low, a, turn(c, far))
                tiles[k + far] = jnp.where(low, turn(a, -far), c)
    return tiles


def two_sum(a, b):
    total = a + b
    part = total - a
    return total, (a - (total - part)) + (b - part)


def halves(a):
    wide = a * 4097.0
    high = wide - (wide - a)
    return high, a - high


def two_prod(a, b):
    total = a * b
    ah, al = halves(a)
    bh, bl = halves(b)
    return total, ((ah * bh - total) + ah * bl + al * bh) + al * bl


def dd_add(a, b):
    total, rest = two_sum(a[0], b[0])
    rest = rest + (a[1] + b[1])
    high = total + rest
    return high, rest - (high - total)


def dd_mul(a, b):
    total, rest = two_prod(a[0], b[0])
    rest = rest + (a[0] * b[1] + a[1] * b[0])
    high = total + rest
    return high, rest - (high - total)


BAND = 16
FOLD = ROWS // 4


def pack_edges(vort, swirl_first, swirl_last):
    lane = iota((FOLD, 128), 1)
    eastward = westward = None
    for run in range(4):
        rows = slice(FOLD * run, FOLD * run + FOLD)
        last = jnp.where(lane == 96, turn(swirl_last[rows, :], 97), vort[rows, COLS - 128 :])
        first = jnp.where(lane == 31, turn(swirl_first[rows, :], 31), vort[rows, :128])
        last, first = turn(last, 32 * run + 32), turn(first, 32 * run)
        mine = lax.shift_right_logical(lane, 5) == run
        eastward = last if run == 0 else jnp.where(mine, last, eastward)
        westward = first if run == 0 else jnp.where(mine, first, westward)
    return eastward, westward


def unpack_edges(west, east, beyond):
    lane = iota((FOLD, 128), 1)
    for run in range(4):
        value = jnp.where(lane >= 96, turn(west, 96 - 32 * run), 0.0)
        beyond[FOLD * run : FOLD * run + FOLD, :] = jnp.where(lane < 32, turn(east, -32 * run), value)


def first_kernel(
    vort_hbm, swirl_hbm, back_hbm, part, swap_a, swap_b, planes, row_top, row_end,
    s0, s1, s2, s3, b0, b1, b2, coef, vort, arrived, swirl_first, swirl_last, ends, ends_arrived,
):
    copies, extras = [], []
    for band in range(ROWS // BAND):
        rows = pl.ds(BAND * band, BAND)
        copies.append(pltpu.make_async_copy(vort_hbm.at[rows, :], vort.at[rows, :], arrived.at[band]))
        copies[-1].start()
    pieces = [(swirl_hbm.at[:, pl.ds(0, 128)], swirl_first), (swirl_hbm.at[:, pl.ds(COLS - 128, 128)], swirl_last)]
    for number, array in enumerate((swirl_hbm, back_hbm)):
        for end, first in enumerate((0, ROWS - 8)):
            pieces.append((array.at[pl.ds(first, 8), :], ends.at[2 * number + end]))
    for number, (src, dst) in enumerate(pieces):
        extras.append(pltpu.make_async_copy(src, dst, ends_arrived.at[number]))
        extras[-1].start()
    fill_coefs(coef)
    zero_pads(((0, s0), (1, s1), (2, s2), (0, b0), (1, b1), (2, b2)))
    for b in range(8):
        for p in range(8):
            at = base(0, b, p) + PAD
            s0[at : at + 4, :] = jnp.zeros((4, 128), F32)
            s0[at + 28 : at + 32, :] = jnp.zeros((4, 128), F32)
        at = base(0, b, 8) + PAD
        s0[at : at + SPAN, :] = jnp.zeros((SPAN, 128), F32)
    for band in range(ROWS // BAND):
        copies[band].wait()
        rows = slice(BAND * band, BAND * band + BAND)
        tiles = [vort[rows, 128 * k : 128 * k + 128] for k in range(8)]
        for p, tile in enumerate(exchanged(tiles)):
            for part_of in range(BAND // 8):
                g = BAND // 8 * band + part_of
                s0[pl.ds(base(0, 0, p) + PAD + 4 + g, 8, stride=9 * TALL), :] = tile[8 * part_of : 8 * part_of + 8]
    for extra in extras:
        extra.wait()
    odd = is_odd("row")
    eastward, westward = pack_edges(vort, swirl_first, swirl_last)
    swap_a[:FOLD, :] = jnp.where(odd, westward, eastward)
    swap_b[:FOLD, :] = jnp.where(odd, eastward, westward)
    for end, (dest, row, edge) in enumerate(((row_top, 0, 0), (row_end, ROWS - 1, 7))):
        for tile in range(COLS // 128):
            lanes = slice(128 * tile, 128 * tile + 128)
            swirl = ends[end, edge : edge + 1, lanes]
            dest[tile : tile + 1, :] = swirl
            dest[8 + tile : 9 + tile, :] = 2.0 * ends[2 + end, edge : edge + 1, lanes] * swirl
            dest[16 + tile : 17 + tile, :] = vort[row : row + 1, lanes]
    for b in range(8):
        for p in range(8):
            at = base(0, b, p) + PAD + 4
            planes[24 * (8 * b + p) : 24 * (8 * b + p) + 24, :] = s0[at : at + 24, :]
    down_level(0, s0, b0, s1, coef)
    down_level(1, s1, b1, s2, coef)
    down_level(2, s2, b2, s3, coef)

    scale = 1.0 / float(4**LEVELS)
    main = s3[PAD : PAD + SPAN, :] * scale
    side = s3[TALL + PAD : TALL + PAD + SPAN, :] * scale
    lane = iota((SPAN, 128), 1)
    main = picked(main, 8 * (lane & 15) + lax.shift_right_logical(lane, 4))
    side = jnp.where((lane < 8) | (lane >= 120), picked(side, 8 * (lane & 15)), 0.0)
    part[:, :128] = main
    part[:, 128:] = side
    high = lane >= 64
    eastward, westward = jnp.where(high, main, side), jnp.where(high, side, main)
    swap_a[FOLD:, :] = jnp.where(odd, westward, eastward)
    swap_b[FOLD:, :] = jnp.where(odd, eastward, westward)


def level_scratch():
    sources = [pltpu.VMEM((plane_rows(level), 128), F32) for level in range(LEVELS + 1)]
    blacks = [pltpu.VMEM((plane_rows(level), 128), F32) for level in range(LEVELS)]
    return sources + blacks + [pltpu.VMEM((COEF_ROWS, 128), F32)]


def vmem():
    return pl.BlockSpec(memory_space=pltpu.VMEM)


def out_copies(pairs, moved):
    return [pltpu.make_async_copy(src, dst, moved.at[at]) for at, (src, dst) in enumerate(pairs)]


def hbm():
    return pl.BlockSpec(memory_space=pltpu.HBM)


def fixed(x):
    return pltpu.with_memory_space_constraint(x, pltpu.HBM)


def shaped(*dims):
    return jax.ShapeDtypeStruct(dims, F32)


def params(mebibytes):
    return dict(compiler_params=pltpu.CompilerParams(vmem_limit_bytes=mebibytes * 2**20))


def run_first(vort, swirl, back):
    return pl.pallas_call(
        first_kernel,
        out_shape=(shaped(32, 256), shaped(FOLD + 32, 128), shaped(FOLD + 32, 128), shaped(64 * 24, 128))
        + (shaped(24, 128),) * 2,
        in_specs=[hbm()] * 3,
        out_specs=[vmem()] * 6,
        scratch_shapes=level_scratch()
        + [pltpu.VMEM((ROWS, COLS), F32), pltpu.SemaphoreType.DMA((ROWS // BAND,))]
        + [pltpu.VMEM((ROWS, 128), F32)] * 2
        + [pltpu.VMEM((4, 8, COLS), F32), pltpu.SemaphoreType.DMA((6,))],
        name="down_own",
        **params(24),
    )(fixed(vort), fixed(swirl), fixed(back))


OUTER = 288


def second_kernel(part, swap_a, swap_b, planes, row_top, row_end, whole, out_a, out_b, to_next, to_prev, beyond):
    high = iota((32, 128), 1) >= 64
    from_west, from_east = chosen("row", swap_a[...], swap_b[...])
    west, east = from_west[FOLD:], from_east[FOLD:]
    main = part[:, :128] + jnp.where(high, east, west)
    side = part[:, 128:] + jnp.where(high, west, east)
    whole[:, :128] = main
    whole[:, 128:] = side
    unpack_edges(from_west[:FOLD], from_east[:FOLD], beyond)
    for dest, g, rows, row in ((to_next, 20, slice(16, 32), row_end), (to_prev, 0, slice(0, 16), row_top)):
        for b in range(8):
            for p in range(8):
                at = 4 * (9 * b + p)
                dest[at : at + 4, :] = planes[24 * (8 * b + p) + g : 24 * (8 * b + p) + g + 4, :]
            at = 4 * (9 * b + 8)
            dest[at : at + 4, :] = beyond[pl.ds(8 * g + b, 4, stride=8), :]
        dest[OUTER : OUTER + 16, :] = main[rows]
        dest[OUTER + 16 : OUTER + 32, :] = side[rows]
        dest[OUTER + 32 :, :] = row[...]
    odd = is_odd("gz")
    out_a[...] = jnp.where(odd, to_prev[...], to_next[...])
    out_b[...] = jnp.where(odd, to_next[...], to_prev[...])


def run_second(part, swap_a, swap_b, planes, row_top, row_end):
    return pl.pallas_call(
        second_kernel,
        out_shape=(shaped(32, 256), shaped(OUTER + 56, 128), shaped(OUTER + 56, 128)),
        in_specs=[vmem()] * 6,
        out_specs=[vmem()] * 3,
        scratch_shapes=[pltpu.VMEM((OUTER + 56, 128), F32)] * 2 + [pltpu.VMEM((ROWS, 128), F32)],
        name="pack_gz",
        **params(24),
    )(part, swap_a, swap_b, planes, row_top, row_end)


def third_kernel(
    whole, swap_a, swap_b, basis_out, message, grid, gram_high, gram_low, basis, moved
):
    copies = out_copies([(basis, basis_out)], moved)
    gz, row, gz_count, row_count = place()
    grid[...] = jnp.zeros((48, 256), F32)
    grid[8:40, :] = whole[...]
    from_prev, from_next = chosen("gz", swap_a[OUTER : OUTER + 32, :], swap_b[OUTER : OUTER + 32, :])
    grid[0:16, :128] += from_prev[:16]
    grid[0:16, 128:] += from_prev[16:]
    grid[32:48, :128] += from_next[:16]
    grid[32:48, 128:] += from_next[16:]

    lane = iota((48, 256), 1)
    cols = jnp.where(lane < 192, lane, lane - 256)
    width = COLS >> LEVELS
    at = iota((48, 256), 0) - 12
    inside = lanes_inside(cols, width, row, row_count)
    low = jnp.where(gz == 0, 0, -64)
    high = jnp.where(gz == gz_count - 1, ROWS >> LEVELS, 128)
    inside = inside & (at >= low) & (at < high)
    spacing = float(2**LEVELS)
    radius = spacing * ((cols + row * width).astype(F32) + 0.5) + 16.0
    term = (1.5 * spacing) / radius
    east = jnp.where(inside, 0.25 + 0.25 * term, 0.0)
    west = jnp.where(inside, 0.25 - 0.25 * term, 0.0)
    quarter = jnp.where(inside, 0.25, 0.0)

    def average(x):
        total = quarter * (pltpu.roll(x, 1, 0) + pltpu.roll(x, 47, 0))
        total = total + east * pltpu.roll(x, 255, 1)
        return total + west * pltpu.roll(x, 1, 1)

    source = jnp.where(inside, grid[...], 0.0)
    older = source - average(source)
    newer = average(older)
    vectors = [source, older, newer]
    for _ in range(BASIS - 3):
        older, newer = newer, 2.0 * average(newer) - older
        vectors.append(newer)
    at = iota((32, 128), 0)
    own = (at >= 4) & (at < 28)
    parts = []
    for k in range(BASIS):
        if k < ITERS:
            basis[32 * k : 32 * k + 32, :] = vectors[k][8:40]
        masked = jnp.where(own, vectors[k][8:40, :128], 0.0)
        parts.append((masked,) + halves(masked))
    copies[0].start()
    for slot, (i, j) in enumerate(PAIRS):
        a, ah, al = parts[i]
        b, bh, bl = parts[j]
        product = a * b
        error = ((ah * bh - product) + ah * bl + al * bh) + al * bl
        top, first = two_sum(product[0:8], product[8:16])
        bottom, second = two_sum(product[16:24], product[24:32])
        total, third = two_sum(top, bottom)
        rest = (error[0:8] + error[8:16]) + (error[16:24] + error[24:32])
        gram_high[8 * slot : 8 * slot + 8, :] = total
        gram_low[8 * slot : 8 * slot + 8, :] = rest + (first + second + third)
    gram_high[8 * len(PAIRS) :, :] = jnp.zeros((8 * (SLOTS - len(PAIRS)), 128), F32)
    gram_low[8 * len(PAIRS) :, :] = jnp.zeros((8 * (SLOTS - len(PAIRS)), 128), F32)
    total = None
    for s in range(8):
        term = (gram_high[pl.ds(s, SLOTS, stride=8), :], gram_low[pl.ds(s, SLOTS, stride=8), :])
        total = term if total is None else dd_add(total, term)
    for by in (64, 32, 16, 8, 4, 2, 1):
        total = dd_add(total, tuple(pltpu.roll(t, by, 1) for t in total))
    lane = iota((SLOTS, 128), 1)
    i = lane // BASIS
    j = lane - BASIS * i
    i, j = jnp.minimum(i, j), jnp.maximum(i, j)
    keep = (iota((SLOTS, 128), 0) == BASIS * i - i * (i - 1) // 2 + j - i) & (lane < BASIS * BASIS)
    rows = [jnp.sum(jnp.where(keep, t, 0.0), axis=0, keepdims=True) for t in total]
    odd = (iota(message.shape, 0) & 1) == 1
    message[...] = jnp.where(odd, rows[1], rows[0])
    for copy in copies:
        copy.wait()


def run_third(whole, swaps, devices):
    return pl.pallas_call(
        third_kernel,
        out_shape=(pltpu.HBM((32 * ITERS, 256), F32), shaped(2 * devices, 128)),
        in_specs=[vmem()] * 3,
        out_specs=[hbm(), vmem()],
        scratch_shapes=[pltpu.VMEM((48, 256), F32)]
        + [pltpu.VMEM((8 * SLOTS, 128), F32)] * 2
        + [pltpu.VMEM((32 * ITERS, 256), F32), pltpu.SemaphoreType.DMA((1,))],
        name="basis_gram",
        **params(24),
    )(whole, *swaps)


def sum_of(terms):
    terms = list(terms)
    while len(terms) > 1:
        added = []
        for left, right in zip(terms[::2], terms[1::2]):
            total, rest = two_sum(left[0], right[0])
            added.append((total, rest + (left[1] + right[1])))
        terms = added + terms[len(terms) // 2 * 2 :]
    return terms[0]


def tidy(pair):
    high = pair[0] + pair[1]
    return high, pair[1] - (high - pair[0])


def coarse_coefs(grams, held, cells):
    devices = grams.shape[0] // 2
    gram = (grams[pl.ds(0, devices, stride=2), :], grams[pl.ds(1, devices, stride=2), :])
    while gram[0].shape[0] > 8:
        half = gram[0].shape[0] // 2
        gram = dd_add(tuple(g[:half] for g in gram), tuple(g[half:] for g in gram))
    for by in (4, 2, 1):
        gram = dd_add(gram, tuple(pltpu.roll(g, by, 0) for g in gram))

    lane = iota((16, 128), 0)
    gram = tuple(jnp.concatenate([g, g], axis=0) for g in gram)
    columns = []
    for j in range(BASIS):
        pick = jnp.minimum(lane * BASIS + j, BASIS * BASIS - 1)
        high, low = (jnp.where(lane < BASIS, picked(g, pick), 0.0) for g in gram)
        columns.append((high, low) + halves(high))

    index = iota((16, 128), 0)
    below = jnp.where(index == 0, 0.0, jnp.where(index == 1, -1.0, jnp.where(index == 2, 1.0, 0.5)))
    below = jnp.where(index < BASIS, below, 0.0)
    above = jnp.where((index > 0) & (index < BASIS - 1), 0.5, 0.0)
    same = jnp.where((index > 0) & (index < BASIS), 1.0, 0.0)

    def image(a):
        moved = sum_of([tuple(below * pltpu.roll(t, 1, 0) for t in a), tuple(above * pltpu.roll(t, 15, 0) for t in a)])
        return tidy(sum_of([tuple(same * t for t in a), tuple(-t for t in moved)]))

    a = (jnp.where(index == 0, 1.0, 0.0), jnp.zeros((16, 128), F32))
    solved = jnp.zeros((16, 128), F32)
    tiny = float(4 ** (2 * LEVELS)) / 16.0 * cells * 1e-12
    for _ in range(ITERS):
        b = image(a)
        held[0:16, :] = b[0]
        held[16:32, :] = b[1]
        terms = []
        for j, (high, low, upper, lower) in enumerate(columns):
            at_j = jnp.broadcast_to(held[j : j + 1, :], (16, 128))
            rest_j = jnp.broadcast_to(held[16 + j : 17 + j, :], (16, 128))
            jh, jl = halves(at_j)
            product = high * at_j
            rest = ((upper * jh - product) + upper * jl + lower * jh) + lower * jl
            terms.append((product, rest + (high * rest_j + low * at_j)))
        image_gram = tidy(sum_of(terms))
        forms = []
        for left in (a, b):
            high, rest = two_prod(left[0], image_gram[0])
            form = (high, rest + (left[0] * image_gram[1] + left[1] * image_gram[0]))
            form = sum_of([tuple(t[:8] for t in form), tuple(t[8:] for t in form)])
            for by in (4, 2, 1):
                form = sum_of([form, tuple(pltpu.roll(t, by, 0) for t in form)])
            forms.append(form[0] + form[1])
        alpha = forms[0] / (forms[1] + tiny)
        alpha = jnp.concatenate([alpha, alpha], axis=0)
        solved = solved + alpha * a[0]
        high, rest = two_prod(alpha, b[0])
        a = tidy(sum_of([a, (-high, -(rest + alpha * b[1]))]))
    return solved * (float(4**LEVELS) * 0.25)


LEVEL_ROWS = [PACKED_SOURCE, PACKED_BLACK] + [plane_rows(level) for level in (1, 1, 2, 2)]


def down_kernel(
    planes_hbm, row_a_hbm, row_b_hbm, a_hbm, b_hbm, s0_out, b0_out, s1_out, b1_out, s2_out, b2_out,
    s0, s1, s2, s3, b0, b1, b2, coef, planes, row_a, row_b, swap_a, swap_b, beyond, s0_packed, b0_packed, arrived, moved,
):
    outer = pl.ds(0, OUTER)
    reads = out_copies(
        [(row_a_hbm, row_a), (row_b_hbm, row_b), (planes_hbm, planes), (a_hbm.at[outer, :], swap_a), (b_hbm.at[outer, :], swap_b)],
        arrived,
    )
    writes = out_copies([(s0_packed, s0_out), (b0_packed, b0_out), (s1, s1_out), (b1, b1_out), (s2, s2_out), (b2, b2_out)], moved)
    for read in reads:
        read.start()
    fill_coefs(coef)
    zero_pads(((0, s0), (1, s1), (2, s2), (0, b0), (1, b1), (2, b2)))
    for read in reads:
        read.wait()
    unpack_edges(*chosen("row", row_a[:FOLD, :], row_b[:FOLD, :]), beyond)
    for b in range(8):
        for p in range(9):
            at = base(0, b, p) + PAD
            edge = 4 * (9 * b + p)
            from_prev, from_next = chosen("gz", swap_a[edge : edge + 4, :], swap_b[edge : edge + 4, :])
            s0[at : at + 4, :] = from_prev
            s0[at + 28 : at + 32, :] = from_next
            if p < 8:
                s0[at + 4 : at + 28, :] = planes[24 * (8 * b + p) : 24 * (8 * b + p) + 24, :]
            else:
                s0[at + 4 : at + 28, :] = beyond[pl.ds(b, 24, stride=8), :]
            s0_packed[packed_source(b, p) : packed_source(b, p) + SPAN, :] = s0[at : at + SPAN, :]
    writes[0].start()
    down_level(0, s0, b0, s1, coef)
    for b in range(8):
        for p in list(range(1 - b % 2, 8, 2)) + [8]:
            at = base(0, b, p) + PAD
            b0_packed[packed_black(b, p) : packed_black(b, p) + SPAN, :] = b0[at : at + SPAN, :]
    writes[1].start()
    writes[2].start()
    down_level(1, s1, b1, s2, coef)
    writes[3].start()
    writes[4].start()
    down_level(2, s2, b2, s3, coef)
    writes[5].start()
    for write in writes:
        write.wait()


def run_down(planes, rows, swaps):
    held = [(64 * 24, 128), (FOLD + 32, 128), (FOLD + 32, 128), (OUTER, 128), (OUTER, 128), (ROWS, 128), (PACKED_SOURCE, 128), (PACKED_BLACK, 128)]
    return pl.pallas_call(
        down_kernel,
        out_shape=tuple(pltpu.HBM((rows, 128), F32) for rows in LEVEL_ROWS),
        in_specs=[hbm()] * 5,
        out_specs=[hbm()] * 6,
        scratch_shapes=level_scratch()
        + [pltpu.VMEM(dims, F32) for dims in held]
        + [pltpu.SemaphoreType.DMA((5,)), pltpu.SemaphoreType.DMA((6,))],
        name="down_all",
        cost_estimate=pl.CostEstimate(flops=40 * ROWS * COLS, bytes_accessed=30 * ROWS * COLS, transcendentals=0),
        **params(24),
    )(*[fixed(x) for x in (planes, *rows, *swaps)])


def fourth_kernel(
    grams, basis_hbm, s0_hbm, b0_hbm, s1_hbm, b1_hbm, s2_hbm, b2_hbm, out,
    s0, s1, s2, s3, b0, b1, b2, v0, coef, held, basis, moved, final, left, *, cells,
):
    reads = out_copies(
        [(basis_hbm, basis), (s2_hbm, s2), (b2_hbm, b2), (s1_hbm, s1), (b1_hbm, b1), (s0_hbm, s0), (b0_hbm, b0)], moved
    )
    for read in reads:
        read.start()
    fill_coefs(coef)
    zero_pads(((0, v0),))
    solved = coarse_coefs(grams, held, cells)
    for read in reads[:3]:
        read.wait()
    value = jnp.zeros((32, 256), F32)
    for k in range(ITERS):
        value = value + solved[k : k + 1, 0:1] * basis[32 * k : 32 * k + 32, :]
    lane = iota((SPAN, 128), 1)
    side = value[:, 128:]
    far = lax.shift_right_logical(lane, 3)
    s3[PAD : PAD + SPAN, :] = picked(value[:, :128], 16 * (lane & 7) + far)
    s3[TALL + PAD : TALL + PAD + SPAN, :] = picked(side, jnp.where(lane < 64, far, far + 112))
    up_level(2, s2, b2, s3, b2, coef)
    for read in reads[3:5]:
        read.wait()
    up_level(1, s1, b1, b2, b1, coef)
    for read in reads[5:]:
        read.wait()
    up_level(0, s0, b0, b1, v0, coef)
    writes = []
    for band in range(ROWS // BAND):
        tiles = []
        for p in range(8):
            at = base(0, 0, p) + PAD + 4 + BAND // 8 * band
            tiles.append(jnp.concatenate([v0[pl.ds(at + g, 8, stride=9 * TALL), :] for g in range(BAND // 8)], axis=0))
        for k, tile in enumerate(exchanged(tiles)):
            final[BAND * band : BAND * band + BAND, 128 * k : 128 * k + 128] = tile
        rows = pl.ds(BAND * band, BAND)
        writes.append(pltpu.make_async_copy(final.at[rows, :], out.at[rows, :], left.at[band]))
        writes[-1].start()
    for write in writes:
        write.wait()


def run_fourth(grams, basis, levels):
    cells = float((ROWS >> LEVELS) * (COLS >> LEVELS) * lax.axis_size("gz") * lax.axis_size("row"))
    tall = [PACKED_SOURCE, *(plane_rows(level) for level in (1, 2, 3)), PACKED_BLACK]
    tall += [plane_rows(level) for level in (1, 2, 0)] + [COEF_ROWS]
    fields = [pltpu.VMEM((rows, 128), F32) for rows in tall]
    held = [(32, 128), (32 * ITERS, 256)]
    return pl.pallas_call(
        functools.partial(fourth_kernel, cells=cells),
        out_shape=shaped(ROWS, COLS),
        in_specs=[vmem()] + [hbm()] * 7,
        out_specs=hbm(),
        scratch_shapes=fields + [pltpu.VMEM(dims, F32) for dims in held]
        + [pltpu.SemaphoreType.DMA((7,)), pltpu.VMEM((ROWS, COLS), F32), pltpu.SemaphoreType.DMA((ROWS // BAND,))],
        name="v_cycle",
        **params(24),
    )(grams, *[fixed(x) for x in (basis, *levels)])


STRIP = FOLD


def rates_kernel(
    swirl, swirl_up, swirl_down, vort, vort_up, vort_down, back, back_up, back_down, row_a, row_b,
    u_a, p_a, w_a, u_b, p_b, w_b, vel_r, vel_z, swirl_coef, vort_coef, swirl_out, vort_out,
):
    strip = pl.program_id(0)
    lane = iota((STRIP, 128), 1)
    at = iota((STRIP, 128), 0)
    tiles = COLS // 128
    west, east = chosen("row", row_a[...], row_b[...])
    west, east = pltpu.roll(west, (224 - 32 * strip) % 128, 1), pltpu.roll(east, (128 - 32 * strip) % 128, 1)

    u_prev, u_next = chosen("gz", u_a[...], u_b[...])
    p_prev, p_next = chosen("gz", p_a[...], p_b[...])
    w_prev, w_next = chosen("gz", w_a[...], w_b[...])
    above, below = strip > 0, strip < ROWS // STRIP - 1

    def slopes(ref, top, bottom, west, east, tile):
        lanes = slice(128 * tile, 128 * tile + 128)
        here = ref[:, lanes]
        left = west if tile == 0 else turn(ref[:, 128 * tile - 128 : 128 * tile], 1)
        right = east if tile == tiles - 1 else turn(ref[:, 128 * tile + 128 : 128 * tile + 256], -1)
        along_r = jnp.where(lane == 127, right, turn(here, -1)) - jnp.where(lane == 0, left, turn(here, 1))
        return here, along_r * 0.5, slope_z(here, top, bottom)

    def slope_z(here, top, bottom):
        ahead = jnp.where(at == STRIP - 1, bottom, pltpu.roll(here, STRIP - 1, 0))
        behind = jnp.where(at == 0, top, pltpu.roll(here, 1, 0))
        return (ahead - behind) * 0.5

    for tile in range(tiles):
        lanes = slice(128 * tile, 128 * tile + 128)
        own = slice(tile, tile + 1)
        u_top = jnp.where(above, swirl_up[7:8, lanes], u_prev[own])
        u_bottom = jnp.where(below, swirl_down[0:1, lanes], u_next[own])
        w_top = jnp.where(above, vort_up[7:8, lanes], w_prev[own])
        w_bottom = jnp.where(below, vort_down[0:1, lanes], w_next[own])
        p_top = jnp.where(above, 2.0 * back_up[7:8, lanes] * u_top, p_prev[own])
        p_bottom = jnp.where(below, 2.0 * back_down[0:1, lanes] * u_bottom, p_next[own])
        u, u_r, u_z = slopes(swirl, u_top, u_bottom, turn(west, 32), turn(east, 96), tile)
        w, w_r, w_z = slopes(vort, w_top, w_bottom, turn(west, 1), turn(east, -1), tile)
        p_z = slope_z(2.0 * back[:, lanes] * u, p_top, p_bottom)
        swirl_out[:, lanes] = swirl_coef[:, lanes] * u - vel_r[:, lanes] * u_r - vel_z[:, lanes] * u_z
        vort_out[:, lanes] = vort_coef[:, lanes] * w - vel_r[:, lanes] * w_r - vel_z[:, lanes] * w_z + p_z


def run_rates(swirl, vort, back, rows, swap_a, swap_b, vel_r, vel_z, swirl_coef, vort_coef):
    per = STRIP // 8
    block = pl.BlockSpec((STRIP, COLS), lambda t: (t, 0))
    up = pl.BlockSpec((8, COLS), lambda t: (jnp.maximum(per * t - 1, 0), 0))
    down = pl.BlockSpec((8, COLS), lambda t: (jnp.minimum(per * t + per, ROWS // 8 - 1), 0))
    singles = [pl.BlockSpec((8, 128), functools.partial(lambda at, t: (at, 0), OUTER // 8 + 4 + k)) for k in range(3)]
    return pl.pallas_call(
        rates_kernel,
        grid=(ROWS // STRIP,),
        out_shape=(shaped(ROWS, COLS), shaped(ROWS, COLS)),
        in_specs=[block, up, down] * 3 + [pl.BlockSpec((FOLD, 128), lambda t: (0, 0))] * 2 + singles * 2 + [block] * 4,
        out_specs=[block] * 2,
        name="rates",
        cost_estimate=pl.CostEstimate(flops=30 * ROWS * COLS, bytes_accessed=36 * ROWS * COLS, transcendentals=0),
        **params(16),
    )(*[fixed(x) for x in (swirl,) * 3 + (vort,) * 3 + (back,) * 3], *[fixed(x) for x in (*rows,) + (swap_a,) * 3 + (swap_b,) * 3 + (vel_r, vel_z, swirl_coef, vort_coef)])


def swapped(axis, first, second):
    count = lax.axis_size(axis)
    pairs = [(i, i ^ 1) for i in range(count)]
    others = [(i, (i + 1) % count if i % 2 else (i - 1) % count) for i in range(count)]
    return lax.ppermute(first, axis, pairs), lax.ppermute(second, axis, others)


def per_device(swirl, vorticity, base_swirl, vel_r, vel_z, swirl_coef, vort_coef):
    devices = lax.axis_size("gz") * lax.axis_size("row")
    part, *swaps, planes, row_top, row_end = run_first(vorticity, swirl, base_swirl)
    rows = swapped("row", *swaps)
    whole, *swaps = run_second(part, *rows, planes, row_top, row_end)
    swaps = swapped("gz", *swaps)
    basis, message = run_third(whole, swaps, devices)
    grams = lax.all_to_all(message, AXES, 0, 0, tiled=True)
    levels = run_down(planes, rows, swaps)
    swirl_rate, vort_rate = run_rates(swirl, vorticity, base_swirl, rows, *swaps, vel_r, vel_z, swirl_coef, vort_coef)
    potential = run_fourth(grams, basis, levels)
    return swirl_rate, vort_rate, potential


def solution(mesh):
    spec = P("gz", "row")
    return jax.shard_map(per_device, mesh=mesh, in_specs=(spec,) * 7, out_specs=(spec,) * 3, check_vma=False)
```
